512 devices in a mesh: dp: 128 (over z, y, core), mp: 4 (over x).
Axes of the slice: x: 4, y: 8, z: 8, core: 2. Of those that a mesh axis runs over, the one named last changes fastest.
Arguments:
- query_feats: bfloat16 [512, 1024], P('dp'), may hold values from -6 to 6
- item_feats: bfloat16 [131072, 1024], P('dp'), may hold values from -6 to 6
- w_in: bfloat16 [1024, 1024], P(None, 'mp'), may hold values from -0.1875 to 0.1875
- w_out: bfloat16 [1024, 256], P('mp'), may hold values from -0.1875 to 0.1875
- negatives: int32 [512, 128], P('dp'), may hold values from 0 to 131071, as said below
- positives: int32 [512], P('dp'), may hold values from 0 to 131071, as said below
- owner_map: int32 [131072], replicated, may hold values from 0 to 131071, as said below
Outputs:
- grad_in: bfloat16 [1024, 1024], P(None, 'mp')
- grad_out: bfloat16 [1024, 256], P('mp')
The draws below stay inside these ranges and needn't reach their ends.
Inputs may be any that keep to these rules, and one draw needn't show every extreme that they name: A permutation of the item ids: item i is row owner_map[i] of item_feats, stored on dp device owner_map[i] // 1024. The hard negatives of the 4 queries of one dp device name at most 16 items stored on any one dp device, counted with repeats; for the queries of dp device i, dp device (i + 64) mod 128 stores exactly 16 of them. `positives`: the positive of a query is stored on the query's own dp device.
All inputs are finite; a program needn't handle non-finite values.
Results may differ from the reference program's by a relative error of at most 0.013.
Values may be sent and summed in bfloat16 or wider, within the bound.
No kernel may reach another device: no remote copies, remote signals or barrier semaphores. Data moves between devices by JAX's collectives and lax.ppermute only.
A program may use at most 64 MiB of HBM per device.

```python
import math
import jax
import jax.numpy as jnp
from jax import lax

F = 1024
H = 1024
E = 256
NEG = 128
Q_DEV = 4
I_DEV = 1024
QUERIES = 512
ITEMS = 131072
N_DP = 128


def shared_layout(key):
    storage = jax.random.permutation(jax.random.fold_in(key, 101), ITEMS).astype(jnp.int32)
    inverse = jnp.zeros((ITEMS,), jnp.int32).at[storage].set(jnp.arange(ITEMS, dtype=jnp.int32))
    return (storage, inverse)


def block_rows(device, key):
    average = Q_DEV * NEG // N_DP
    request_count = Q_DEV * NEG
    far_owner = ((device + N_DP // 2) % N_DP).astype(jnp.int32)
    order = jax.random.permutation(jax.random.fold_in(key, 1), N_DP).astype(jnp.int32)
    where_far = jnp.argmax(order == far_owner)
    leading = order[0]
    order = order.at[where_far].set(leading).at[0].set(far_owner)
    spread = jax.random.randint(jax.random.fold_in(key, 2), ((N_DP - 4) // 2,), 0, average + 1).astype(jnp.int32)
    counts = jnp.zeros((N_DP,), jnp.int32)
    counts = counts.at[order[0]].set(4 * average)
    counts = counts.at[order[4::2]].set(average + spread).at[order[5::2]].set(average - spread)
    bounds = jnp.cumsum(counts)
    owners = jnp.searchsorted(bounds, jnp.arange(request_count, dtype=jnp.int32), side='right').astype(jnp.int32)
    shuffle = jax.random.permutation(jax.random.fold_in(key, 3), request_count)
    owners = owners[shuffle]
    local_rows = jax.random.randint(jax.random.fold_in(key, 4), (request_count,), 0, I_DEV).astype(jnp.int32)
    return owners * I_DEV + local_rows


def draw_negatives(key, part):
    storage, inverse = shared_layout(key)
    key = jax.random.fold_in(key, 3)
    block_keys = jax.random.split(key, N_DP)
    devices = jnp.arange(N_DP, dtype=jnp.int32)
    stored = jax.vmap(block_rows)(devices, block_keys)
    return inverse[stored].reshape(QUERIES, NEG)


def draw_positives(key, part):
    storage, inverse = shared_layout(key)
    key = jax.random.fold_in(key, 5)
    device_of = jnp.arange(QUERIES, dtype=jnp.int32) // Q_DEV
    local_rows = jax.random.randint(key, (QUERIES,), 0, I_DEV).astype(jnp.int32)
    return inverse[device_of * I_DEV + local_rows]


def draw_owner_map(key, part):
    layout = shared_layout(key)
    return layout[0]


def shard_levels(own_key, shape, cuts, low, high):
    def one(axis_at, blocks):
        steps = jax.random.uniform(jax.random.fold_in(jax.random.fold_in(own_key, 6), axis_at), (blocks,), jnp.float32, low / len(cuts), high / len(cuts))
        return jnp.repeat(jnp.exp(steps), shape[axis_at] // blocks).reshape((-1,) + (1,) * (len(shape) - axis_at - 1))

    factor_of = one(*cuts[0])
    for cut in cuts[1:]:
        factor_of = factor_of * one(*cut)
    return factor_of


def bell_draw(rng, shape, deviation, most, pieces=(), kind=jnp.bfloat16):
    drawn = jax.random.normal(rng, shape, jnp.float32) * deviation
    if len(pieces) > 0:
        drawn = shard_levels(rng, shape, pieces, -0.22, 0.18) * drawn
    return jnp.clip(drawn, min=-most, max=most).astype(kind)


def setup_inputs(seed: int = 0) -> dict:
    seeds = jax.random.split(jax.random.key(seed), 8)
    return {
        "query_feats": bell_draw(seeds[0], (QUERIES, F), 1.0, 6.0, ((0, 128),)),
        "item_feats": bell_draw(seeds[1], (ITEMS, F), 1.0, 6.0, ((0, 128),)),
        "w_in": bell_draw(seeds[2], (F, H), F ** -0.5, 0.1875, ((1, 4),)),
        "w_out": bell_draw(seeds[3], (H, E), H ** -0.5, 0.1875, ((0, 4),)),
        "negatives": draw_negatives(jax.random.fold_in(seeds[7], 71), 0),
        "positives": draw_positives(jax.random.fold_in(seeds[7], 71), 0),
        "owner_map": draw_owner_map(jax.random.fold_in(seeds[7], 71), 0),
    }


def encoder(features, w_in, w_out):
    preact = jnp.dot(features, w_in, preferred_element_type=jnp.float32)
    hidden = jnp.maximum(preact, 0.0).astype(jnp.bfloat16)
    embedding = jnp.tanh(jnp.dot(hidden, w_out, preferred_element_type=jnp.float32))
    return (preact, hidden, embedding)

def reference(query_feats, item_feats, w_in, w_out, negatives, positives, owner_map):
    score_scale = 4.0 / math.sqrt(E)
    features = jnp.concatenate([query_feats, item_feats], 0)
    preact, hidden, embedding = encoder(features, w_in, w_out)
    emb16 = embedding.astype(jnp.bfloat16)
    query32 = emb16[:QUERIES].astype(jnp.float32)
    item16 = emb16[QUERIES:]
    neg_rows = owner_map[negatives].astype(jnp.int32)
    pos_rows = owner_map[positives].astype(jnp.int32)
    neg32 = item16[neg_rows].astype(jnp.float32)
    pos32 = item16[pos_rows].astype(jnp.float32)
    neg_score = score_scale * jnp.einsum('qd,qkd->qk', query32, neg32)
    pos_score = score_scale * lax.optimization_barrier(jnp.sum(query32 * pos32, 1))
    pos_exp = jnp.exp(pos_score)
    neg_exp = jnp.exp(neg_score)
    denominator = pos_exp + lax.optimization_barrier(jnp.sum(neg_exp, 1))
    pos_grad = pos_exp / denominator - 1.0
    neg_grad = neg_exp / denominator[:, None]
    pair_neg = (score_scale * neg_grad[:, :, None] * query32[:, None, :]).astype(jnp.bfloat16)
    pair_pos = (score_scale * pos_grad[:, None] * query32).astype(jnp.bfloat16)
    query_grad = score_scale * (pos_grad[:, None] * pos32 + lax.optimization_barrier(jnp.sum(neg_grad[:, :, None] * neg32, 1)))
    item_grad = jnp.zeros((ITEMS, E), jnp.float32)
    item_grad = item_grad.at[neg_rows.reshape(-1)].add(pair_neg.reshape(-1, E).astype(jnp.float32))
    item_grad = item_grad.at[pos_rows].add(pair_pos.astype(jnp.float32))
    emb_grad = jnp.concatenate([query_grad, item_grad], 0)
    tanh_grad = (emb_grad * (1.0 - embedding * embedding)).astype(jnp.bfloat16)
    grad_out = jnp.dot(hidden.T, tanh_grad, preferred_element_type=jnp.float32).astype(jnp.bfloat16)
    hidden_grad = jnp.dot(tanh_grad, w_out.T, preferred_element_type=jnp.float32)
    preact_grad = jnp.where(preact > 0, hidden_grad, 0.0).astype(jnp.bfloat16)
    grad_in = jnp.dot(features.T, preact_grad, preferred_element_type=jnp.float32).astype(jnp.bfloat16)
    return (grad_in, grad_out)
```

```python
import math

import jax
import jax.numpy as jnp
from jax import lax
from jax.sharding import Mesh, PartitionSpec as P

F32 = jnp.float32
BF16 = jnp.bfloat16
DP = ("z", "y", "c")


def exchange(blocks, axes):
    return lax.all_to_all(blocks, axes, split_axis=0, concat_axis=0, tiled=True)


def spread(block, axes):
    count = lax.axis_size(axes)
    return exchange(jnp.broadcast_to(block[None], (count,) + block.shape), axes)


def total(blocks):
    return jnp.sum(blocks.astype(F32), 0)


def request_codes(negatives, owner_map, dp_count, item_count, capacity):
    query_count, negative_count = negatives.shape
    rows = jnp.take(owner_map, negatives.reshape(-1), axis=0)
    pairs = rows.shape[0]
    owners = rows // item_count
    code = rows - owners * item_count + 1
    owner_hot = owners[:, None] == jnp.arange(dp_count, dtype=jnp.int32)[None, :]
    earlier = jnp.arange(pairs)[:, None] >= jnp.arange(pairs)[None, :]
    running = jnp.dot(earlier.astype(BF16), owner_hot.astype(BF16), preferred_element_type=F32)
    slot = jnp.sum(jnp.where(owner_hot, running, 0.0), 1).astype(jnp.int32) - 1
    query = jnp.arange(pairs, dtype=jnp.int32) // negative_count
    place = query * capacity + slot
    place_hot = place[:, None] == jnp.arange(query_count * capacity, dtype=jnp.int32)[None, :]
    high = jnp.where(place_hot, (code // 32)[:, None], 0).astype(BF16)
    low = jnp.where(place_hot, (code % 32)[:, None], 0).astype(BF16)
    return lax.dot_general(
        owner_hot.astype(BF16),
        jnp.concatenate([high, low], 1),
        (((0,), (0,)), ((), ())),
        preferred_element_type=F32,
    ).astype(BF16)


def local(query_feats, item_feats, w_in, w_out, negatives, positives, owner_map):
    dp_count = lax.axis_size(DP)
    own_index = lax.axis_index(DP)
    z_count, y_count, c_count = (lax.axis_size(a) for a in DP)
    x_count = lax.axis_size("x")
    yc_count = y_count * c_count
    query_count = query_feats.shape[0]
    item_count = item_feats.shape[0]
    width = w_out.shape[1]
    negative_count = negatives.shape[1]
    scale = 4.0 / math.sqrt(width)
    capacity = 4 * query_count * negative_count // dp_count
    queries = query_count * dp_count

    codes = request_codes(negatives, owner_map, dp_count, item_count, capacity)
    pos_local = jnp.take(owner_map, positives, axis=0) - own_index * item_count

    hidden = jnp.maximum(jnp.dot(item_feats, w_in, preferred_element_type=F32), 0.0).astype(BF16)
    hidden_q = jnp.maximum(jnp.dot(query_feats, w_in, preferred_element_type=F32), 0.0).astype(BF16)
    partial = jnp.dot(hidden, w_out, preferred_element_type=F32)
    partial_q = jnp.dot(hidden_q, w_out, preferred_element_type=F32)
    share = item_count // x_count
    blocks = jnp.concatenate(
        [
            partial.reshape(x_count, share, width),
            jnp.broadcast_to(jnp.pad(partial_q, ((0, 4), (0, 0)))[None], (x_count, 8, width)),
        ],
        1,
    )
    own = jnp.tanh(total(exchange(blocks, "x")))
    emb_q = own[share : share + query_count]
    item_emb = lax.all_gather(own[:share], "x", axis=0, tiled=True)

    message = jnp.concatenate(
        [
            jnp.broadcast_to(emb_q.astype(BF16).reshape(1, -1), (dp_count, query_count * width)),
            codes,
        ],
        1,
    )
    asked = exchange(message, DP)
    all_q = asked[:, : query_count * width].reshape(queries, width)
    got = asked[:, query_count * width :].astype(F32)
    half = query_count * capacity
    wanted = (got[:, :half] * 32.0 + got[:, half:]).astype(jnp.int32)
    wanted = wanted.reshape(queries, capacity).T

    emb16 = item_emb.astype(BF16)
    row_id = jnp.arange(item_count, dtype=jnp.int32)
    column = jnp.arange(queries, dtype=jnp.int32)
    own_column = column - own_index * query_count
    pos_of = jnp.where(
        (own_column >= 0) & (own_column < query_count),
        jnp.sum(jnp.where(own_column[None, :] == jnp.arange(query_count)[:, None], pos_local[:, None], 0), 0),
        -1,
    )
    pos_hot = row_id[:, None] == pos_of[None, :]
    counts = jnp.sum((wanted[:, None, :] == row_id[None, :, None] + 1).astype(F32), 0)
    scores = lax.dot_general(emb16, all_q, (((1,), (1,)), ((), ())), preferred_element_type=F32)
    weight = (counts + pos_hot.astype(F32)) * jnp.exp(scale * scores)
    part_d = jnp.sum(weight, 0)
    part_u = lax.dot_general(
        weight.astype(BF16), emb16, (((0,), (0,)), ((), ())), preferred_element_type=F32
    ).astype(BF16)

    def split(d):
        high = d.astype(BF16)
        low = (d - high.astype(F32)).astype(BF16)
        return jnp.concatenate([high.reshape(-1, width), low.reshape(-1, width)], 0)

    d_rows = queries // width

    def joined(rows):
        return (rows[:d_rows] + rows[d_rows : 2 * d_rows]).reshape(queries)

    zq = queries // z_count
    first = total(
        exchange(
            jnp.concatenate(
                [
                    part_u.reshape(z_count, zq, width),
                    jnp.broadcast_to(jnp.pad(split(part_d), ((0, 4), (0, 0)))[None], (z_count, 8, width)),
                ],
                1,
            ),
            "z",
        )
    )
    second = total(
        exchange(
            jnp.concatenate(
                [
                    first[:zq].astype(BF16).reshape(yc_count, query_count, width),
                    jnp.broadcast_to(split(joined(first[zq:]))[None], (yc_count, 2 * d_rows, width)),
                ],
                1,
            ),
            ("y", "c"),
        )
    )
    denominator = joined(second[query_count:])
    own_d = lax.dynamic_slice(denominator, (own_index * query_count,), (query_count,))
    pos_emb = jnp.take(emb16, pos_local, axis=0).astype(F32)
    query_grad = scale * (second[:query_count] / own_d[:, None] - pos_emb)
    coefficient = scale * (weight / denominator[None, :] - pos_hot.astype(F32))
    item_grad = jnp.dot(coefficient.astype(BF16), all_q, preferred_element_type=F32)
    tanh_grad = (item_grad * (1.0 - item_emb * item_emb)).astype(BF16)
    tanh_grad_q = (query_grad * (1.0 - emb_q * emb_q)).astype(BF16)

    def back(feats, hid, grad):
        out_term = lax.dot_general(hid, grad, (((0,), (0,)), ((), ())), preferred_element_type=F32)
        hid_grad = lax.dot_general(grad, w_out, (((1,), (1,)), ((), ())), preferred_element_type=F32)
        pre_grad = jnp.where(hid > 0, hid_grad, 0.0).astype(BF16)
        in_term = lax.dot_general(feats, pre_grad, (((0,), (0,)), ((), ())), preferred_element_type=F32)
        return in_term, out_term

    in_i, out_i = back(item_feats, hidden, tanh_grad)
    in_q, out_q = back(query_feats, hidden_q, tanh_grad_q)
    grads = jnp.concatenate([in_i + in_q, out_i + out_q], 0)
    depth = grads.shape[0]
    grads = total(exchange(grads.astype(BF16).reshape(c_count, depth // c_count, width), "c"))
    grads = total(exchange(grads.astype(BF16).reshape(y_count, -1, width), "y"))
    grads = total(spread(grads.astype(BF16), "z")).astype(BF16)
    grads = spread(grads, "y").reshape(-1, width)
    grads = spread(grads, "c").reshape(-1, width)
    return grads[: w_in.shape[0]], grads[w_in.shape[0] :]


def solution(mesh):
    grid = Mesh(mesh.devices.reshape(8, 8, 2, 4), ("z", "y", "c", "x"))
    return jax.shard_map(
        local,
        mesh=grid,
        in_specs=(
            P(DP, None),
            P(DP, None),
            P(None, "x"),
            P("x", None),
            P(DP, None),
            P(DP),
            P(),
        ),
        out_specs=(P(None, "x"), P("x", None)),
        check_vma=False,
    )
```

```python
import functools
import math

import jax
import jax.numpy as jnp
from jax import lax
from jax.experimental import pallas as pl
from jax.experimental.pallas import tpu as pltpu
from jax.sharding import Mesh, PartitionSpec as P

F32 = jnp.float32
BF16 = jnp.bfloat16
DP = ("z", "y", "c")
YCZ = ("y", "c", "z")
ROWS = 256
VMEM = 48 * 1024 * 1024


def exchange(blocks, axes):
    return lax.all_to_all(blocks, axes, split_axis=0, concat_axis=0, tiled=True)


def spread(block, axes):
    count = lax.axis_size(axes)
    return exchange(jnp.broadcast_to(block[None], (count,) + block.shape), axes)


def total(blocks):
    return jnp.sum(blocks.astype(F32), 0)


def dot(a, b):
    return jnp.dot(a, b, preferred_element_type=F32)


def dot_rows(a, b):
    return lax.dot_general(a, b, (((0,), (0,)), ((), ())), preferred_element_type=F32)


def dot_lanes(a, b):
    return lax.dot_general(a, b, (((1,), (1,)), ((), ())), preferred_element_type=F32)


def forward_kernel(q_ref, x_ref, w_in_ref, w_out_ref, part_ref, hid_ref, hid_q_ref, keep, rows):
    @pl.when(pl.program_id(0) == 0)
    def _():
        few = q_ref.shape[0]
        hid_q = jnp.maximum(dot(q_ref[...], w_in_ref[...]), 0.0)
        rows[...] = jnp.zeros_like(rows)
        rows[:few, :] = hid_q
        hid_q_ref[...] = rows[...].astype(BF16)
        keep[...] = dot(hid_q_ref[...], w_out_ref[...])

    hid = jnp.maximum(dot(x_ref[...], w_in_ref[...]), 0.0).astype(BF16)
    hid_ref[...] = hid
    part_ref[0, : hid.shape[0], :] = dot(hid, w_out_ref[...])
    part_ref[0, hid.shape[0] :, :] = keep[:8, :]


def forward(query_feats, item_feats, w_in, w_out):
    few, feats = query_feats.shape
    items = item_feats.shape[0]
    units = w_in.shape[1]
    width = w_out.shape[1]
    steps = items // ROWS
    return pl.pallas_call(
        forward_kernel,
        grid=(steps,),
        in_specs=[
            pl.BlockSpec((few, feats), lambda i: (0, 0)),
            pl.BlockSpec((ROWS, feats), lambda i: (i, 0)),
            pl.BlockSpec((feats, units), lambda i: (0, 0)),
            pl.BlockSpec((units, width), lambda i: (0, 0)),
        ],
        out_specs=[
            pl.BlockSpec((1, ROWS + 8, width), lambda i: (i, 0, 0)),
            pl.BlockSpec((ROWS, units), lambda i: (i, 0)),
            pl.BlockSpec((16, units), lambda i: (0, 0)),
        ],
        out_shape=[
            jax.ShapeDtypeStruct((steps, ROWS + 8, width), F32),
            jax.ShapeDtypeStruct((items, units), BF16),
            jax.ShapeDtypeStruct((16, units), BF16),
        ],
        scratch_shapes=[pltpu.VMEM((16, width), F32), pltpu.VMEM((16, units), F32)],
        compiler_params=pltpu.CompilerParams(vmem_limit_bytes=VMEM),
    )(query_feats, item_feats, w_in, w_out)


def position_row(info_ref, queries, few):
    lane = lax.broadcasted_iota(jnp.int32, (1, queries), 1)
    row = jnp.zeros((1, queries), F32)
    for i in range(few):
        row = jnp.where(lane == info_ref[few] + i, (info_ref[i] + 1).astype(F32), row)
    return row


def row_ids(shape):
    first = pl.program_id(0) * shape[0] + 1
    return (lax.broadcasted_iota(jnp.int32, shape, 0) + first).astype(F32)


def score_kernel(few, scale, info_ref, e_ref, msg_ref, weight_ref, u_ref, d_ref, codes, total_u, total_d):
    step = pl.program_id(0)
    queries = msg_ref.shape[0]
    width = e_ref.shape[1]
    slots = codes.shape[0] - 8

    @pl.when(step == 0)
    def _():
        turned = msg_ref[:, width:].astype(F32).T
        codes[:slots, :] = turned[:slots] * 32.0 + turned[slots : 2 * slots]
        codes[slots:, :] = jnp.broadcast_to(position_row(info_ref, queries, few), (8, queries))
        total_u[...] = jnp.zeros_like(total_u)
        total_d[...] = jnp.zeros_like(total_d)

    e16 = e_ref[...].astype(BF16)
    scores = dot_lanes(e16, msg_ref[:, :width])
    ids = row_ids(scores.shape)
    count = jnp.zeros_like(scores)
    for s in range(slots + 1):
        count = count + jnp.where(codes[s : s + 1, :] == ids, 1.0, 0.0)
    weight = count * jnp.exp(scale * scores)
    weight_ref[...] = weight
    total_d[...] += jnp.sum(weight, 0, keepdims=True)
    total_u[...] += dot_rows(weight.astype(BF16), e16)

    @pl.when(step == pl.num_programs(0) - 1)
    def _():
        u_ref[...] = total_u[...].astype(BF16)
        d_ref[...] = total_d[...]


def score(info, item_emb, message, few, capacity, scale):
    items, width = item_emb.shape
    queries, wide = message.shape
    return pl.pallas_call(
        functools.partial(score_kernel, few, scale),
        grid=(items // ROWS,),
        in_specs=[
            pl.BlockSpec(memory_space=pltpu.SMEM),
            pl.BlockSpec((ROWS, width), lambda i: (i, 0)),
            pl.BlockSpec((queries, wide), lambda i: (0, 0)),
        ],
        out_specs=[
            pl.BlockSpec((ROWS, queries), lambda i: (i, 0)),
            pl.BlockSpec((queries, width), lambda i: (0, 0)),
            pl.BlockSpec((1, queries), lambda i: (0, 0)),
        ],
        out_shape=[
            jax.ShapeDtypeStruct((items, queries), F32),
            jax.ShapeDtypeStruct((queries, width), BF16),
            jax.ShapeDtypeStruct((1, queries), F32),
        ],
        scratch_shapes=[
            pltpu.VMEM((capacity + 8, queries), F32),
            pltpu.VMEM((queries, width), F32),
            pltpu.VMEM((1, queries), F32),
        ],
        compiler_params=pltpu.CompilerParams(vmem_limit_bytes=VMEM),
    )(info, item_emb, message)


def backward_kernel(
    few, scale, info_ref, sums_ref, weight_ref, e_ref, msg_ref, hid_ref, x_ref, w_out_ref,
    emb_q_ref, hid_q_ref, q_ref, out_ref, factor, denom, pos, pos_emb, in_total, out_total,
):
    step = pl.program_id(0)
    queries = msg_ref.shape[0]
    width = e_ref.shape[1]
    feats = x_ref.shape[1]

    @pl.when(step == 0)
    def _():
        sums = jnp.sum(sums_ref[...].astype(F32), 0)
        d = sums[few : few + 2] + sums[few + 2 : few + 4]
        d = jnp.concatenate([d[0:1], d[1:2]], 1)
        denom[...] = d
        factor[...] = scale / d
        pos[...] = position_row(info_ref, queries, few)
        pos_emb[...] = jnp.zeros_like(pos_emb)
        in_total[...] = jnp.zeros_like(in_total)
        out_total[...] = jnp.zeros_like(out_total)

    def accumulate(hid, grad, feats_rows):
        out_total[...] += dot_rows(hid, grad)
        hid_grad = dot_lanes(grad, w_out_ref[...])
        pre_grad = jnp.where(hid > 0, hid_grad, 0.0).astype(BF16)
        in_total[...] += dot_rows(pre_grad, feats_rows)

    e = e_ref[...]
    weight = weight_ref[...]
    hot = jnp.where(pos[...] == row_ids(weight.shape), scale, 0.0)
    coefficient = (weight * factor[...] - hot).astype(BF16)
    item_grad = dot(coefficient, msg_ref[:, :width])
    accumulate(hid_ref[...], (item_grad * (1.0 - e * e)).astype(BF16), x_ref[...])

    lane = lax.broadcasted_iota(jnp.int32, (16, ROWS), 1) + step * ROWS
    line = lax.broadcasted_iota(jnp.int32, (16, ROWS), 0)
    picked = jnp.zeros((16, ROWS), F32)
    for i in range(few):
        picked = jnp.where((line == i) & (lane == info_ref[i]), 1.0, picked)
    pos_emb[...] += dot(picked.astype(BF16), e.astype(BF16))

    @pl.when(step == pl.num_programs(0) - 1)
    def _():
        sums = jnp.sum(sums_ref[...].astype(F32), 0)
        sums = jnp.concatenate([sums, jnp.zeros_like(sums)], 0)
        line = lax.broadcasted_iota(jnp.int32, (16, queries), 0)
        column = lax.broadcasted_iota(jnp.int32, (16, queries), 1)
        own_d = jnp.sum(jnp.where(column == line + info_ref[few], denom[...], 0.0), 1, keepdims=True)
        live = lax.broadcasted_iota(jnp.int32, sums.shape, 0) < few
        emb_q = emb_q_ref[...]
        grad = scale * (sums / own_d - pos_emb[...]) * (1.0 - emb_q * emb_q)
        accumulate(hid_q_ref[...], jnp.where(live, grad, 0.0).astype(BF16), q_ref[...])
        out_ref[:feats, :] = in_total[...].astype(BF16).T
        out_ref[feats:, :] = out_total[...].astype(BF16)


def backward(info, sums, weight, item_emb, message, hidden, item_feats, w_out, emb_q, hidden_q, feats_q, few, scale):
    items, width = item_emb.shape
    queries, wide = message.shape
    feats = item_feats.shape[1]
    units = hidden.shape[1]

    def whole(a):
        return pl.BlockSpec(a.shape, lambda i: (0,) * a.ndim)

    def part(a):
        return pl.BlockSpec((ROWS, a.shape[1]), lambda i: (i, 0))

    return pl.pallas_call(
        functools.partial(backward_kernel, few, scale),
        grid=(items // ROWS,),
        in_specs=[
            pl.BlockSpec(memory_space=pltpu.SMEM),
            whole(sums),
            part(weight),
            part(item_emb),
            whole(message),
            part(hidden),
            part(item_feats),
            whole(w_out),
            whole(emb_q),
            whole(hidden_q),
            whole(feats_q),
        ],
        out_specs=pl.BlockSpec((feats + units, width), lambda i: (0, 0)),
        out_shape=jax.ShapeDtypeStruct((feats + units, width), BF16),
        scratch_shapes=[
            pltpu.VMEM((1, queries), F32),
            pltpu.VMEM((1, queries), F32),
            pltpu.VMEM((1, queries), F32),
            pltpu.VMEM((16, width), F32),
            pltpu.VMEM((units, feats), F32),
            pltpu.VMEM((units, width), F32),
        ],
        compiler_params=pltpu.CompilerParams(vmem_limit_bytes=VMEM),
    )(info, sums, weight, item_emb, message, hidden, item_feats, w_out, emb_q, hidden_q, feats_q)


def request_codes(rows, query_count, item_count, capacity, order, dp_count):
    pairs = rows.shape[0]
    owners = rows // item_count
    code = rows - owners * item_count + 1
    owner_hot = order(owners)[:, None] == jnp.arange(dp_count, dtype=jnp.int32)[None, :]
    earlier = jnp.arange(pairs)[:, None] >= jnp.arange(pairs)[None, :]
    running = dot(earlier.astype(BF16), owner_hot.astype(BF16))
    slot = jnp.sum(jnp.where(owner_hot, running, 0.0), 1).astype(jnp.int32) - 1
    query = jnp.arange(pairs, dtype=jnp.int32) // (pairs // query_count)
    place = query * 2 * capacity + slot
    places = jnp.arange(query_count * 2 * capacity, dtype=jnp.int32)[None, :]
    high = jnp.where(place[:, None] == places, (code // 32)[:, None], 0)
    low = jnp.where(place[:, None] + capacity == places, (code % 32)[:, None], 0)
    return dot_rows(owner_hot.astype(BF16), (high + low).astype(BF16)).astype(BF16)


def local(query_feats, item_feats, w_in, w_out, negatives, positives, owner_map):
    dp_count = lax.axis_size(DP)
    own_index = lax.axis_index(DP)
    z_count = lax.axis_size("z")
    x_count = lax.axis_size("x")
    yc_count = dp_count // z_count
    few = query_feats.shape[0]
    item_count = item_feats.shape[0]
    width = w_out.shape[1]
    negative_count = negatives.shape[1]
    scale = 4.0 / math.sqrt(width)
    capacity = 4 * few * negative_count // dp_count
    queries = few * dp_count

    blocks, hidden, hidden_q = forward(query_feats, item_feats, w_in, w_out)
    arrived = exchange(blocks, "x")

    named = jnp.concatenate([negatives.reshape(-1), positives])
    rows = jnp.take(owner_map, named, axis=0)
    pos_local = rows[few * negative_count :] - own_index * item_count
    info = jnp.concatenate([pos_local, lax.axis_index(YCZ).reshape(1) * few])
    codes = request_codes(
        rows[: few * negative_count],
        few,
        item_count,
        capacity,
        lambda o: (o % yc_count) * z_count + o // yc_count,
        dp_count,
    )
    codes = codes.reshape(dp_count, few, 2 * capacity)
    codes = jnp.pad(codes, ((0, 0), (0, 0), (0, 128 - 2 * capacity)))

    own = jnp.tanh(total(arrived[:, :ROWS]))
    own_q = jnp.tanh(total(arrived[:, ROWS:]))
    sent_q = jnp.broadcast_to(own_q[None, :few].astype(BF16), (dp_count, few, width))
    message = exchange(jnp.concatenate([sent_q, codes], 2), YCZ)
    message = message.reshape(queries, width + 128)
    item_emb = spread(own, "x").reshape(item_count, width)

    weight, part_u, part_d = score(info, item_emb, message, few, capacity, scale)

    def split(d):
        high = d.astype(BF16)
        low = (d - high.astype(F32)).astype(BF16)
        return jnp.concatenate([high.reshape(-1, width), low.reshape(-1, width)], 0)

    d_rows = queries // width
    mine = queries // yc_count
    first = total(
        exchange(
            jnp.concatenate(
                [
                    part_u.reshape(yc_count, mine, width),
                    jnp.broadcast_to(
                        jnp.pad(split(part_d), ((0, 8 - 2 * d_rows), (0, 0)))[None], (yc_count, 8, width)
                    ),
                ],
                1,
            ),
            ("y", "c"),
        )
    )
    d_part = first[mine : mine + d_rows] + first[mine + d_rows : mine + 2 * d_rows]
    sums = exchange(
        jnp.concatenate(
            [
                first[:mine].astype(BF16).reshape(z_count, few, width),
                jnp.broadcast_to(split(d_part)[None], (z_count, 2 * d_rows, width)),
            ],
            1,
        ),
        "z",
    )
    emb_q = jnp.pad(own_q, ((0, 8), (0, 0)))
    feats_q = jnp.pad(query_feats, ((0, 16 - few), (0, 0)))
    grads = backward(
        info, sums, weight, item_emb, message, hidden, item_feats, w_out, emb_q, hidden_q, feats_q, few, scale
    )
    depth = grads.shape[0]
    c_count, y_count = lax.axis_size("c"), lax.axis_size("y")
    grads = total(exchange(grads.reshape(c_count, depth // c_count, width), "c"))
    grads = total(exchange(grads.astype(BF16).reshape(y_count, -1, width), "y"))
    grads = total(spread(grads.astype(BF16), "z")).astype(BF16)
    grads = spread(grads, "y").reshape(-1, width)
    grads = spread(grads, "c").reshape(-1, width)
    return grads[: w_in.shape[0]], grads[w_in.shape[0] :]


def solution(mesh):
    grid = Mesh(mesh.devices.reshape(8, 8, 2, 4), ("z", "y", "c", "x"))
    return jax.shard_map(
        local,
        mesh=grid,
        in_specs=(
            P(DP, None),
            P(DP, None),
            P(None, "x"),
            P("x", None),
            P(DP, None),
            P(DP),
            P(),
        ),
        out_specs=(P(None, "x"), P("x", None)),
        check_vma=False,
    )
```

```python
import functools
import math

import jax
import jax.numpy as jnp
from jax import lax
from jax.experimental import pallas as pl
from jax.experimental.pallas import tpu as pltpu
from jax.sharding import Mesh, PartitionSpec as P

F32 = jnp.float32
BF16 = jnp.bfloat16
DP = ("z", "y", "c")
YCZ = ("y", "c", "z")
ROWS = 256
VMEM = 20 * 1024 * 1024


def exchange(blocks, axes):
    return lax.all_to_all(blocks, axes, split_axis=0, concat_axis=0, tiled=True)


def spread(block, axes):
    count = lax.axis_size(axes)
    return exchange(jnp.broadcast_to(block[None], (count,) + block.shape), axes)


def total(blocks):
    return jnp.sum(blocks.astype(F32), 0)


def dot(a, b):
    return jnp.dot(a, b, preferred_element_type=F32)


def dot_rows(a, b):
    return lax.dot_general(a, b, (((0,), (0,)), ((), ())), preferred_element_type=F32)


def dot_lanes(a, b):
    return lax.dot_general(a, b, (((1,), (1,)), ((), ())), preferred_element_type=F32)


def forward_kernel(
    q_ref, x_hbm, w_in_hbm, w_out_hbm, part_hbm, hid_ref, hid_q_ref, x_buf, w_in_buf, w_out_buf, part_buf, rows, sems
):
    steps = part_buf.shape[0]
    few = q_ref.shape[0]
    chunks = [pl.ds(i * ROWS, ROWS) for i in range(steps)]
    loads = [
        pltpu.make_async_copy(w_in_hbm, w_in_buf, sems.at[0]),
        pltpu.make_async_copy(w_out_hbm, w_out_buf, sems.at[1]),
    ]
    for i, chunk in enumerate(chunks):
        loads.append(pltpu.make_async_copy(x_hbm.at[chunk, :], x_buf.at[chunk, :], sems.at[2 + i]))
    for load in loads:
        load.start()
    rows[...] = jnp.zeros_like(rows)
    loads[0].wait()
    rows[:few, :] = jnp.maximum(dot(q_ref[...], w_in_buf[...]), 0.0)
    hid_q = rows[...].astype(BF16)
    hid_q_ref[...] = hid_q
    loads[1].wait()
    keep = dot(hid_q, w_out_buf[...])[:8]
    stores = []
    for i, chunk in enumerate(chunks):
        loads[2 + i].wait()
        hid = jnp.maximum(dot(x_buf[chunk, :], w_in_buf[...]), 0.0).astype(BF16)
        hid_ref[chunk, :] = hid
        part_buf[i, :ROWS, :] = dot(hid, w_out_buf[...])
        part_buf[i, ROWS:, :] = keep
        stores.append(pltpu.make_async_copy(part_buf.at[i], part_hbm.at[i], sems.at[2 + steps + i]))
        stores[i].start()
    for store in stores:
        store.wait()


def forward(query_feats, item_feats, w_in, w_out):
    items, feats = item_feats.shape
    units = w_in.shape[1]
    width = w_out.shape[1]
    steps = items // ROWS
    anywhere = pl.BlockSpec(memory_space=pltpu.HBM)
    near = pl.BlockSpec(memory_space=pltpu.VMEM)
    return pl.pallas_call(
        forward_kernel,
        in_specs=[near, anywhere, anywhere, anywhere],
        out_specs=[anywhere, near, near],
        out_shape=[
            jax.ShapeDtypeStruct((steps, ROWS + 8, width), F32),
            jax.ShapeDtypeStruct((items, units), BF16),
            jax.ShapeDtypeStruct((16, units), BF16),
        ],
        scratch_shapes=[
            pltpu.VMEM((items, feats), BF16),
            pltpu.VMEM((feats, units), BF16),
            pltpu.VMEM((units, width), BF16),
            pltpu.VMEM((steps, ROWS + 8, width), F32),
            pltpu.VMEM((16, units), F32),
            pltpu.SemaphoreType.DMA((2 + 2 * steps,)),
        ],
        compiler_params=pltpu.CompilerParams(vmem_limit_bytes=VMEM),
    )(query_feats, item_feats, w_in, w_out)


def row_ids(block, shape):
    return (lax.broadcasted_iota(jnp.int32, shape, 0) + block * shape[0]).astype(F32)


def score_kernel(
    few, slots, scale, info_ref, own_ref, by1_ref, by2_ref, by3_ref, msg_ref,
    weight_ref, e_ref, all_q_ref, pay_ref, code, digit, total_u,
):
    queries = msg_ref.shape[0]
    width = e_ref.shape[1]
    group = queries // few
    near = (own_ref, by1_ref, by2_ref, by3_ref)
    for far, ref in enumerate(near):
        first = lax.rem(info_ref[few + 1] + len(near) - far, len(near)) * ROWS
        e_ref[pl.ds(pl.multiple_of(first, ROWS), ROWS), :] = ref[...]

    line = lax.broadcasted_iota(jnp.int32, (queries, queries), 0)
    column = lax.broadcasted_iota(jnp.int32, (queries, queries), 1)
    order = jnp.where(column == (line % group) * few + line // group, 1.0, 0.0).astype(BF16)
    turned = dot(order, msg_ref[...])
    all_q = turned[:, :width].astype(BF16)
    all_q_ref[...] = all_q
    asked = turned[:group, width:].T
    who = asked[2 * slots : 3 * slots]
    code[:slots, :] = jnp.where(who > 0.0, asked[:slots] * 32.0 + asked[slots : 2 * slots], -1.0)
    power = jnp.zeros_like(who)
    for i in range(few):
        power = jnp.where(who == i + 1.0, 32.0**i, power)
    digit[:slots, :] = power
    lane = lax.broadcasted_iota(jnp.int32, (1, group), 1)
    for i in range(few):
        code[slots + i : slots + i + 1, :] = jnp.where(lane == info_ref[few], info_ref[i], -1).astype(F32)
        digit[slots + i : slots + i + 1, :] = jnp.full((1, group), 32.0**i, F32)

    total_d = jnp.zeros((1, queries), F32)
    for block in range(e_ref.shape[0] // ROWS):
        chunk = pl.ds(block * ROWS, ROWS)
        e16 = e_ref[chunk, :].astype(BF16)
        grown = jnp.exp(scale * dot_lanes(e16, all_q))
        ids = row_ids(block, (ROWS, group))
        digits = jnp.zeros((ROWS, group), F32)
        for s in range(slots + few):
            digits = digits + jnp.where(code[s : s + 1, :] == ids, digit[s : s + 1, :], 0.0)
        digits = digits.astype(jnp.int32)
        times = [((digits >> (5 * i)) & 31).astype(F32) for i in range(few)]
        weight = jnp.concatenate(times, 1) * grown
        weight_ref[chunk, :] = weight
        total_d = total_d + jnp.sum(weight, 0, keepdims=True)
        part = dot_rows(weight.astype(BF16), e16)
        total_u[...] = part if block == 0 else total_u[...] + part

    d = jnp.concatenate([total_d[:, i * width : (i + 1) * width] for i in range(queries // width)], 0)
    high = d.astype(BF16).astype(F32)
    tail = jnp.concatenate([high, d - high, jnp.zeros((8 - 2 * d.shape[0], width), F32)], 0)
    for y in range(pay_ref.shape[0]):
        mine = [total_u[i * group + y * 8 : i * group + y * 8 + 8, :] for i in range(few)]
        pay_ref[y] = jnp.concatenate([*mine, tail], 0).astype(BF16)


def score(info, embs, message, few, slots, scale, peers):
    share, width = embs[0].shape
    items = share * len(embs)
    queries, wide = message.shape
    near = pl.BlockSpec(memory_space=pltpu.VMEM)
    return pl.pallas_call(
        functools.partial(score_kernel, few, slots, scale),
        in_specs=[pl.BlockSpec(memory_space=pltpu.SMEM)] + [near] * (len(embs) + 1),
        out_specs=[near] * 4,
        out_shape=[
            jax.ShapeDtypeStruct((items, queries), F32),
            jax.ShapeDtypeStruct((items, width), F32),
            jax.ShapeDtypeStruct((queries, width), BF16),
            jax.ShapeDtypeStruct((peers, queries // peers + 8, width), BF16),
        ],
        scratch_shapes=[
            pltpu.VMEM((slots + 8, queries // few), F32),
            pltpu.VMEM((slots + 8, queries // few), F32),
            pltpu.VMEM((queries, width), F32),
        ],
        compiler_params=pltpu.CompilerParams(vmem_limit_bytes=VMEM),
    )(info, *embs, message)


def backward_kernel(
    few, scale, info_ref, sums_ref, weight_ref, e_ref, all_q_ref, hid_ref, x_ref, w_out_ref,
    emb_q_ref, hid_q_ref, q_ref, out_ref, tanh_grad, pre_grad,
):
    queries = all_q_ref.shape[0]
    items, width = e_ref.shape
    feats = x_ref.shape[1]
    group = queries // few
    sums = jnp.sum(sums_ref[...].astype(F32), 0)
    d = sums[few : few + 2] + sums[few + 2 : few + 4]
    d = jnp.concatenate([d[0:1], d[1:2]], 1)
    factor = scale / d
    lane = lax.broadcasted_iota(jnp.int32, (1, queries), 1)
    position = jnp.full((1, queries), -1.0, F32)
    for i in range(few):
        position = jnp.where(lane == info_ref[few] + i * group, info_ref[i].astype(F32), position)

    pos_emb = jnp.zeros((16, width), F32)
    for block in range(items // ROWS):
        chunk = pl.ds(block * ROWS, ROWS)
        e = e_ref[chunk, :]
        hot = jnp.where(position == row_ids(block, (ROWS, queries)), scale, 0.0)
        coefficient = (weight_ref[chunk, :] * factor - hot).astype(BF16)
        grad = (dot(coefficient, all_q_ref[...]) * (1.0 - e * e)).astype(BF16)
        tanh_grad[chunk, :] = grad
        hid_grad = dot_lanes(grad, w_out_ref[...])
        pre_grad[chunk, :] = jnp.where(hid_ref[chunk, :] > 0, hid_grad, 0.0).astype(BF16)
        place = lax.broadcasted_iota(jnp.int32, (16, ROWS), 1) + block * ROWS
        line = lax.broadcasted_iota(jnp.int32, (16, ROWS), 0)
        picked = jnp.zeros((16, ROWS), F32)
        for i in range(few):
            picked = jnp.where((line == i) & (place == info_ref[i]), 1.0, picked)
        pos_emb = pos_emb + dot(picked.astype(BF16), e.astype(BF16))

    line = lax.broadcasted_iota(jnp.int32, (8, queries), 0)
    own_lane = lax.broadcasted_iota(jnp.int32, (8, queries), 1)
    own_d = jnp.sum(jnp.where(own_lane == line * group + info_ref[few], d, 0.0), 1, keepdims=True)
    live = lax.broadcasted_iota(jnp.int32, (8, width), 0) < few
    emb_q = emb_q_ref[...]
    grad = scale * (sums / own_d - pos_emb[:8]) * (1.0 - emb_q * emb_q)
    grad = jnp.where(live, grad, 0.0)
    grad_q = jnp.concatenate([grad, jnp.zeros_like(grad)], 0).astype(BF16)
    hid_q = hid_q_ref[...]
    pre_grad_q = jnp.where(hid_q > 0, dot_lanes(grad_q, w_out_ref[...]), 0.0).astype(BF16)
    out_ref[feats:, :] = (dot_rows(hid_ref[...], tanh_grad[...]) + dot_rows(hid_q, grad_q)).astype(BF16)
    in_total = dot_rows(pre_grad[...], x_ref[...]) + dot_rows(pre_grad_q, q_ref[...])
    out_ref[:feats, :] = in_total.astype(BF16).T


def backward(info, sums, weight, item_emb, all_q, hidden, item_feats, w_out, emb_q, hidden_q, feats_q, few, scale):
    items, width = item_emb.shape
    feats = item_feats.shape[1]
    units = hidden.shape[1]
    near = pl.BlockSpec(memory_space=pltpu.VMEM)
    return pl.pallas_call(
        functools.partial(backward_kernel, few, scale),
        in_specs=[pl.BlockSpec(memory_space=pltpu.SMEM)] + [near] * 10,
        out_specs=near,
        out_shape=jax.ShapeDtypeStruct((feats + units, width), BF16),
        scratch_shapes=[pltpu.VMEM((items, width), BF16), pltpu.VMEM((items, units), BF16)],
        compiler_params=pltpu.CompilerParams(vmem_limit_bytes=VMEM),
    )(info, sums, weight, item_emb, all_q, hidden, item_feats, w_out, emb_q, hidden_q, feats_q)


def request_codes(rows, query_count, item_count, capacity, order, dp_count):
    pairs = rows.shape[0]
    owners = rows // item_count
    code = rows - owners * item_count
    owner_hot = order(owners)[:, None] == jnp.arange(dp_count, dtype=jnp.int32)[None, :]
    earlier = jnp.arange(pairs)[:, None] >= jnp.arange(pairs)[None, :]
    running = dot(earlier.astype(BF16), owner_hot.astype(BF16))
    slot = jnp.sum(jnp.where(owner_hot, running, 0.0), 1).astype(jnp.int32) - 1
    who = jnp.arange(pairs, dtype=jnp.int32) // (pairs // query_count) + 1
    lane = jnp.arange(128, dtype=jnp.int32)[None, :]
    value = jnp.zeros((pairs, 128), jnp.int32)
    for at, part in enumerate((code // 32, code % 32, who)):
        value = jnp.where(slot[:, None] + at * capacity == lane, part[:, None], value)
    return dot_rows(owner_hot.astype(BF16), value.astype(BF16)).astype(BF16)


def local(query_feats, item_feats, w_in, w_out, negatives, positives, owner_map):
    dp_count = lax.axis_size(DP)
    own_index = lax.axis_index(DP)
    z_count = lax.axis_size("z")
    x_count = lax.axis_size("x")
    yc_count = dp_count // z_count
    few = query_feats.shape[0]
    item_count = item_feats.shape[0]
    width = w_out.shape[1]
    negative_count = negatives.shape[1]
    scale = 4.0 / math.sqrt(width)
    capacity = 4 * few * negative_count // dp_count
    queries = few * dp_count

    blocks, hidden, hidden_q = forward(query_feats, item_feats, w_in, w_out)
    arrived = exchange(blocks, "x")

    named = jnp.concatenate([negatives.reshape(-1), positives])
    rows = jnp.take(owner_map, named, axis=0)
    pos_local = rows[few * negative_count :] - own_index * item_count
    info = jnp.concatenate([pos_local, jnp.stack([lax.axis_index(YCZ), lax.axis_index("x")])])
    codes = request_codes(
        rows[: few * negative_count],
        few,
        item_count,
        capacity,
        lambda o: (o % yc_count) * z_count + o // yc_count,
        dp_count,
    )
    codes = jnp.pad(codes[:, None, :], ((0, 0), (0, few - 1), (0, 0)))

    own = jnp.tanh(total(arrived[:, :ROWS]))
    own_q = jnp.tanh(total(arrived[:, ROWS:]))
    sent_q = jnp.broadcast_to(own_q[None, :few].astype(BF16), (dp_count, few, width))
    message = exchange(jnp.concatenate([sent_q, codes], 2), YCZ)
    message = message.reshape(queries, width + 128)
    embs = [own]
    for far in range(1, x_count):
        embs.append(lax.ppermute(own, "x", [(i, (i + far) % x_count) for i in range(x_count)]))

    weight, item_emb, all_q, pay = score(info, embs, message, few, capacity, scale, yc_count)
    first = total(exchange(pay, ("y", "c")))
    mine = queries // yc_count
    d_rows = queries // width
    d_part = first[mine : mine + d_rows] + first[mine + d_rows : mine + 2 * d_rows]
    high = d_part.astype(BF16)
    tail = jnp.concatenate([high, (d_part - high.astype(F32)).astype(BF16)], 0)
    sums = exchange(
        jnp.concatenate(
            [
                first[:mine].astype(BF16).reshape(few, z_count, width).transpose(1, 0, 2),
                jnp.broadcast_to(tail[None], (z_count, 2 * d_rows, width)),
            ],
            1,
        ),
        "z",
    )
    feats_q = jnp.pad(query_feats, ((0, 16 - few), (0, 0)))
    grads = backward(
        info, sums, weight, item_emb, all_q, hidden, item_feats, w_out, own_q, hidden_q, feats_q, few, scale
    )
    depth = grads.shape[0]
    c_count, y_count = lax.axis_size("c"), lax.axis_size("y")
    grads = total(exchange(grads.reshape(c_count, depth // c_count, width), "c"))
    grads = total(exchange(grads.astype(BF16).reshape(y_count, -1, width), "y"))
    grads = total(spread(grads.astype(BF16), "z")).astype(BF16)
    grads = spread(grads, "y").reshape(-1, width)
    grads = spread(grads, "c").reshape(-1, width)
    return grads[: w_in.shape[0]], grads[w_in.shape[0] :]


def solution(mesh):
    grid = Mesh(mesh.devices.reshape(8, 8, 2, 4), ("z", "y", "c", "x"))
    return jax.shard_map(
        local,
        mesh=grid,
        in_specs=(
            P(DP, None),
            P(DP, None),
            P(None, "x"),
            P("x", None),
            P(DP, None),
            P(DP),
            P(),
        ),
        out_specs=(P(None, "x"), P("x", None)),
        check_vma=False,
    )
```

```python
import functools
import math

import jax
import jax.numpy as jnp
from jax import lax
from jax.experimental import pallas as pl
from jax.experimental.pallas import tpu as pltpu
from jax.sharding import Mesh, PartitionSpec as P

F32 = jnp.float32
BF16 = jnp.bfloat16
DP = ("z", "y", "c")
YCZ = ("y", "c", "z")
ROWS = 256
VMEM = 20 * 1024 * 1024


def exchange(blocks, axes):
    return lax.all_to_all(blocks, axes, split_axis=0, concat_axis=0, tiled=True)


def spread(block, axes):
    count = lax.axis_size(axes)
    return exchange(jnp.broadcast_to(block[None], (count,) + block.shape), axes)


def total(blocks):
    return jnp.sum(blocks.astype(F32), 0)


def dot(a, b):
    return jnp.dot(a, b, preferred_element_type=F32)


def dot_rows(a, b):
    return lax.dot_general(a, b, (((0,), (0,)), ((), ())), preferred_element_type=F32)


def dot_lanes(a, b):
    return lax.dot_general(a, b, (((1,), (1,)), ((), ())), preferred_element_type=F32)


def blocks_of(items):
    return [pl.ds(i * ROWS, ROWS) for i in range(items // ROWS)]


class Copies:
    def __init__(self, sems):
        self.sems = sems
        self.used = 0

    def start(self, source, target):
        copy = pltpu.make_async_copy(source, target, self.sems.at[self.used])
        copy.start()
        self.used += 1
        return copy


def forward_kernel(
    q_hbm, x_hbm, w_in_hbm, w_out_hbm, part_hbm, hid_hbm, hid_q_hbm,
    q_buf, x_buf, w_in_buf, w_out_buf, part_buf, hid_buf, hid_q_buf, rows, sems,
):
    few = q_buf.shape[0]
    chunks = blocks_of(x_buf.shape[0])
    copies = Copies(sems)
    load_in = copies.start(w_in_hbm, w_in_buf)
    load_q = copies.start(q_hbm, q_buf)
    load_x = [copies.start(x_hbm.at[chunks[0], :], x_buf.at[chunks[0], :])]
    load_out = copies.start(w_out_hbm, w_out_buf)
    for chunk in chunks[1:]:
        load_x.append(copies.start(x_hbm.at[chunk, :], x_buf.at[chunk, :]))
    rows[...] = jnp.zeros_like(rows)
    load_in.wait()
    load_q.wait()
    rows[:few, :] = jnp.maximum(dot(q_buf[...], w_in_buf[...]), 0.0)
    hid_q_buf[...] = rows[...].astype(BF16)
    stores = [copies.start(hid_q_buf, hid_q_hbm)]
    load_out.wait()
    keep = dot(hid_q_buf[...], w_out_buf[...])[:8]
    for i, chunk in enumerate(chunks):
        load_x[i].wait()
        hid = jnp.maximum(dot(x_buf[chunk, :], w_in_buf[...]), 0.0).astype(BF16)
        hid_buf[chunk, :] = hid
        part_buf[i, :ROWS, :] = dot(hid, w_out_buf[...])
        part_buf[i, ROWS:, :] = keep
        stores.append(copies.start(part_buf.at[i], part_hbm.at[i]))
        stores.append(copies.start(hid_buf.at[chunk, :], hid_hbm.at[chunk, :]))
    for store in stores:
        store.wait()


FAR = pl.BlockSpec(memory_space=pltpu.HBM)
NEAR = pl.BlockSpec(memory_space=pltpu.VMEM)


def pinned(*arrays):
    return [pltpu.with_memory_space_constraint(a, pltpu.HBM) for a in arrays]


def forward(query_feats, item_feats, w_in, w_out):
    few = query_feats.shape[0]
    items, feats = item_feats.shape
    units = w_in.shape[1]
    width = w_out.shape[1]
    steps = items // ROWS
    return pl.pallas_call(
        forward_kernel,
        in_specs=[FAR] * 4,
        out_specs=[FAR] * 3,
        out_shape=[
            pltpu.HBM((steps, ROWS + 8, width), F32),
            pltpu.HBM((items, units), BF16),
            pltpu.HBM((16, units), BF16),
        ],
        scratch_shapes=[
            pltpu.VMEM((few, feats), BF16),
            pltpu.VMEM((items, feats), BF16),
            pltpu.VMEM((feats, units), BF16),
            pltpu.VMEM((units, width), BF16),
            pltpu.VMEM((steps, ROWS + 8, width), F32),
            pltpu.VMEM((items, units), BF16),
            pltpu.VMEM((16, units), BF16),
            pltpu.VMEM((16, units), F32),
            pltpu.SemaphoreType.DMA((4 + 3 * steps,)),
        ],
        compiler_params=pltpu.CompilerParams(vmem_limit_bytes=VMEM),
    )(*pinned(query_feats, item_feats, w_in, w_out))


def row_ids(block, shape):
    return (lax.broadcasted_iota(jnp.int32, shape, 0) + block * shape[0]).astype(F32)


def score_kernel(
    few, slots, scale, info_ref, own_ref, by1_ref, by2_ref, by3_ref, msg_ref,
    weight_hbm, e_hbm, all_q_hbm, pay_hbm, weight_ref, e_ref, all_q_ref, pay_ref, code, digit, total_u, sems,
):
    copies = Copies(sems)
    queries = msg_ref.shape[0]
    width = e_ref.shape[1]
    group = queries // few
    near = (own_ref, by1_ref, by2_ref, by3_ref)
    for far, ref in enumerate(near):
        first = lax.rem(info_ref[few + 1] + len(near) - far, len(near)) * ROWS
        e_ref[pl.ds(pl.multiple_of(first, ROWS), ROWS), :] = ref[...]

    line = lax.broadcasted_iota(jnp.int32, (queries, queries), 0)
    column = lax.broadcasted_iota(jnp.int32, (queries, queries), 1)
    order = jnp.where(column == (line % group) * few + line // group, 1.0, 0.0).astype(BF16)
    turned = dot(order, msg_ref[...])
    all_q = turned[:, :width].astype(BF16)
    all_q_ref[...] = all_q
    stores = [copies.start(e_ref, e_hbm), copies.start(all_q_ref, all_q_hbm)]
    asked = turned[:group, width:].T
    who = asked[2 * slots : 3 * slots]
    code[:slots, :] = jnp.where(who > 0.0, asked[:slots] * 32.0 + asked[slots : 2 * slots], -1.0)
    power = jnp.zeros_like(who)
    for i in range(few):
        power = jnp.where(who == i + 1.0, 32.0**i, power)
    digit[:slots, :] = power
    lane = lax.broadcasted_iota(jnp.int32, (1, group), 1)
    for i in range(few):
        code[slots + i : slots + i + 1, :] = jnp.where(lane == info_ref[few], info_ref[i], -1).astype(F32)
        digit[slots + i : slots + i + 1, :] = jnp.full((1, group), 32.0**i, F32)

    total_d = jnp.zeros((1, queries), F32)
    for block, chunk in enumerate(blocks_of(e_ref.shape[0])):
        e16 = e_ref[chunk, :].astype(BF16)
        grown = jnp.exp(scale * dot_lanes(e16, all_q))
        ids = row_ids(block, (ROWS, group))
        digits = jnp.zeros((ROWS, group), F32)
        for s in range(slots + few):
            digits = digits + jnp.where(code[s : s + 1, :] == ids, digit[s : s + 1, :], 0.0)
        digits = digits.astype(jnp.int32)
        times = [((digits >> (5 * i)) & 31).astype(F32) for i in range(few)]
        weight = jnp.concatenate(times, 1) * grown
        weight_ref[chunk, :] = weight
        stores.append(copies.start(weight_ref.at[chunk, :], weight_hbm.at[chunk, :]))
        total_d = total_d + jnp.sum(weight, 0, keepdims=True)
        part = dot_rows(weight.astype(BF16), e16)
        total_u[...] = part if block == 0 else total_u[...] + part

    d = jnp.concatenate([total_d[:, i * width : (i + 1) * width] for i in range(queries // width)], 0)
    high = d.astype(BF16).astype(F32)
    tail = jnp.concatenate([high, d - high, jnp.zeros((8 - 2 * d.shape[0], width), F32)], 0)
    for y in range(pay_ref.shape[0]):
        mine = [total_u[i * group + y * 8 : i * group + y * 8 + 8, :] for i in range(few)]
        pay_ref[y] = jnp.concatenate([*mine, tail], 0).astype(BF16)
    stores.append(copies.start(pay_ref, pay_hbm))
    for store in stores:
        store.wait()


def score(info, embs, message, few, slots, scale, peers):
    share, width = embs[0].shape
    items = share * len(embs)
    queries, wide = message.shape
    pay = (peers, queries // peers + 8, width)
    return pl.pallas_call(
        functools.partial(score_kernel, few, slots, scale),
        in_specs=[pl.BlockSpec(memory_space=pltpu.SMEM)] + [NEAR] * (len(embs) + 1),
        out_specs=[FAR] * 4,
        out_shape=[
            pltpu.HBM((items, queries), F32),
            pltpu.HBM((items, width), F32),
            pltpu.HBM((queries, width), BF16),
            pltpu.HBM(pay, BF16),
        ],
        scratch_shapes=[
            pltpu.VMEM((items, queries), F32),
            pltpu.VMEM((items, width), F32),
            pltpu.VMEM((queries, width), BF16),
            pltpu.VMEM(pay, BF16),
            pltpu.VMEM((slots + 8, queries // few), F32),
            pltpu.VMEM((slots + 8, queries // few), F32),
            pltpu.VMEM((queries, width), F32),
            pltpu.SemaphoreType.DMA((3 + items // ROWS,)),
        ],
        compiler_params=pltpu.CompilerParams(vmem_limit_bytes=VMEM),
    )(info, *embs, message)


def backward_kernel(
    few, scale, info_ref, all_q_hbm, weight_hbm, e_hbm, hid_hbm, sums_ref, w_out_ref, x_ref,
    emb_q_ref, hid_q_ref, q_ref, out_ref, all_q_ref, weight_ref, e_ref, hid_ref, tanh_grad, pre_grad, sems,
):
    copies = Copies(sems)
    load_q = copies.start(all_q_hbm, all_q_ref)
    loads = []
    for chunk in blocks_of(e_ref.shape[0]):
        pairs = ((weight_hbm, weight_ref), (e_hbm, e_ref), (hid_hbm, hid_ref))
        loads.append([copies.start(source.at[chunk, :], target.at[chunk, :]) for source, target in pairs])
    queries = all_q_ref.shape[0]
    items, width = e_ref.shape
    feats = x_ref.shape[1]
    group = queries // few
    sums = jnp.sum(sums_ref[...].astype(F32), 0)
    d = sums[few : few + 2] + sums[few + 2 : few + 4]
    d = jnp.concatenate([d[0:1], d[1:2]], 1)
    factor = scale / d
    lane = lax.broadcasted_iota(jnp.int32, (1, queries), 1)
    position = jnp.full((1, queries), -1.0, F32)
    for i in range(few):
        position = jnp.where(lane == info_ref[few] + i * group, info_ref[i].astype(F32), position)

    pos_emb = jnp.zeros((16, width), F32)
    load_q.wait()
    for block, chunk in enumerate(blocks_of(items)):
        for copy in loads[block]:
            copy.wait()
        e = e_ref[chunk, :]
        hot = jnp.where(position == row_ids(block, (ROWS, queries)), scale, 0.0)
        coefficient = (weight_ref[chunk, :] * factor - hot).astype(BF16)
        grad = (dot(coefficient, all_q_ref[...]) * (1.0 - e * e)).astype(BF16)
        tanh_grad[chunk, :] = grad
        hid_grad = dot_lanes(grad, w_out_ref[...])
        pre_grad[chunk, :] = jnp.where(hid_ref[chunk, :] > 0, hid_grad, 0.0).astype(BF16)
        place = lax.broadcasted_iota(jnp.int32, (16, ROWS), 1) + block * ROWS
        line = lax.broadcasted_iota(jnp.int32, (16, ROWS), 0)
        picked = jnp.zeros((16, ROWS), F32)
        for i in range(few):
            picked = jnp.where((line == i) & (place == info_ref[i]), 1.0, picked)
        pos_emb = pos_emb + dot(picked.astype(BF16), e.astype(BF16))

    line = lax.broadcasted_iota(jnp.int32, (8, queries), 0)
    own_lane = lax.broadcasted_iota(jnp.int32, (8, queries), 1)
    own_d = jnp.sum(jnp.where(own_lane == line * group + info_ref[few], d, 0.0), 1, keepdims=True)
    live = lax.broadcasted_iota(jnp.int32, (8, width), 0) < few
    emb_q = emb_q_ref[...]
    grad = scale * (sums / own_d - pos_emb[:8]) * (1.0 - emb_q * emb_q)
    grad = jnp.where(live, grad, 0.0)
    grad_q = jnp.concatenate([grad, jnp.zeros_like(grad)], 0).astype(BF16)
    hid_q = hid_q_ref[...]
    pre_grad_q = jnp.where(hid_q > 0, dot_lanes(grad_q, w_out_ref[...]), 0.0).astype(BF16)
    out_ref[feats:, :] = (dot_rows(hid_ref[...], tanh_grad[...]) + dot_rows(hid_q, grad_q)).astype(BF16)
    in_total = dot_rows(pre_grad[...], x_ref[...]) + dot_rows(pre_grad_q, q_ref[...])
    out_ref[:feats, :] = in_total.astype(BF16).T


def backward(info, far, near, few, scale):
    items, width = far[2].shape
    units = far[3].shape[1]
    feats = near[2].shape[1]
    return pl.pallas_call(
        functools.partial(backward_kernel, few, scale),
        in_specs=[pl.BlockSpec(memory_space=pltpu.SMEM)] + [FAR] * len(far) + [NEAR] * len(near),
        out_specs=NEAR,
        out_shape=jax.ShapeDtypeStruct((feats + units, width), BF16),
        scratch_shapes=[
            *[pltpu.VMEM(a.shape, a.dtype) for a in far],
            pltpu.VMEM((items, width), BF16),
            pltpu.VMEM((items, units), BF16),
            pltpu.SemaphoreType.DMA((1 + 3 * (items // ROWS),)),
        ],
        compiler_params=pltpu.CompilerParams(vmem_limit_bytes=VMEM),
    )(info, *pinned(*far), *near)


def request_codes(rows, query_count, item_count, capacity, order, dp_count):
    pairs = rows.shape[0]
    owners = rows // item_count
    code = rows - owners * item_count
    owner_hot = order(owners)[:, None] == jnp.arange(dp_count, dtype=jnp.int32)[None, :]
    earlier = jnp.arange(pairs)[:, None] >= jnp.arange(pairs)[None, :]
    running = dot(earlier.astype(BF16), owner_hot.astype(BF16))
    slot = jnp.sum(jnp.where(owner_hot, running, 0.0), 1).astype(jnp.int32) - 1
    who = jnp.arange(pairs, dtype=jnp.int32) // (pairs // query_count) + 1
    lane = jnp.arange(128, dtype=jnp.int32)[None, :]
    value = jnp.zeros((pairs, 128), jnp.int32)
    for at, part in enumerate((code // 32, code % 32, who)):
        value = jnp.where(slot[:, None] + at * capacity == lane, part[:, None], value)
    return dot_rows(owner_hot.astype(BF16), value.astype(BF16)).astype(BF16)


def local(query_feats, item_feats, w_in, w_out, negatives, positives, owner_map):
    dp_count = lax.axis_size(DP)
    own_index = lax.axis_index(DP)
    z_count = lax.axis_size("z")
    x_count = lax.axis_size("x")
    yc_count = dp_count // z_count
    few = query_feats.shape[0]
    item_count = item_feats.shape[0]
    width = w_out.shape[1]
    negative_count = negatives.shape[1]
    scale = 4.0 / math.sqrt(width)
    capacity = 4 * few * negative_count // dp_count
    queries = few * dp_count

    blocks, hidden, hidden_q = forward(query_feats, item_feats, w_in, w_out)
    arrived = exchange(blocks, "x")

    named = jnp.concatenate([negatives.reshape(-1), positives])
    rows = jnp.take(owner_map, named, axis=0)
    pos_local = rows[few * negative_count :] - own_index * item_count
    info = jnp.concatenate([pos_local, jnp.stack([lax.axis_index(YCZ), lax.axis_index("x")])])
    codes = request_codes(
        rows[: few * negative_count],
        few,
        item_count,
        capacity,
        lambda o: (o % yc_count) * z_count + o // yc_count,
        dp_count,
    )
    codes = jnp.pad(codes[:, None, :], ((0, 0), (0, few - 1), (0, 0)))

    own = jnp.tanh(total(arrived[:, :ROWS]))
    own_q = jnp.tanh(total(arrived[:, ROWS:]))
    sent_q = jnp.broadcast_to(own_q[None, :few].astype(BF16), (dp_count, few, width))
    message = exchange(jnp.concatenate([sent_q, codes], 2), YCZ)
    message = message.reshape(queries, width + 128)
    embs = [own]
    for far in range(1, x_count):
        embs.append(lax.ppermute(own, "x", [(i, (i + far) % x_count) for i in range(x_count)]))

    weight, item_emb, all_q, pay = score(info, embs, message, few, capacity, scale, yc_count)
    first = total(exchange(pay, ("y", "c")))
    mine = queries // yc_count
    d_rows = queries // width
    d_part = first[mine : mine + d_rows] + first[mine + d_rows : mine + 2 * d_rows]
    high = d_part.astype(BF16)
    tail = jnp.concatenate([high, (d_part - high.astype(F32)).astype(BF16)], 0)
    sums = exchange(
        jnp.concatenate(
            [
                first[:mine].astype(BF16).reshape(few, z_count, width).transpose(1, 0, 2),
                jnp.broadcast_to(tail[None], (z_count, 2 * d_rows, width)),
            ],
            1,
        ),
        "z",
    )
    feats_q = jnp.pad(query_feats, ((0, 16 - few), (0, 0)))
    near = (sums, w_out, item_feats, own_q, hidden_q, feats_q)
    grads = backward(info, (all_q, weight, item_emb, hidden), near, few, scale)
    depth = grads.shape[0]
    c_count, y_count = lax.axis_size("c"), lax.axis_size("y")
    grads = total(exchange(grads.reshape(c_count, depth // c_count, width), "c"))
    grads = total(exchange(grads.astype(BF16).reshape(y_count, -1, width), "y"))
    grads = total(spread(grads.astype(BF16), "z")).astype(BF16)
    grads = spread(grads, "y").reshape(-1, width)
    grads = spread(grads, "c").reshape(-1, width)
    return grads[: w_in.shape[0]], grads[w_in.shape[0] :]


def solution(mesh):
    grid = Mesh(mesh.devices.reshape(8, 8, 2, 4), ("z", "y", "c", "x"))
    return jax.shard_map(
        local,
        mesh=grid,
        in_specs=(
            P(DP, None),
            P(DP, None),
            P(None, "x"),
            P("x", None),
            P(DP, None),
            P(DP),
            P(),
        ),
        out_specs=(P(None, "x"), P("x", None)),
        check_vma=False,
    )
```

```python
import functools
import math

import jax
import jax.numpy as jnp
from jax import lax
from jax.experimental import pallas as pl
from jax.experimental.pallas import tpu as pltpu
from jax.sharding import Mesh, PartitionSpec as P

F32 = jnp.float32
BF16 = jnp.bfloat16
DP = ("z", "y", "c")
YCZ = ("y", "c", "z")
ROWS = 256
VMEM = 20 * 1024 * 1024


def exchange(blocks, axes):
    return lax.all_to_all(blocks, axes, split_axis=0, concat_axis=0, tiled=True)


def spread(block, axes):
    count = lax.axis_size(axes)
    return exchange(jnp.broadcast_to(block[None], (count,) + block.shape), axes)


def total(blocks):
    return jnp.sum(blocks.astype(F32), 0)


def dot(a, b):
    return jnp.dot(a, b, preferred_element_type=F32)


def dot_rows(a, b):
    return lax.dot_general(a, b, (((0,), (0,)), ((), ())), preferred_element_type=F32)


def dot_lanes(a, b):
    return lax.dot_general(a, b, (((1,), (1,)), ((), ())), preferred_element_type=F32)


def blocks_of(items):
    return [pl.ds(i * ROWS, ROWS) for i in range(items // ROWS)]


class Copies:
    def __init__(self, sems):
        self.sems = sems
        self.used = 0

    def start(self, source, target):
        copy = pltpu.make_async_copy(source, target, self.sems.at[self.used])
        copy.start()
        self.used += 1
        return copy


def forward_kernel(
    q_hbm, x_hbm, w_in_hbm, w_out_hbm, part_hbm, hid_hbm, hid_q_hbm,
    q_buf, x_buf, w_in_buf, w_out_buf, part_buf, hid_buf, hid_q_buf, rows, sems,
):
    few = q_buf.shape[0]
    chunks = blocks_of(x_buf.shape[0])
    copies = Copies(sems)
    load_in = copies.start(w_in_hbm, w_in_buf)
    load_q = copies.start(q_hbm, q_buf)
    load_x = [copies.start(x_hbm.at[chunks[0], :], x_buf.at[chunks[0], :])]
    load_out = copies.start(w_out_hbm, w_out_buf)
    for chunk in chunks[1:]:
        load_x.append(copies.start(x_hbm.at[chunk, :], x_buf.at[chunk, :]))
    rows[...] = jnp.zeros_like(rows)
    load_in.wait()
    load_q.wait()
    rows[:few, :] = jnp.maximum(dot(q_buf[...], w_in_buf[...]), 0.0)
    hid_q_buf[...] = rows[...].astype(BF16)
    stores = [copies.start(hid_q_buf, hid_q_hbm)]
    load_out.wait()
    keep = dot(hid_q_buf[...], w_out_buf[...])[:8]
    for i, chunk in enumerate(chunks):
        load_x[i].wait()
        hid = jnp.maximum(dot(x_buf[chunk, :], w_in_buf[...]), 0.0).astype(BF16)
        hid_buf[chunk, :] = hid
        part_buf[i, :ROWS, :] = dot(hid, w_out_buf[...])
        part_buf[i, ROWS:, :] = keep
        stores.append(copies.start(part_buf.at[i], part_hbm.at[i]))
        stores.append(copies.start(hid_buf.at[chunk, :], hid_hbm.at[chunk, :]))
    for store in stores:
        store.wait()


FAR = pl.BlockSpec(memory_space=pltpu.HBM)
NEAR = pl.BlockSpec(memory_space=pltpu.VMEM)


def pinned(*arrays):
    return [pltpu.with_memory_space_constraint(a, pltpu.HBM) for a in arrays]


def forward(query_feats, item_feats, w_in, w_out):
    few = query_feats.shape[0]
    items, feats = item_feats.shape
    units = w_in.shape[1]
    width = w_out.shape[1]
    steps = items // ROWS
    return pl.pallas_call(
        forward_kernel,
        in_specs=[FAR] * 4,
        out_specs=[FAR] * 3,
        out_shape=[
            pltpu.HBM((steps, ROWS + 8, width), F32),
            pltpu.HBM((items, units), BF16),
            pltpu.HBM((16, units), BF16),
        ],
        scratch_shapes=[
            pltpu.VMEM((few, feats), BF16),
            pltpu.VMEM((items, feats), BF16),
            pltpu.VMEM((feats, units), BF16),
            pltpu.VMEM((units, width), BF16),
            pltpu.VMEM((steps, ROWS + 8, width), F32),
            pltpu.VMEM((items, units), BF16),
            pltpu.VMEM((16, units), BF16),
            pltpu.VMEM((16, units), F32),
            pltpu.SemaphoreType.DMA((4 + 3 * steps,)),
        ],
        compiler_params=pltpu.CompilerParams(vmem_limit_bytes=VMEM),
    )(*pinned(query_feats, item_feats, w_in, w_out))


def row_ids(block, shape):
    return (lax.broadcasted_iota(jnp.int32, shape, 0) + block * shape[0]).astype(F32)


def score_kernel(
    few, slots, scale, info_ref, own_ref, by1_ref, by2_ref, by3_ref, msg_ref,
    weight_hbm, layer_hbm, all_q_hbm, pay_hbm, weight_ref, layer_ref, all_q_ref, pay_ref, code, digit, total_u, sems,
):
    copies = Copies(sems)
    lines = msg_ref.shape[0]
    width = layer_ref.shape[1]
    queries = lines * 2
    group = queries // few
    near = (own_ref, by1_ref, by2_ref, by3_ref)
    for far, ref in enumerate(near):
        first = lax.rem(info_ref[few + 1] + len(near) - far, len(near)) * ROWS
        layer_ref[pl.ds(pl.multiple_of(first, ROWS), ROWS), :] = ref[...]

    line = lax.broadcasted_iota(jnp.int32, (lines, lines), 0)
    column = lax.broadcasted_iota(jnp.int32, (lines, lines), 1)
    order = jnp.where(column == (line % group) * 2 + line // group, 1.0, 0.0).astype(BF16)
    turned = dot(order, msg_ref[...])
    parts = []
    for i in range(few):
        first = (i % 2) * width
        parts.append(turned[(i // 2) * group : (i // 2 + 1) * group, first : first + width])
    all_q = jnp.concatenate(parts, 0).astype(BF16)
    all_q_ref[...] = all_q
    stores = [copies.start(layer_ref, layer_hbm), copies.start(all_q_ref, all_q_hbm)]
    asked = turned[:group, 2 * width :].T
    who = asked[2 * slots : 3 * slots]
    code[:slots, :] = jnp.where(who > 0.0, asked[:slots] * 32.0 + asked[slots : 2 * slots], -1.0)
    power = jnp.zeros_like(who)
    for i in range(few):
        power = jnp.where(who == i + 1.0, 32.0**i, power)
    digit[:slots, :] = power
    lane = lax.broadcasted_iota(jnp.int32, (1, group), 1)
    for i in range(few):
        code[slots + i : slots + i + 1, :] = jnp.where(lane == info_ref[few], info_ref[i], -1).astype(F32)
        digit[slots + i : slots + i + 1, :] = jnp.full((1, group), 32.0**i, F32)

    total_d = jnp.zeros((1, queries), F32)
    for block, chunk in enumerate(blocks_of(layer_ref.shape[0])):
        e16 = jnp.tanh(layer_ref[chunk, :].astype(F32)).astype(BF16)
        grown = jnp.exp(scale * dot_lanes(e16, all_q))
        ids = row_ids(block, (ROWS, group))
        digits = jnp.zeros((ROWS, group), F32)
        for s in range(slots + few):
            digits = digits + jnp.where(code[s : s + 1, :] == ids, digit[s : s + 1, :], 0.0)
        digits = digits.astype(jnp.int32)
        times = [((digits >> (5 * i)) & 31).astype(F32) for i in range(few)]
        weight = jnp.concatenate(times, 1) * grown
        weight16 = weight.astype(BF16)
        weight_ref[chunk, :] = weight16
        stores.append(copies.start(weight_ref.at[chunk, :], weight_hbm.at[chunk, :]))
        total_d = total_d + jnp.sum(weight, 0, keepdims=True)
        part = dot_rows(weight16, e16)
        total_u[...] = part if block == 0 else total_u[...] + part

    d = jnp.concatenate([total_d[:, i * width : (i + 1) * width] for i in range(queries // width)], 0)
    high = d.astype(BF16).astype(F32)
    tail = jnp.concatenate([high, d - high, jnp.zeros((8 - 2 * d.shape[0], width), F32)], 0)
    for y in range(pay_ref.shape[0]):
        mine = [total_u[i * group + y * 8 : i * group + y * 8 + 8, :] for i in range(few)]
        pay_ref[y] = jnp.concatenate([*mine, tail], 0).astype(BF16)
    stores.append(copies.start(pay_ref, pay_hbm))
    for store in stores:
        store.wait()


def score(info, layers, message, few, slots, scale, peers):
    share, width = layers[0].shape
    items = share * len(layers)
    queries = 2 * message.shape[0]
    pay = (peers, queries // peers + 8, width)
    return pl.pallas_call(
        functools.partial(score_kernel, few, slots, scale),
        in_specs=[pl.BlockSpec(memory_space=pltpu.SMEM)] + [NEAR] * (len(layers) + 1),
        out_specs=[FAR] * 4,
        out_shape=[
            pltpu.HBM((items, queries), BF16),
            pltpu.HBM((items, width), BF16),
            pltpu.HBM((queries, width), BF16),
            pltpu.HBM(pay, BF16),
        ],
        scratch_shapes=[
            pltpu.VMEM((items, queries), BF16),
            pltpu.VMEM((items, width), BF16),
            pltpu.VMEM((queries, width), BF16),
            pltpu.VMEM(pay, BF16),
            pltpu.VMEM((slots + 8, queries // few), F32),
            pltpu.VMEM((slots + 8, queries // few), F32),
            pltpu.VMEM((queries, width), F32),
            pltpu.SemaphoreType.DMA((3 + items // ROWS,)),
        ],
        compiler_params=pltpu.CompilerParams(vmem_limit_bytes=VMEM),
    )(info, *layers, message)


def backward_kernel(
    few, scale, info_ref, all_q_hbm, weight_hbm, layer_hbm, hid_hbm, sums_ref, w_out_ref, x_ref,
    emb_q_ref, hid_q_ref, q_ref, mine_ref, other_ref,
    all_q_ref, weight_ref, layer_ref, hid_ref, tanh_grad, pre_grad, summed, sems,
):
    copies = Copies(sems)
    load_q = copies.start(all_q_hbm, all_q_ref)
    loads = []
    for chunk in blocks_of(layer_ref.shape[0]):
        pairs = ((weight_hbm, weight_ref), (layer_hbm, layer_ref), (hid_hbm, hid_ref))
        loads.append([copies.start(source.at[chunk, :], target.at[chunk, :]) for source, target in pairs])
    queries = all_q_ref.shape[0]
    items, width = layer_ref.shape
    feats = x_ref.shape[1]
    group = queries // few
    sums = jnp.sum(sums_ref[...].astype(F32), 0)
    d = sums[few : few + 2] + sums[few + 2 : few + 4]
    d = jnp.concatenate([d[0:1], d[1:2]], 1)
    factor = jnp.broadcast_to(scale / d, (8, queries)).T[:, :1]
    emb_q = emb_q_ref[...]
    own_q = jnp.concatenate([emb_q, jnp.zeros_like(emb_q)], 0).astype(BF16)
    load_q.wait()
    scaled = all_q_ref[...].astype(F32) * factor
    high = scaled.astype(BF16)
    low = (scaled - high.astype(F32)).astype(BF16)

    pos_emb = jnp.zeros((16, width), F32)
    for block, chunk in enumerate(blocks_of(items)):
        for copy in loads[block]:
            copy.wait()
        e = jnp.tanh(layer_ref[chunk, :].astype(F32))
        place = lax.broadcasted_iota(jnp.int32, (16, ROWS), 1) + block * ROWS
        line = lax.broadcasted_iota(jnp.int32, (16, ROWS), 0)
        picked = jnp.zeros((16, ROWS), F32)
        for i in range(few):
            picked = jnp.where((line == i) & (place == info_ref[i]), 1.0, picked)
        picked = picked.astype(BF16)
        pos_emb = pos_emb + dot(picked, e.astype(BF16))
        weight = weight_ref[chunk, :]
        item_grad = dot(weight, high) + dot(weight, low) - scale * dot_rows(picked, own_q)
        grad = (item_grad * (1.0 - e * e)).astype(BF16)
        tanh_grad[chunk, :] = grad
        hid_grad = dot_lanes(grad, w_out_ref[...])
        pre_grad[chunk, :] = jnp.where(hid_ref[chunk, :] > 0, hid_grad, 0.0).astype(BF16)

    line = lax.broadcasted_iota(jnp.int32, (8, queries), 0)
    own_lane = lax.broadcasted_iota(jnp.int32, (8, queries), 1)
    own_d = jnp.sum(jnp.where(own_lane == line * group + info_ref[few], d, 0.0), 1, keepdims=True)
    live = lax.broadcasted_iota(jnp.int32, (8, width), 0) < few
    grad = scale * (sums / own_d - pos_emb[:8]) * (1.0 - emb_q * emb_q)
    grad = jnp.where(live, grad, 0.0)
    grad_q = jnp.concatenate([grad, jnp.zeros_like(grad)], 0).astype(BF16)
    hid_q = hid_q_ref[...]
    pre_grad_q = jnp.where(hid_q > 0, dot_lanes(grad_q, w_out_ref[...]), 0.0).astype(BF16)
    in_total = dot_rows(pre_grad[...], x_ref[...]) + dot_rows(pre_grad_q, q_ref[...])
    summed[:feats, :] = in_total.astype(BF16).T
    summed[feats:, :] = (dot_rows(hid_ref[...], tanh_grad[...]) + dot_rows(hid_q, grad_q)).astype(BF16)
    half = mine_ref.shape[0]
    core = info_ref[few + 2]

    @pl.when(core == 0)
    def _():
        mine_ref[...] = summed[:half, :]
        other_ref[...] = summed[half:, :]

    @pl.when(core != 0)
    def _():
        mine_ref[...] = summed[half:, :]
        other_ref[...] = summed[:half, :]


def backward(info, far, near, few, scale):
    items, width = far[2].shape
    units = far[3].shape[1]
    feats = near[2].shape[1]
    return pl.pallas_call(
        functools.partial(backward_kernel, few, scale),
        in_specs=[pl.BlockSpec(memory_space=pltpu.SMEM)] + [FAR] * len(far) + [NEAR] * len(near),
        out_specs=[NEAR] * 2,
        out_shape=[jax.ShapeDtypeStruct(((feats + units) // 2, width), BF16)] * 2,
        scratch_shapes=[
            *[pltpu.VMEM(a.shape, a.dtype) for a in far],
            pltpu.VMEM((items, width), BF16),
            pltpu.VMEM((items, units), BF16),
            pltpu.VMEM((feats + units, width), BF16),
            pltpu.SemaphoreType.DMA((1 + 3 * (items // ROWS),)),
        ],
        compiler_params=pltpu.CompilerParams(vmem_limit_bytes=VMEM),
    )(info, *pinned(*far), *near)


def assemble_kernel(core_ref, mine_ref, other_ref, in_hbm, out_hbm, sems):
    half = mine_ref.shape[0]
    rest = in_hbm.shape[0] - half

    def place(first, second):
        copies = Copies(sems)
        made = [
            copies.start(first, in_hbm.at[pl.ds(0, half), :]),
            copies.start(second.at[pl.ds(0, rest), :], in_hbm.at[pl.ds(half, rest), :]),
            copies.start(second.at[pl.ds(rest, half - rest), :], out_hbm),
        ]
        for copy in made:
            copy.wait()

    @pl.when(core_ref[0] == 0)
    def _():
        place(mine_ref, other_ref)

    @pl.when(core_ref[0] != 0)
    def _():
        place(other_ref, mine_ref)


def assemble(mine, other, feats):
    half, width = mine.shape
    return pl.pallas_call(
        assemble_kernel,
        in_specs=[pl.BlockSpec(memory_space=pltpu.SMEM)] + [NEAR] * 2,
        out_specs=[FAR] * 2,
        out_shape=[
            jax.ShapeDtypeStruct((feats, width), BF16),
            jax.ShapeDtypeStruct((2 * half - feats, width), BF16),
        ],
        scratch_shapes=[pltpu.SemaphoreType.DMA((3,))],
        compiler_params=pltpu.CompilerParams(vmem_limit_bytes=VMEM),
    )(lax.axis_index("c").reshape(1), mine, other)


def request_codes(rows, query_count, item_count, capacity, order, dp_count):
    pairs = rows.shape[0]
    owners = rows // item_count
    code = rows - owners * item_count
    owner_hot = order(owners)[:, None] == jnp.arange(dp_count, dtype=jnp.int32)[None, :]
    earlier = jnp.arange(pairs)[:, None] >= jnp.arange(pairs)[None, :]
    running = dot(earlier.astype(BF16), owner_hot.astype(BF16))
    slot = jnp.sum(jnp.where(owner_hot, running, 0.0), 1).astype(jnp.int32) - 1
    who = jnp.arange(pairs, dtype=jnp.int32) // (pairs // query_count) + 1
    lane = jnp.arange(128, dtype=jnp.int32)[None, :]
    value = jnp.zeros((pairs, 128), jnp.int32)
    for at, part in enumerate((code // 32, code % 32, who)):
        value = jnp.where(slot[:, None] + at * capacity == lane, part[:, None], value)
    return dot_rows(owner_hot.astype(BF16), value.astype(BF16)).astype(BF16)


def local(query_feats, item_feats, w_in, w_out, negatives, positives, owner_map):
    dp_count = lax.axis_size(DP)
    own_index = lax.axis_index(DP)
    z_count = lax.axis_size("z")
    x_count = lax.axis_size("x")
    yc_count = dp_count // z_count
    few = query_feats.shape[0]
    item_count = item_feats.shape[0]
    width = w_out.shape[1]
    negative_count = negatives.shape[1]
    scale = 4.0 / math.sqrt(width)
    capacity = 4 * few * negative_count // dp_count
    queries = few * dp_count

    blocks, hidden, hidden_q = forward(query_feats, item_feats, w_in, w_out)
    arrived = exchange(blocks, "x")

    named = jnp.concatenate([negatives.reshape(-1), positives])
    rows = jnp.take(owner_map, named, axis=0)
    pos_local = rows[few * negative_count :] - own_index * item_count
    places = [lax.axis_index(YCZ), lax.axis_index("x"), lax.axis_index("c")]
    info = jnp.concatenate([pos_local, jnp.stack(places)])
    codes = request_codes(
        rows[: few * negative_count],
        few,
        item_count,
        capacity,
        lambda o: (o % yc_count) * z_count + o // yc_count,
        dp_count,
    )
    codes = jnp.pad(codes[:, None, :], ((0, 0), (0, 1), (0, 0)))

    own = total(arrived[:, :ROWS]).astype(BF16)
    own_q = jnp.tanh(total(arrived[:, ROWS:]))
    sent_q = jnp.broadcast_to(own_q[:few].astype(BF16).reshape(1, 2, -1), (dp_count, 2, few // 2 * width))
    message = exchange(jnp.concatenate([sent_q, codes], 2), YCZ)
    message = message.reshape(2 * dp_count, -1)
    layers = [own]
    for far in range(1, x_count):
        layers.append(lax.ppermute(own, "x", [(i, (i + far) % x_count) for i in range(x_count)]))

    weight, layer_out, all_q, pay = score(info, layers, message, few, capacity, scale, yc_count)
    first = total(exchange(pay, ("y", "c")))
    mine = queries // yc_count
    d_rows = queries // width
    d_part = first[mine : mine + d_rows] + first[mine + d_rows : mine + 2 * d_rows]
    high = d_part.astype(BF16)
    tail = jnp.concatenate([high, (d_part - high.astype(F32)).astype(BF16)], 0)
    sums = exchange(
        jnp.concatenate(
            [
                first[:mine].astype(BF16).reshape(few, z_count, width).transpose(1, 0, 2),
                jnp.broadcast_to(tail[None], (z_count, 2 * d_rows, width)),
            ],
            1,
        ),
        "z",
    )
    feats_q = jnp.pad(query_feats, ((0, 16 - few), (0, 0)))
    near = (sums, w_out, item_feats, own_q, hidden_q, feats_q)
    mine, other = backward(info, (all_q, weight, layer_out, hidden), near, few, scale)
    y_count = lax.axis_size("y")
    swap = [(0, 1), (1, 0)]
    grads = (mine.astype(F32) + lax.ppermute(other, "c", swap).astype(F32)).astype(BF16)
    grads = total(exchange(grads.reshape(y_count, -1, width), "y"))
    grads = total(spread(grads.astype(BF16), "z")).astype(BF16)
    grads = spread(grads, "y").reshape(-1, width)
    return tuple(assemble(grads, lax.ppermute(grads, "c", swap), w_in.shape[0]))


def solution(mesh):
    grid = Mesh(mesh.devices.reshape(8, 8, 2, 4), ("z", "y", "c", "x"))
    return jax.shard_map(
        local,
        mesh=grid,
        in_specs=(
            P(DP, None),
            P(DP, None),
            P(None, "x"),
            P("x", None),
            P(DP, None),
            P(DP),
            P(),
        ),
        out_specs=(P(None, "x"), P("x", None)),
        check_vma=False,
    )
```

```python
import functools
import math

import jax
import jax.numpy as jnp
from jax import lax
from jax.experimental import pallas as pl
from jax.experimental.pallas import tpu as pltpu
from jax.sharding import Mesh, PartitionSpec as P

F32 = jnp.float32
BF16 = jnp.bfloat16
DP = ("z", "y", "c")
YCZ = ("y", "c", "z")
ROWS = 256
VMEM = 20 * 1024 * 1024


def exchange(blocks, axes):
    return lax.all_to_all(blocks, axes, split_axis=0, concat_axis=0, tiled=True)


def spread(block, axes):
    count = lax.axis_size(axes)
    return exchange(jnp.broadcast_to(block[None], (count,) + block.shape), axes)


def total(blocks):
    return jnp.sum(blocks.astype(F32), 0)


def dot(a, b):
    return jnp.dot(a, b, preferred_element_type=F32)


def dot_rows(a, b):
    return lax.dot_general(a, b, (((0,), (0,)), ((), ())), preferred_element_type=F32)


def dot_lanes(a, b):
    return lax.dot_general(a, b, (((1,), (1,)), ((), ())), preferred_element_type=F32)


def blocks_of(items):
    return [pl.ds(i * ROWS, ROWS) for i in range(items // ROWS)]


class Copies:
    def __init__(self, sems):
        self.sems = sems
        self.used = 0

    def start(self, source, target):
        copy = pltpu.make_async_copy(source, target, self.sems.at[self.used])
        copy.start()
        self.used += 1
        return copy


def forward_kernel(
    q_hbm, x_hbm, w_in_hbm, w_out_hbm, part_hbm, hid_hbm, hid_q_hbm,
    q_buf, x_buf, w_in_buf, w_out_buf, part_buf, hid_buf, sems,
):
    few, feats = q_buf.shape
    steps = part_buf.shape[0]
    lead = x_buf.shape[0] - steps * ROWS
    copies = Copies(sems)
    load_in = copies.start(w_in_hbm, w_in_buf)
    load_q = copies.start(q_hbm, q_buf)
    load_x = []
    for i in range(steps):
        source = x_hbm.at[pl.ds(i * ROWS, ROWS), :]
        load_x.append(copies.start(source, x_buf.at[pl.ds(lead + i * ROWS, ROWS), :]))
    load_out = copies.start(w_out_hbm, w_out_buf)
    load_q.wait()
    padded = jnp.concatenate([q_buf[...].astype(F32), jnp.zeros((lead - few, feats), F32)], 0)
    x_buf[:lead, :] = padded.astype(BF16)
    stores = []
    load_in.wait()
    pair = 2
    for i in range(0, steps, pair):
        for load in load_x[i : i + pair]:
            load.wait()
        first = 0 if i == 0 else lead + i * ROWS
        skip = lead if i == 0 else 0
        span = pl.ds(first, skip + pair * ROWS)
        hid = jnp.maximum(dot(x_buf[span, :], w_in_buf[...]), 0.0).astype(BF16)
        hid_buf[span, :] = hid
        if i == 0:
            load_out.wait()
            stores.append(copies.start(hid_buf.at[pl.ds(0, lead), :], hid_q_hbm))
        out = dot(hid, w_out_buf[...])
        if i == 0:
            for j in range(steps):
                part_buf[j, ROWS:, :] = out[:8]
        for j in range(pair):
            part_buf[i + j, :ROWS, :] = out[skip + j * ROWS : skip + (j + 1) * ROWS]
            stores.append(copies.start(part_buf.at[i + j], part_hbm.at[i + j]))
        rows = pl.ds(lead + i * ROWS, pair * ROWS)
        stores.append(copies.start(hid_buf.at[rows, :], hid_hbm.at[pl.ds(i * ROWS, pair * ROWS), :]))
    for store in stores:
        store.wait()


FAR = pl.BlockSpec(memory_space=pltpu.HBM)
NEAR = pl.BlockSpec(memory_space=pltpu.VMEM)


def pinned(*arrays):
    return [pltpu.with_memory_space_constraint(a, pltpu.HBM) for a in arrays]


def forward(query_feats, item_feats, w_in, w_out):
    few = query_feats.shape[0]
    items, feats = item_feats.shape
    units = w_in.shape[1]
    width = w_out.shape[1]
    steps = items // ROWS
    return pl.pallas_call(
        forward_kernel,
        in_specs=[FAR] * 4,
        out_specs=[FAR] * 3,
        out_shape=[
            pltpu.HBM((steps, ROWS + 8, width), F32),
            pltpu.HBM((items, units), BF16),
            pltpu.HBM((16, units), BF16),
        ],
        scratch_shapes=[
            pltpu.VMEM((few, feats), BF16),
            pltpu.VMEM((16 + items, feats), BF16),
            pltpu.VMEM((feats, units), BF16),
            pltpu.VMEM((units, width), BF16),
            pltpu.VMEM((steps, ROWS + 8, width), F32),
            pltpu.VMEM((16 + items, units), BF16),
            pltpu.SemaphoreType.DMA((4 + 3 * steps,)),
        ],
        compiler_params=pltpu.CompilerParams(vmem_limit_bytes=VMEM),
    )(*pinned(query_feats, item_feats, w_in, w_out))


def row_ids(block, shape):
    return (lax.broadcasted_iota(jnp.int32, shape, 0) + block * shape[0]).astype(F32)


def score_kernel(
    few, slots, scale, info_ref, own_ref, by1_ref, by2_ref, by3_ref, msg_ref,
    weight_hbm, layer_hbm, all_q_hbm, pay_hbm, weight_ref, layer_ref, all_q_ref, pay_ref, code, digit, total_u, emb, sems,
):
    copies = Copies(sems)
    lines = msg_ref.shape[0]
    width = layer_ref.shape[1]
    queries = lines * 2
    group = queries // few
    near = (own_ref, by1_ref, by2_ref, by3_ref)
    for far, ref in enumerate(near):
        first = lax.rem(info_ref[few + 1] + len(near) - far, len(near)) * ROWS
        layer_ref[pl.ds(pl.multiple_of(first, ROWS), ROWS), :] = ref[...]

    line = lax.broadcasted_iota(jnp.int32, (lines, lines), 0)
    column = lax.broadcasted_iota(jnp.int32, (lines, lines), 1)
    order = jnp.where(column == (line % group) * 2 + line // group, 1.0, 0.0).astype(BF16)
    turned = dot(order, msg_ref[...])
    parts = []
    for i in range(few):
        first = (i % 2) * width
        parts.append(turned[(i // 2) * group : (i // 2 + 1) * group, first : first + width])
    all_q = jnp.concatenate(parts, 0).astype(BF16)
    all_q_ref[...] = all_q
    stores = [copies.start(layer_ref, layer_hbm), copies.start(all_q_ref, all_q_hbm)]
    asked = turned[:group, 2 * width :].T
    who = asked[2 * slots : 3 * slots]
    code[:slots, :] = jnp.where(who > 0.0, asked[:slots] * 32.0 + asked[slots : 2 * slots], -1.0)
    power = jnp.zeros_like(who)
    for i in range(few):
        power = jnp.where(who == i + 1.0, 32.0**i, power)
    digit[:slots, :] = power
    lane = lax.broadcasted_iota(jnp.int32, (1, group), 1)
    for i in range(few):
        code[slots + i : slots + i + 1, :] = jnp.where(lane == info_ref[few], info_ref[i], -1).astype(F32)
        digit[slots + i : slots + i + 1, :] = jnp.full((1, group), 32.0**i, F32)

    total_d = jnp.zeros((1, queries), F32)
    for block, chunk in enumerate(blocks_of(layer_ref.shape[0])):
        e16 = jnp.tanh(layer_ref[chunk, :].astype(F32)).astype(BF16)
        emb[chunk, :] = e16
        grown = jnp.exp(scale * dot_lanes(e16, all_q))
        ids = row_ids(block, (ROWS, group))
        digits = jnp.zeros((ROWS, group), F32)
        for s in range(slots + few):
            digits = digits + jnp.where(code[s : s + 1, :] == ids, digit[s : s + 1, :], 0.0)
        digits = digits.astype(jnp.int32)
        times = [((digits >> (5 * i)) & 31).astype(F32) for i in range(few)]
        weight = jnp.concatenate(times, 1) * grown
        weight16 = weight.astype(BF16)
        weight_ref[chunk, :] = weight16
        stores.append(copies.start(weight_ref.at[chunk, :], weight_hbm.at[chunk, :]))
        total_d = total_d + jnp.sum(weight, 0, keepdims=True)

    total_u[...] = dot_rows(weight_ref[...], emb[...])
    d = jnp.concatenate([total_d[:, i * width : (i + 1) * width] for i in range(queries // width)], 0)
    high = d.astype(BF16).astype(F32)
    tail = jnp.concatenate([high, d - high, jnp.zeros((8 - 2 * d.shape[0], width), F32)], 0)
    for y in range(pay_ref.shape[0]):
        mine = [total_u[i * group + y * 8 : i * group + y * 8 + 8, :] for i in range(few)]
        pay_ref[y] = jnp.concatenate([*mine, tail], 0).astype(BF16)
    stores.append(copies.start(pay_ref, pay_hbm))
    for store in stores:
        store.wait()


def score(info, layers, message, few, slots, scale, peers):
    share, width = layers[0].shape
    items = share * len(layers)
    queries = 2 * message.shape[0]
    pay = (peers, queries // peers + 8, width)
    return pl.pallas_call(
        functools.partial(score_kernel, few, slots, scale),
        in_specs=[pl.BlockSpec(memory_space=pltpu.SMEM)] + [NEAR] * (len(layers) + 1),
        out_specs=[FAR] * 4,
        out_shape=[
            pltpu.HBM((items, queries), BF16),
            pltpu.HBM((items, width), BF16),
            pltpu.HBM((queries, width), BF16),
            pltpu.HBM(pay, BF16),
        ],
        scratch_shapes=[
            pltpu.VMEM((items, queries), BF16),
            pltpu.VMEM((items, width), BF16),
            pltpu.VMEM((queries, width), BF16),
            pltpu.VMEM(pay, BF16),
            pltpu.VMEM((slots + 8, queries // few), F32),
            pltpu.VMEM((slots + 8, queries // few), F32),
            pltpu.VMEM((queries, width), F32),
            pltpu.VMEM((items, width), BF16),
            pltpu.SemaphoreType.DMA((3 + items // ROWS,)),
        ],
        compiler_params=pltpu.CompilerParams(vmem_limit_bytes=VMEM),
    )(info, *layers, message)


def backward_kernel(
    few, scale, info_ref, all_q_hbm, weight_hbm, layer_hbm, hid_hbm, sums_ref, w_out_ref, x_ref,
    emb_q_ref, hid_q_ref, q_ref, mine_ref, other_ref,
    all_q_ref, weight_ref, layer_ref, hid_ref, item_grad, tanh_grad, pre_grad, summed, sems,
):
    items, width = layer_ref.shape
    feats = x_ref.shape[1]
    halves = [pl.ds(i * 2 * ROWS, 2 * ROWS) for i in range(items // (2 * ROWS))]
    copies = Copies(sems)
    load_q = copies.start(all_q_hbm, all_q_ref)
    load_weight = [copies.start(weight_hbm.at[half, :], weight_ref.at[half, :]) for half in halves]
    load_layer = copies.start(layer_hbm, layer_ref)
    load_hid = copies.start(hid_hbm, hid_ref)

    queries = all_q_ref.shape[0]
    group = queries // few
    sums = jnp.sum(sums_ref[...].astype(F32), 0)
    d = sums[few : few + 2] + sums[few + 2 : few + 4]
    d = jnp.concatenate([d[0:1], d[1:2]], 1)
    factor = jnp.broadcast_to(scale / d, (8, queries)).T[:, :1]
    line = lax.broadcasted_iota(jnp.int32, (8, queries), 0)
    own_lane = lax.broadcasted_iota(jnp.int32, (8, queries), 1)
    own_d = jnp.sum(jnp.where(own_lane == line * group + info_ref[few], d, 0.0), 1, keepdims=True)
    emb_q = emb_q_ref[...]
    own_q = emb_q.astype(BF16).astype(F32)
    load_q.wait()
    scaled = (all_q_ref[...].astype(F32) * factor).astype(BF16)
    for half, load in zip(halves, load_weight):
        load.wait()
        item_grad[half, :] = dot(weight_ref[half, :], scaled)
    load_layer.wait()
    named = []
    for i in range(few):
        place = info_ref[i]
        item_grad[pl.ds(place, 1), :] = item_grad[pl.ds(place, 1), :] - scale * own_q[i : i + 1]
        base = (place // 16) * 16
        near = layer_ref[pl.ds(pl.multiple_of(base, 16), 16), :].astype(F32)
        at = lax.broadcasted_iota(jnp.int32, near.shape, 0) == place - base
        named.append(jnp.sum(jnp.where(at, near, 0.0), 0, keepdims=True))
    named.append(jnp.zeros((8 - few, width), F32))
    pos_emb = jnp.tanh(jnp.concatenate(named, 0)).astype(BF16).astype(F32)

    load_hid.wait()
    for chunk in halves:
        e = jnp.tanh(layer_ref[chunk, :].astype(F32))
        grad = (item_grad[chunk, :] * (1.0 - e * e)).astype(BF16)
        tanh_grad[chunk, :] = grad
        hid_grad = dot_lanes(grad, w_out_ref[...])
        pre_grad[chunk, :] = jnp.where(hid_ref[chunk, :] > 0, hid_grad, 0.0).astype(BF16)

    live = lax.broadcasted_iota(jnp.int32, (8, width), 0) < few
    grad = scale * (sums / own_d - pos_emb) * (1.0 - emb_q * emb_q)
    grad = jnp.where(live, grad, 0.0)
    grad_q = jnp.concatenate([grad, jnp.zeros_like(grad)], 0).astype(BF16)
    hid_q = hid_q_ref[...]
    pre_grad_q = jnp.where(hid_q > 0, dot_lanes(grad_q, w_out_ref[...]), 0.0).astype(BF16)
    in_total = dot_rows(pre_grad[...], x_ref[...]) + dot_rows(pre_grad_q, q_ref[...])
    summed[:feats, :] = in_total.astype(BF16).T
    summed[feats:, :] = (dot_rows(hid_ref[...], tanh_grad[...]) + dot_rows(hid_q, grad_q)).astype(BF16)
    half = mine_ref.shape[0]
    core = info_ref[few + 2]

    @pl.when(core == 0)
    def _():
        mine_ref[...] = summed[:half, :]
        other_ref[...] = summed[half:, :]

    @pl.when(core != 0)
    def _():
        mine_ref[...] = summed[half:, :]
        other_ref[...] = summed[:half, :]


def backward(info, far, near, few, scale):
    items, width = far[2].shape
    units = far[3].shape[1]
    feats = near[2].shape[1]
    return pl.pallas_call(
        functools.partial(backward_kernel, few, scale),
        in_specs=[pl.BlockSpec(memory_space=pltpu.SMEM)] + [FAR] * len(far) + [NEAR] * len(near),
        out_specs=[NEAR] * 2,
        out_shape=[jax.ShapeDtypeStruct(((feats + units) // 2, width), BF16)] * 2,
        scratch_shapes=[
            *[pltpu.VMEM(a.shape, a.dtype) for a in far],
            pltpu.VMEM((items, width), F32),
            pltpu.VMEM((items, width), BF16),
            pltpu.VMEM((items, units), BF16),
            pltpu.VMEM((feats + units, width), BF16),
            pltpu.SemaphoreType.DMA((3 + items // (2 * ROWS),)),
        ],
        compiler_params=pltpu.CompilerParams(vmem_limit_bytes=VMEM),
    )(info, *pinned(*far), *near)


def assemble_kernel(core_ref, mine_ref, other_ref, in_hbm, out_hbm, sems):
    half = mine_ref.shape[0]
    rest = in_hbm.shape[0] - half

    def place(first, second):
        copies = Copies(sems)
        made = [
            copies.start(first, in_hbm.at[pl.ds(0, half), :]),
            copies.start(second.at[pl.ds(0, rest), :], in_hbm.at[pl.ds(half, rest), :]),
            copies.start(second.at[pl.ds(rest, half - rest), :], out_hbm),
        ]
        for copy in made:
            copy.wait()

    @pl.when(core_ref[0] == 0)
    def _():
        place(mine_ref, other_ref)

    @pl.when(core_ref[0] != 0)
    def _():
        place(other_ref, mine_ref)


def assemble(mine, other, feats):
    half, width = mine.shape
    return pl.pallas_call(
        assemble_kernel,
        in_specs=[pl.BlockSpec(memory_space=pltpu.SMEM)] + [NEAR] * 2,
        out_specs=[FAR] * 2,
        out_shape=[
            jax.ShapeDtypeStruct((feats, width), BF16),
            jax.ShapeDtypeStruct((2 * half - feats, width), BF16),
        ],
        scratch_shapes=[pltpu.SemaphoreType.DMA((3,))],
        compiler_params=pltpu.CompilerParams(vmem_limit_bytes=VMEM),
    )(lax.axis_index("c").reshape(1), mine, other)


def request_codes(rows, query_count, item_count, capacity, order, dp_count):
    pairs = rows.shape[0]
    owners = rows // item_count
    code = rows - owners * item_count
    owner_hot = order(owners)[:, None] == jnp.arange(dp_count, dtype=jnp.int32)[None, :]
    earlier = jnp.arange(pairs)[:, None] >= jnp.arange(pairs)[None, :]
    running = dot(earlier.astype(BF16), owner_hot.astype(BF16))
    slot = jnp.sum(jnp.where(owner_hot, running, 0.0), 1).astype(jnp.int32) - 1
    who = jnp.arange(pairs, dtype=jnp.int32) // (pairs // query_count) + 1
    lane = jnp.arange(128, dtype=jnp.int32)[None, :]
    value = jnp.zeros((pairs, 128), jnp.int32)
    for at, part in enumerate((code // 32, code % 32, who)):
        value = jnp.where(slot[:, None] + at * capacity == lane, part[:, None], value)
    return dot_rows(owner_hot.astype(BF16), value.astype(BF16)).astype(BF16)


def local(query_feats, item_feats, w_in, w_out, negatives, positives, owner_map):
    dp_count = lax.axis_size(DP)
    own_index = lax.axis_index(DP)
    z_count = lax.axis_size("z")
    x_count = lax.axis_size("x")
    yc_count = dp_count // z_count
    few = query_feats.shape[0]
    item_count = item_feats.shape[0]
    width = w_out.shape[1]
    negative_count = negatives.shape[1]
    scale = 4.0 / math.sqrt(width)
    capacity = 4 * few * negative_count // dp_count
    queries = few * dp_count

    blocks, hidden, hidden_q = forward(query_feats, item_feats, w_in, w_out)
    arrived = exchange(blocks, "x")

    named = jnp.concatenate([negatives.reshape(-1), positives])
    rows = jnp.take(owner_map, named, axis=0)
    pos_local = jnp.clip(rows[few * negative_count :] - own_index * item_count, 0, item_count - 1)
    places = [lax.axis_index(YCZ), lax.axis_index("x"), lax.axis_index("c")]
    info = jnp.concatenate([pos_local, jnp.stack(places)])
    codes = request_codes(
        rows[: few * negative_count],
        few,
        item_count,
        capacity,
        lambda o: (o % yc_count) * z_count + o // yc_count,
        dp_count,
    )
    codes = jnp.pad(codes[:, None, :], ((0, 0), (0, 1), (0, 0)))

    own = total(arrived[:, :ROWS]).astype(BF16)
    own_q = jnp.tanh(total(arrived[:, ROWS:]))
    sent_q = jnp.broadcast_to(own_q[:few].astype(BF16).reshape(1, 2, -1), (dp_count, 2, few // 2 * width))
    message = exchange(jnp.concatenate([sent_q, codes], 2), YCZ)
    message = message.reshape(2 * dp_count, -1)
    layers = [own]
    for far in range(1, x_count):
        layers.append(lax.ppermute(own, "x", [(i, (i + far) % x_count) for i in range(x_count)]))

    weight, layer_out, all_q, pay = score(info, layers, message, few, capacity, scale, yc_count)
    first = total(exchange(pay, ("y", "c")))
    mine = queries // yc_count
    d_rows = queries // width
    d_part = first[mine : mine + d_rows] + first[mine + d_rows : mine + 2 * d_rows]
    high = d_part.astype(BF16)
    tail = jnp.concatenate([high, (d_part - high.astype(F32)).astype(BF16)], 0)
    sums = exchange(
        jnp.concatenate(
            [
                first[:mine].astype(BF16).reshape(few, z_count, width).transpose(1, 0, 2),
                jnp.broadcast_to(tail[None], (z_count, 2 * d_rows, width)),
            ],
            1,
        ),
        "z",
    )
    feats_q = jnp.pad(query_feats, ((0, 16 - few), (0, 0)))
    near = (sums, w_out, item_feats, own_q, hidden_q, feats_q)
    mine, other = backward(info, (all_q, weight, layer_out, hidden), near, few, scale)
    y_count = lax.axis_size("y")
    swap = [(0, 1), (1, 0)]
    grads = (mine.astype(F32) + lax.ppermute(other, "c", swap).astype(F32)).astype(BF16)
    grads = total(exchange(grads.reshape(y_count, -1, width), "y"))
    grads = total(spread(grads.astype(BF16), "z")).astype(BF16)
    grads = spread(grads, "y").reshape(-1, width)
    return tuple(assemble(grads, lax.ppermute(grads, "c", swap), w_in.shape[0]))


def solution(mesh):
    grid = Mesh(mesh.devices.reshape(8, 8, 2, 4), ("z", "y", "c", "x"))
    return jax.shard_map(
        local,
        mesh=grid,
        in_specs=(
            P(DP, None),
            P(DP, None),
            P(None, "x"),
            P("x", None),
            P(DP, None),
            P(DP),
            P(),
        ),
        out_specs=(P(None, "x"), P("x", None)),
        check_vma=False,
    )
```

```python
import functools
import math

import jax
import jax.numpy as jnp
from jax import lax
from jax.experimental import pallas as pl
from jax.experimental.pallas import tpu as pltpu
from jax.sharding import Mesh, PartitionSpec as P

F32 = jnp.float32
BF16 = jnp.bfloat16
DP = ("z", "y", "c")
YCZ = ("y", "c", "z")
ROWS = 256
VMEM = 20 * 1024 * 1024


def exchange(blocks, axes):
    return lax.all_to_all(blocks, axes, split_axis=0, concat_axis=0, tiled=True)


def spread(block, axes):
    count = lax.axis_size(axes)
    return exchange(jnp.broadcast_to(block[None], (count,) + block.shape), axes)


def total(blocks):
    return jnp.sum(blocks.astype(F32), 0)


def dot(a, b):
    return jnp.dot(a, b, preferred_element_type=F32)


def dot_rows(a, b):
    return lax.dot_general(a, b, (((0,), (0,)), ((), ())), preferred_element_type=F32)


def dot_lanes(a, b):
    return lax.dot_general(a, b, (((1,), (1,)), ((), ())), preferred_element_type=F32)


def blocks_of(items):
    return [pl.ds(i * ROWS, ROWS) for i in range(items // ROWS)]


class Copies:
    def __init__(self, sems):
        self.sems = sems
        self.used = 0

    def start(self, source, target):
        copy = pltpu.make_async_copy(source, target, self.sems.at[self.used])
        copy.start()
        self.used += 1
        return copy


def forward_kernel(
    q_hbm, x_hbm, w_in_hbm, w_out_hbm, part_hbm, hid_hbm, hid_q_hbm,
    q_buf, x_buf, w_in_buf, w_out_buf, part_buf, hid_buf, sems,
):
    few, feats = q_buf.shape
    steps = part_buf.shape[0]
    lead = x_buf.shape[0] - steps * ROWS
    copies = Copies(sems)
    load_in = copies.start(w_in_hbm, w_in_buf)
    load_q = copies.start(q_hbm, q_buf)
    load_x = []
    for i in range(steps):
        source = x_hbm.at[pl.ds(i * ROWS, ROWS), :]
        load_x.append(copies.start(source, x_buf.at[pl.ds(lead + i * ROWS, ROWS), :]))
    load_out = copies.start(w_out_hbm, w_out_buf)
    load_q.wait()
    padded = jnp.concatenate([q_buf[...].astype(F32), jnp.zeros((lead - few, feats), F32)], 0)
    x_buf[:lead, :] = padded.astype(BF16)
    stores = []
    load_in.wait()
    pair = 2
    for i in range(0, steps, pair):
        for load in load_x[i : i + pair]:
            load.wait()
        first = 0 if i == 0 else lead + i * ROWS
        skip = lead if i == 0 else 0
        span = pl.ds(first, skip + pair * ROWS)
        hid = jnp.maximum(dot(x_buf[span, :], w_in_buf[...]), 0.0).astype(BF16)
        hid_buf[span, :] = hid
        if i == 0:
            load_out.wait()
            stores.append(copies.start(hid_buf.at[pl.ds(0, lead), :], hid_q_hbm))
        out = dot(hid, w_out_buf[...])
        if i == 0:
            for j in range(steps):
                part_buf[j, ROWS:, :] = out[:8]
        for j in range(pair):
            part_buf[i + j, :ROWS, :] = out[skip + j * ROWS : skip + (j + 1) * ROWS]
            stores.append(copies.start(part_buf.at[i + j], part_hbm.at[i + j]))
        rows = pl.ds(lead + i * ROWS, pair * ROWS)
        stores.append(copies.start(hid_buf.at[rows, :], hid_hbm.at[pl.ds(i * ROWS, pair * ROWS), :]))
    for store in stores:
        store.wait()


FAR = pl.BlockSpec(memory_space=pltpu.HBM)
NEAR = pl.BlockSpec(memory_space=pltpu.VMEM)


def pinned(*arrays):
    return [pltpu.with_memory_space_constraint(a, pltpu.HBM) for a in arrays]


def forward(query_feats, item_feats, w_in, w_out):
    few = query_feats.shape[0]
    items, feats = item_feats.shape
    units = w_in.shape[1]
    width = w_out.shape[1]
    steps = items // ROWS
    return pl.pallas_call(
        forward_kernel,
        in_specs=[FAR] * 4,
        out_specs=[FAR] * 3,
        out_shape=[
            pltpu.HBM((steps, ROWS + 8, width), F32),
            pltpu.HBM((items, units), BF16),
            pltpu.HBM((16, units), BF16),
        ],
        scratch_shapes=[
            pltpu.VMEM((few, feats), BF16),
            pltpu.VMEM((16 + items, feats), BF16),
            pltpu.VMEM((feats, units), BF16),
            pltpu.VMEM((units, width), BF16),
            pltpu.VMEM((steps, ROWS + 8, width), F32),
            pltpu.VMEM((16 + items, units), BF16),
            pltpu.SemaphoreType.DMA((4 + 3 * steps,)),
        ],
        compiler_params=pltpu.CompilerParams(vmem_limit_bytes=VMEM),
    )(*pinned(query_feats, item_feats, w_in, w_out))


def row_ids(block, shape):
    return (lax.broadcasted_iota(jnp.int32, shape, 0) + block * shape[0]).astype(F32)


def score_kernel(
    few, slots, scale, info_ref, own_ref, by1_ref, by2_ref, by3_ref, msg_ref,
    weight_hbm, layer_hbm, all_q_hbm, pay_ref, weight_ref, layer_ref, all_q_ref, code, digit, total_u, emb, sems,
):
    copies = Copies(sems)
    lines = msg_ref.shape[0]
    width = layer_ref.shape[1]
    queries = lines * 2
    group = queries // few
    near = (own_ref, by1_ref, by2_ref, by3_ref)
    for far, ref in enumerate(near):
        first = lax.rem(info_ref[few + 1] + len(near) - far, len(near)) * ROWS
        layer_ref[pl.ds(pl.multiple_of(first, ROWS), ROWS), :] = ref[...]

    line = lax.broadcasted_iota(jnp.int32, (lines, lines), 0)
    column = lax.broadcasted_iota(jnp.int32, (lines, lines), 1)
    order = jnp.where(column == (line % group) * 2 + line // group, 1.0, 0.0).astype(BF16)
    turned = dot(order, msg_ref[...])
    parts = []
    for i in range(few):
        first = (i % 2) * width
        parts.append(turned[(i // 2) * group : (i // 2 + 1) * group, first : first + width])
    all_q = jnp.concatenate(parts, 0).astype(BF16)
    all_q_ref[...] = all_q
    stores = [copies.start(layer_ref, layer_hbm), copies.start(all_q_ref, all_q_hbm)]
    asked = turned[:group, 2 * width :].T
    who = asked[2 * slots : 3 * slots]
    code[:slots, :] = jnp.where(who > 0.0, asked[:slots] * 32.0 + asked[slots : 2 * slots], -1.0)
    power = jnp.zeros_like(who)
    for i in range(few):
        power = jnp.where(who == i + 1.0, 32.0**i, power)
    digit[:slots, :] = power
    lane = lax.broadcasted_iota(jnp.int32, (1, group), 1)
    for i in range(few):
        code[slots + i : slots + i + 1, :] = jnp.where(lane == info_ref[few], info_ref[i], -1).astype(F32)
        digit[slots + i : slots + i + 1, :] = jnp.full((1, group), 32.0**i, F32)

    total_d = jnp.zeros((1, queries), F32)
    for block, chunk in enumerate(blocks_of(layer_ref.shape[0])):
        e16 = jnp.tanh(layer_ref[chunk, :].astype(F32)).astype(BF16)
        emb[chunk, :] = e16
        grown = jnp.exp(scale * dot_lanes(e16, all_q))
        ids = row_ids(block, (ROWS, group))
        digits = jnp.zeros((ROWS, group), F32)
        for s in range(slots + few):
            digits = digits + jnp.where(code[s : s + 1, :] == ids, digit[s : s + 1, :], 0.0)
        digits = digits.astype(jnp.int32)
        times = [((digits >> (5 * i)) & 31).astype(F32) for i in range(few)]
        weight = jnp.concatenate(times, 1) * grown
        weight16 = weight.astype(BF16)
        weight_ref[chunk, :] = weight16
        stores.append(copies.start(weight_ref.at[chunk, :], weight_hbm.at[chunk, :]))
        total_d = total_d + jnp.sum(weight, 0, keepdims=True)

    total_u[...] = dot_rows(weight_ref[...], emb[...])
    d = jnp.concatenate([total_d[:, i * width : (i + 1) * width] for i in range(queries // width)], 0)
    high = d.astype(BF16).astype(F32)
    tail = jnp.concatenate([high, d - high, jnp.zeros((8 - 2 * d.shape[0], width), F32)], 0)
    for y in range(pay_ref.shape[0]):
        mine = [total_u[i * group + y * 8 : i * group + y * 8 + 8, :] for i in range(few)]
        pay_ref[y] = jnp.concatenate([*mine, tail], 0).astype(BF16)
    for store in stores:
        store.wait()


def score(info, layers, message, few, slots, scale, peers):
    share, width = layers[0].shape
    items = share * len(layers)
    queries = 2 * message.shape[0]
    pay = (peers, queries // peers + 8, width)
    return pl.pallas_call(
        functools.partial(score_kernel, few, slots, scale),
        in_specs=[pl.BlockSpec(memory_space=pltpu.SMEM)] + [NEAR] * (len(layers) + 1),
        out_specs=[FAR] * 3 + [NEAR],
        out_shape=[
            pltpu.HBM((items, queries), BF16),
            pltpu.HBM((items, width), BF16),
            pltpu.HBM((queries, width), BF16),
            jax.ShapeDtypeStruct(pay, BF16),
        ],
        scratch_shapes=[
            pltpu.VMEM((items, queries), BF16),
            pltpu.VMEM((items, width), BF16),
            pltpu.VMEM((queries, width), BF16),
            pltpu.VMEM((slots + 8, queries // few), F32),
            pltpu.VMEM((slots + 8, queries // few), F32),
            pltpu.VMEM((queries, width), F32),
            pltpu.VMEM((items, width), BF16),
            pltpu.SemaphoreType.DMA((3 + items // ROWS,)),
        ],
        compiler_params=pltpu.CompilerParams(vmem_limit_bytes=VMEM),
    )(info, *layers, message)


def backward_kernel(
    few, scale, info_ref, all_q_hbm, weight_hbm, layer_hbm, hid_hbm, x_hbm, sums_ref, w_out_ref,
    emb_q_ref, hid_q_ref, q_ref, mine_ref, other_ref,
    all_q_ref, weight_ref, layer_ref, hid_ref, x_ref, item_grad, tanh_grad, pre_grad, summed, sems,
):
    items, width = layer_ref.shape
    feats = x_ref.shape[1]
    halves = [pl.ds(i * 2 * ROWS, 2 * ROWS) for i in range(items // (2 * ROWS))]
    copies = Copies(sems)
    load_q = copies.start(all_q_hbm, all_q_ref)
    load_weight = [copies.start(weight_hbm.at[half, :], weight_ref.at[half, :]) for half in halves]
    load_layer = copies.start(layer_hbm, layer_ref)
    load_hid = copies.start(hid_hbm, hid_ref)
    load_x = copies.start(x_hbm, x_ref)

    queries = all_q_ref.shape[0]
    group = queries // few
    sums = jnp.sum(sums_ref[...].astype(F32), 0)
    d = sums[few : few + 2] + sums[few + 2 : few + 4]
    d = jnp.concatenate([d[0:1], d[1:2]], 1)
    factor = jnp.broadcast_to(scale / d, (8, queries)).T[:, :1]
    line = lax.broadcasted_iota(jnp.int32, (8, queries), 0)
    own_lane = lax.broadcasted_iota(jnp.int32, (8, queries), 1)
    own_d = jnp.sum(jnp.where(own_lane == line * group + info_ref[few], d, 0.0), 1, keepdims=True)
    emb_q = emb_q_ref[...]
    own_q = emb_q.astype(BF16).astype(F32)
    load_q.wait()
    scaled = (all_q_ref[...].astype(F32) * factor).astype(BF16)
    for half, load in zip(halves, load_weight):
        load.wait()
        item_grad[half, :] = dot(weight_ref[half, :], scaled)
    load_layer.wait()
    named = []
    for i in range(few):
        place = info_ref[i]
        item_grad[pl.ds(place, 1), :] = item_grad[pl.ds(place, 1), :] - scale * own_q[i : i + 1]
        base = (place // 16) * 16
        near = layer_ref[pl.ds(pl.multiple_of(base, 16), 16), :].astype(F32)
        at = lax.broadcasted_iota(jnp.int32, near.shape, 0) == place - base
        named.append(jnp.sum(jnp.where(at, near, 0.0), 0, keepdims=True))
    named.append(jnp.zeros((8 - few, width), F32))
    pos_emb = jnp.tanh(jnp.concatenate(named, 0)).astype(BF16).astype(F32)

    load_hid.wait()
    for chunk in halves:
        e = jnp.tanh(layer_ref[chunk, :].astype(F32))
        grad = (item_grad[chunk, :] * (1.0 - e * e)).astype(BF16)
        tanh_grad[chunk, :] = grad
        hid_grad = dot_lanes(grad, w_out_ref[...])
        pre_grad[chunk, :] = jnp.where(hid_ref[chunk, :] > 0, hid_grad, 0.0).astype(BF16)

    live = lax.broadcasted_iota(jnp.int32, (8, width), 0) < few
    grad = scale * (sums / own_d - pos_emb) * (1.0 - emb_q * emb_q)
    grad = jnp.where(live, grad, 0.0)
    grad_q = jnp.concatenate([grad, jnp.zeros_like(grad)], 0).astype(BF16)
    hid_q = hid_q_ref[...]
    pre_grad_q = jnp.where(hid_q > 0, dot_lanes(grad_q, w_out_ref[...]), 0.0).astype(BF16)
    load_x.wait()
    in_total = dot_rows(pre_grad[...], x_ref[...]) + dot_rows(pre_grad_q, q_ref[...])
    summed[:feats, :] = in_total.astype(BF16).T
    summed[feats:, :] = (dot_rows(hid_ref[...], tanh_grad[...]) + dot_rows(hid_q, grad_q)).astype(BF16)
    half = mine_ref.shape[0]
    core = info_ref[few + 2]

    @pl.when(core == 0)
    def _():
        mine_ref[...] = summed[:half, :]
        other_ref[...] = summed[half:, :]

    @pl.when(core != 0)
    def _():
        mine_ref[...] = summed[half:, :]
        other_ref[...] = summed[:half, :]


def backward(info, far, near, few, scale):
    items, width = far[2].shape
    units = far[3].shape[1]
    feats = far[4].shape[1]
    return pl.pallas_call(
        functools.partial(backward_kernel, few, scale),
        in_specs=[pl.BlockSpec(memory_space=pltpu.SMEM)] + [FAR] * len(far) + [NEAR] * len(near),
        out_specs=[NEAR] * 2,
        out_shape=[jax.ShapeDtypeStruct(((feats + units) // 2, width), BF16)] * 2,
        scratch_shapes=[
            *[pltpu.VMEM(a.shape, a.dtype) for a in far],
            pltpu.VMEM((items, width), F32),
            pltpu.VMEM((items, width), BF16),
            pltpu.VMEM((items, units), BF16),
            pltpu.VMEM((feats + units, width), BF16),
            pltpu.SemaphoreType.DMA((4 + items // (2 * ROWS),)),
        ],
        compiler_params=pltpu.CompilerParams(vmem_limit_bytes=VMEM),
    )(info, *pinned(*far), *near)


def assemble_kernel(core_ref, mine_ref, other_ref, in_hbm, out_hbm, sems):
    half = mine_ref.shape[0]
    rest = in_hbm.shape[0] - half

    def place(first, second):
        copies = Copies(sems)
        made = [
            copies.start(first, in_hbm.at[pl.ds(0, half), :]),
            copies.start(second.at[pl.ds(0, rest), :], in_hbm.at[pl.ds(half, rest), :]),
            copies.start(second.at[pl.ds(rest, half - rest), :], out_hbm),
        ]
        for copy in made:
            copy.wait()

    @pl.when(core_ref[0] == 0)
    def _():
        place(mine_ref, other_ref)

    @pl.when(core_ref[0] != 0)
    def _():
        place(other_ref, mine_ref)


def assemble(mine, other, feats):
    half, width = mine.shape
    return pl.pallas_call(
        assemble_kernel,
        in_specs=[pl.BlockSpec(memory_space=pltpu.SMEM)] + [NEAR] * 2,
        out_specs=[FAR] * 2,
        out_shape=[
            jax.ShapeDtypeStruct((feats, width), BF16),
            jax.ShapeDtypeStruct((2 * half - feats, width), BF16),
        ],
        scratch_shapes=[pltpu.SemaphoreType.DMA((3,))],
        compiler_params=pltpu.CompilerParams(vmem_limit_bytes=VMEM),
    )(lax.axis_index("c").reshape(1), mine, other)


def request_codes(rows, query_count, item_count, capacity, order, dp_count):
    pairs = rows.shape[0]
    owners = rows // item_count
    code = rows - owners * item_count
    owner_hot = order(owners)[:, None] == jnp.arange(dp_count, dtype=jnp.int32)[None, :]
    earlier = jnp.arange(pairs)[:, None] >= jnp.arange(pairs)[None, :]
    running = dot(earlier.astype(BF16), owner_hot.astype(BF16))
    slot = jnp.sum(jnp.where(owner_hot, running, 0.0), 1).astype(jnp.int32) - 1
    who = jnp.arange(pairs, dtype=jnp.int32) // (pairs // query_count) + 1
    lane = jnp.arange(128, dtype=jnp.int32)[None, :]
    value = jnp.zeros((pairs, 128), jnp.int32)
    for at, part in enumerate((code // 32, code % 32, who)):
        value = jnp.where(slot[:, None] + at * capacity == lane, part[:, None], value)
    return dot_rows(owner_hot.astype(BF16), value.astype(BF16)).astype(BF16)


def local(query_feats, item_feats, w_in, w_out, negatives, positives, owner_map):
    dp_count = lax.axis_size(DP)
    own_index = lax.axis_index(DP)
    z_count = lax.axis_size("z")
    x_count = lax.axis_size("x")
    yc_count = dp_count // z_count
    few = query_feats.shape[0]
    item_count = item_feats.shape[0]
    width = w_out.shape[1]
    negative_count = negatives.shape[1]
    scale = 4.0 / math.sqrt(width)
    capacity = 4 * few * negative_count // dp_count
    queries = few * dp_count

    blocks, hidden, hidden_q = forward(query_feats, item_feats, w_in, w_out)
    arrived = exchange(blocks, "x")

    named = jnp.concatenate([negatives.reshape(-1), positives])
    rows = jnp.take(owner_map, named, axis=0)
    pos_local = jnp.clip(rows[few * negative_count :] - own_index * item_count, 0, item_count - 1)
    places = [lax.axis_index(YCZ), lax.axis_index("x"), lax.axis_index("c")]
    info = jnp.concatenate([pos_local, jnp.stack(places)])
    codes = request_codes(
        rows[: few * negative_count],
        few,
        item_count,
        capacity,
        lambda o: (o % yc_count) * z_count + o // yc_count,
        dp_count,
    )
    codes = jnp.pad(codes[:, None, :], ((0, 0), (0, 1), (0, 0)))

    own = total(arrived[:, :ROWS]).astype(BF16)
    own_q = jnp.tanh(total(arrived[:, ROWS:]))
    sent_q = jnp.broadcast_to(own_q[:few].astype(BF16).reshape(1, 2, -1), (dp_count, 2, few // 2 * width))
    message = exchange(jnp.concatenate([sent_q, codes], 2), YCZ)
    message = message.reshape(2 * dp_count, -1)
    layers = [own]
    for far in range(1, x_count):
        layers.append(lax.ppermute(own, "x", [(i, (i + far) % x_count) for i in range(x_count)]))

    weight, layer_out, all_q, pay = score(info, layers, message, few, capacity, scale, yc_count)
    first = total(exchange(pay, ("y", "c")))
    mine = queries // yc_count
    d_rows = queries // width
    d_part = first[mine : mine + d_rows] + first[mine + d_rows : mine + 2 * d_rows]
    high = d_part.astype(BF16)
    tail = jnp.concatenate([high, (d_part - high.astype(F32)).astype(BF16)], 0)
    sums = exchange(
        jnp.concatenate(
            [
                first[:mine].astype(BF16).reshape(few, z_count, width).transpose(1, 0, 2),
                jnp.broadcast_to(tail[None], (z_count, 2 * d_rows, width)),
            ],
            1,
        ),
        "z",
    )
    feats_q = jnp.pad(query_feats, ((0, 16 - few), (0, 0)))
    near = (sums, w_out, own_q, hidden_q, feats_q)
    mine, other = backward(info, (all_q, weight, layer_out, hidden, item_feats), near, few, scale)
    y_count = lax.axis_size("y")
    swap = [(0, 1), (1, 0)]
    grads = (mine.astype(F32) + lax.ppermute(other, "c", swap).astype(F32)).astype(BF16)
    grads = total(exchange(grads.reshape(y_count, -1, width), "y"))
    grads = total(spread(grads.astype(BF16), "z")).astype(BF16)
    grads = spread(grads, "y").reshape(-1, width)
    return tuple(assemble(grads, lax.ppermute(grads, "c", swap), w_in.shape[0]))


def solution(mesh):
    grid = Mesh(mesh.devices.reshape(8, 8, 2, 4), ("z", "y", "c", "x"))
    return jax.shard_map(
        local,
        mesh=grid,
        in_specs=(
            P(DP, None),
            P(DP, None),
            P(None, "x"),
            P("x", None),
            P(DP, None),
            P(DP),
            P(),
        ),
        out_specs=(P(None, "x"), P("x", None)),
        check_vma=False,
    )
```

```python
import functools
import math

import jax
import jax.numpy as jnp
from jax import lax
from jax.experimental import pallas as pl
from jax.experimental.pallas import tpu as pltpu
from jax.sharding import Mesh, PartitionSpec as P

F32 = jnp.float32
BF16 = jnp.bfloat16
DP = ("z", "y", "c")
YCZ = ("y", "c", "z")
ROWS = 256
VMEM = 20 * 1024 * 1024


def exchange(blocks, axes):
    return lax.all_to_all(blocks, axes, split_axis=0, concat_axis=0, tiled=True)


def spread(block, axes):
    count = lax.axis_size(axes)
    return exchange(jnp.broadcast_to(block[None], (count,) + block.shape), axes)


def total(blocks):
    return jnp.sum(blocks.astype(F32), 0)


def dot(a, b):
    return jnp.dot(a, b, preferred_element_type=F32)


def dot_rows(a, b):
    return lax.dot_general(a, b, (((0,), (0,)), ((), ())), preferred_element_type=F32)


def dot_lanes(a, b):
    return lax.dot_general(a, b, (((1,), (1,)), ((), ())), preferred_element_type=F32)


def blocks_of(items):
    return [pl.ds(i * ROWS, ROWS) for i in range(items // ROWS)]


class Copies:
    def __init__(self, sems):
        self.sems = sems
        self.used = 0

    def start(self, source, target):
        copy = pltpu.make_async_copy(source, target, self.sems.at[self.used])
        copy.start()
        self.used += 1
        return copy


def forward_kernel(
    q_hbm, x_hbm, w_in_hbm, w_out_hbm, part_hbm, hid_hbm, hid_q_hbm,
    q_buf, x_buf, w_in_buf, w_out_buf, part_buf, hid_buf, sems,
):
    few, feats = q_buf.shape
    steps = part_buf.shape[0]
    lead = x_buf.shape[0] - steps * ROWS
    copies = Copies(sems)
    load_in = copies.start(w_in_hbm, w_in_buf)
    load_q = copies.start(q_hbm, q_buf)
    load_x = []
    for i in range(steps):
        source = x_hbm.at[pl.ds(i * ROWS, ROWS), :]
        load_x.append(copies.start(source, x_buf.at[pl.ds(lead + i * ROWS, ROWS), :]))
    load_out = copies.start(w_out_hbm, w_out_buf)
    load_q.wait()
    padded = jnp.concatenate([q_buf[...].astype(F32), jnp.zeros((lead - few, feats), F32)], 0)
    x_buf[:lead, :] = padded.astype(BF16)
    stores = []
    load_in.wait()
    pair = 2
    for i in range(0, steps, pair):
        for load in load_x[i : i + pair]:
            load.wait()
        first = 0 if i == 0 else lead + i * ROWS
        skip = lead if i == 0 else 0
        span = pl.ds(first, skip + pair * ROWS)
        hid = jnp.maximum(dot(x_buf[span, :], w_in_buf[...]), 0.0).astype(BF16)
        hid_buf[span, :] = hid
        if i == 0:
            load_out.wait()
            stores.append(copies.start(hid_buf.at[pl.ds(0, lead), :], hid_q_hbm))
        out = dot(hid, w_out_buf[...])
        if i == 0:
            for j in range(steps):
                part_buf[j, ROWS:, :] = out[:8]
        for j in range(pair):
            part_buf[i + j, :ROWS, :] = out[skip + j * ROWS : skip + (j + 1) * ROWS]
            stores.append(copies.start(part_buf.at[i + j], part_hbm.at[i + j]))
        rows = pl.ds(lead + i * ROWS, pair * ROWS)
        stores.append(copies.start(hid_buf.at[rows, :], hid_hbm.at[pl.ds(i * ROWS, pair * ROWS), :]))
    for store in stores:
        store.wait()


FAR = pl.BlockSpec(memory_space=pltpu.HBM)
NEAR = pl.BlockSpec(memory_space=pltpu.VMEM)


def pinned(*arrays):
    return [pltpu.with_memory_space_constraint(a, pltpu.HBM) for a in arrays]


def forward(query_feats, item_feats, w_in, w_out):
    few = query_feats.shape[0]
    items, feats = item_feats.shape
    units = w_in.shape[1]
    width = w_out.shape[1]
    steps = items // ROWS
    return pl.pallas_call(
        forward_kernel,
        in_specs=[FAR] * 4,
        out_specs=[FAR] * 3,
        out_shape=[
            pltpu.HBM((steps, ROWS + 8, width), F32),
            pltpu.HBM((items, units), BF16),
            pltpu.HBM((16, units), BF16),
        ],
        scratch_shapes=[
            pltpu.VMEM((few, feats), BF16),
            pltpu.VMEM((16 + items, feats), BF16),
            pltpu.VMEM((feats, units), BF16),
            pltpu.VMEM((units, width), BF16),
            pltpu.VMEM((steps, ROWS + 8, width), F32),
            pltpu.VMEM((16 + items, units), BF16),
            pltpu.SemaphoreType.DMA((4 + 3 * steps,)),
        ],
        compiler_params=pltpu.CompilerParams(vmem_limit_bytes=VMEM),
    )(*pinned(query_feats, item_feats, w_in, w_out))


def row_ids(block, shape):
    return (lax.broadcasted_iota(jnp.int32, shape, 0) + block * shape[0]).astype(F32)


def counts_kernel(few, slots, info_ref, msg_ref, all_q_ref, digit_ref, code, digit):
    lines = msg_ref.shape[0]
    width = all_q_ref.shape[1]
    group = lines * 2 // few
    line = lax.broadcasted_iota(jnp.int32, (lines, lines), 0)
    column = lax.broadcasted_iota(jnp.int32, (lines, lines), 1)
    order = jnp.where(column == (line % group) * 2 + line // group, 1.0, 0.0).astype(BF16)
    turned = dot(order, msg_ref[...])
    parts = []
    for i in range(few):
        first = (i % 2) * width
        parts.append(turned[(i // 2) * group : (i // 2 + 1) * group, first : first + width])
    all_q_ref[...] = jnp.concatenate(parts, 0).astype(BF16)
    asked = turned[:group, 2 * width :].T
    who = asked[2 * slots : 3 * slots]
    code[:slots, :] = jnp.where(who > 0.0, asked[:slots] * 32.0 + asked[slots : 2 * slots], -1.0)
    power = jnp.zeros_like(who)
    for i in range(few):
        power = jnp.where(who == i + 1.0, 32.0**i, power)
    digit[:slots, :] = power
    lane = lax.broadcasted_iota(jnp.int32, (1, group), 1)
    for i in range(few):
        code[slots + i : slots + i + 1, :] = jnp.where(lane == info_ref[few], info_ref[i], -1).astype(F32)
        digit[slots + i : slots + i + 1, :] = jnp.full((1, group), 32.0**i, F32)
    for block, chunk in enumerate(blocks_of(digit_ref.shape[0])):
        ids = row_ids(block, (ROWS, group))
        digits = jnp.zeros((ROWS, group), F32)
        for s in range(slots + few):
            digits = digits + jnp.where(code[s : s + 1, :] == ids, digit[s : s + 1, :], 0.0)
        digit_ref[chunk, :] = digits.astype(jnp.int32)


def counts(info, message, few, slots, items, width):
    lines = message.shape[0]
    group = 2 * lines // few
    return pl.pallas_call(
        functools.partial(counts_kernel, few, slots),
        in_specs=[pl.BlockSpec(memory_space=pltpu.SMEM), NEAR],
        out_specs=[NEAR] * 2,
        out_shape=[
            jax.ShapeDtypeStruct((2 * lines, width), BF16),
            jax.ShapeDtypeStruct((items, group), jnp.int32),
        ],
        scratch_shapes=[pltpu.VMEM((slots + 8, group), F32)] * 2,
        compiler_params=pltpu.CompilerParams(vmem_limit_bytes=VMEM),
        cost_estimate=pl.CostEstimate(flops=3 * 2**30, bytes_accessed=2**20, transcendentals=0),
    )(info, message)


def score_kernel(
    few, scale, info_ref, own_ref, by1_ref, by2_ref, by3_ref, all_q_ref, digit_ref,
    weight_hbm, layer_hbm, all_q_hbm, pay_ref, weight_ref, layer_ref, total_u, emb, sems,
):
    copies = Copies(sems)
    queries, width = all_q_ref.shape
    group = queries // few
    near = (own_ref, by1_ref, by2_ref, by3_ref)
    for far, ref in enumerate(near):
        first = lax.rem(info_ref[few + 1] + len(near) - far, len(near)) * ROWS
        layer_ref[pl.ds(pl.multiple_of(first, ROWS), ROWS), :] = ref[...]
    stores = [copies.start(layer_ref, layer_hbm), copies.start(all_q_ref, all_q_hbm)]
    all_q = all_q_ref[...]

    total_d = jnp.zeros((1, queries), F32)
    for block, chunk in enumerate(blocks_of(layer_ref.shape[0])):
        e16 = jnp.tanh(layer_ref[chunk, :].astype(F32)).astype(BF16)
        emb[chunk, :] = e16
        grown = jnp.exp(scale * dot_lanes(e16, all_q))
        digits = digit_ref[chunk, :]
        times = [((digits >> (5 * i)) & 31).astype(F32) for i in range(few)]
        weight = jnp.concatenate(times, 1) * grown
        weight16 = weight.astype(BF16)
        weight_ref[chunk, :] = weight16
        stores.append(copies.start(weight_ref.at[chunk, :], weight_hbm.at[chunk, :]))
        total_d = total_d + jnp.sum(weight, 0, keepdims=True)

    total_u[...] = dot_rows(weight_ref[...], emb[...])
    d = jnp.concatenate([total_d[:, i * width : (i + 1) * width] for i in range(queries // width)], 0)
    high = d.astype(BF16).astype(F32)
    tail = jnp.concatenate([high, d - high, jnp.zeros((8 - 2 * d.shape[0], width), F32)], 0)
    for y in range(pay_ref.shape[0]):
        mine = [total_u[i * group + y * 8 : i * group + y * 8 + 8, :] for i in range(few)]
        pay_ref[y] = jnp.concatenate([*mine, tail], 0).astype(BF16)
    for store in stores:
        store.wait()


def score(info, layers, all_q, digits, few, scale, peers):
    share, width = layers[0].shape
    items = share * len(layers)
    queries = all_q.shape[0]
    pay = (peers, queries // peers + 8, width)
    return pl.pallas_call(
        functools.partial(score_kernel, few, scale),
        in_specs=[pl.BlockSpec(memory_space=pltpu.SMEM)] + [NEAR] * (len(layers) + 2),
        out_specs=[FAR] * 3 + [NEAR],
        out_shape=[
            pltpu.HBM((items, queries), BF16),
            pltpu.HBM((items, width), BF16),
            pltpu.HBM((queries, width), BF16),
            jax.ShapeDtypeStruct(pay, BF16),
        ],
        scratch_shapes=[
            pltpu.VMEM((items, queries), BF16),
            pltpu.VMEM((items, width), BF16),
            pltpu.VMEM((queries, width), F32),
            pltpu.VMEM((items, width), BF16),
            pltpu.SemaphoreType.DMA((3 + items // ROWS,)),
        ],
        compiler_params=pltpu.CompilerParams(vmem_limit_bytes=VMEM),
    )(info, *layers, all_q, digits)


def backward_kernel(
    few, scale, info_ref, all_q_hbm, weight_hbm, layer_hbm, hid_hbm, x_hbm, sums_ref, w_out_ref,
    emb_q_ref, hid_q_ref, q_ref, mine_ref, other_ref,
    all_q_ref, weight_ref, layer_ref, hid_ref, x_ref, item_grad, tanh_grad, pre_grad, summed, sems,
):
    items, width = layer_ref.shape
    feats = x_ref.shape[1]
    halves = [pl.ds(i * 2 * ROWS, 2 * ROWS) for i in range(items // (2 * ROWS))]
    copies = Copies(sems)
    load_q = copies.start(all_q_hbm, all_q_ref)
    load_weight = [copies.start(weight_hbm.at[half, :], weight_ref.at[half, :]) for half in halves]
    load_layer = copies.start(layer_hbm, layer_ref)
    load_hid = copies.start(hid_hbm, hid_ref)
    load_x = copies.start(x_hbm, x_ref)

    queries = all_q_ref.shape[0]
    group = queries // few
    sums = jnp.sum(sums_ref[...].astype(F32), 0)
    d = sums[few : few + 2] + sums[few + 2 : few + 4]
    d = jnp.concatenate([d[0:1], d[1:2]], 1)
    factor = jnp.broadcast_to(scale / d, (8, queries)).T[:, :1]
    line = lax.broadcasted_iota(jnp.int32, (8, queries), 0)
    own_lane = lax.broadcasted_iota(jnp.int32, (8, queries), 1)
    own_d = jnp.sum(jnp.where(own_lane == line * group + info_ref[few], d, 0.0), 1, keepdims=True)
    emb_q = emb_q_ref[...]
    own_q = emb_q.astype(BF16).astype(F32)
    load_q.wait()
    scaled = (all_q_ref[...].astype(F32) * factor).astype(BF16)
    for half, load in zip(halves, load_weight):
        load.wait()
        item_grad[half, :] = dot(weight_ref[half, :], scaled)
    load_layer.wait()
    named = []
    for i in range(few):
        place = info_ref[i]
        item_grad[pl.ds(place, 1), :] = item_grad[pl.ds(place, 1), :] - scale * own_q[i : i + 1]
        base = (place // 16) * 16
        near = layer_ref[pl.ds(pl.multiple_of(base, 16), 16), :].astype(F32)
        at = lax.broadcasted_iota(jnp.int32, near.shape, 0) == place - base
        named.append(jnp.sum(jnp.where(at, near, 0.0), 0, keepdims=True))
    named.append(jnp.zeros((8 - few, width), F32))
    pos_emb = jnp.tanh(jnp.concatenate(named, 0)).astype(BF16).astype(F32)

    load_hid.wait()
    for chunk in halves:
        e = jnp.tanh(layer_ref[chunk, :].astype(F32))
        grad = (item_grad[chunk, :] * (1.0 - e * e)).astype(BF16)
        tanh_grad[chunk, :] = grad
        hid_grad = dot_lanes(grad, w_out_ref[...])
        pre_grad[chunk, :] = jnp.where(hid_ref[chunk, :] > 0, hid_grad, 0.0).astype(BF16)

    live = lax.broadcasted_iota(jnp.int32, (8, width), 0) < few
    grad = scale * (sums / own_d - pos_emb) * (1.0 - emb_q * emb_q)
    grad = jnp.where(live, grad, 0.0)
    grad_q = jnp.concatenate([grad, jnp.zeros_like(grad)], 0).astype(BF16)
    hid_q = hid_q_ref[...]
    pre_grad_q = jnp.where(hid_q > 0, dot_lanes(grad_q, w_out_ref[...]), 0.0).astype(BF16)
    load_x.wait()
    in_total = dot_rows(pre_grad[...], x_ref[...]) + dot_rows(pre_grad_q, q_ref[...])
    summed[:feats, :] = in_total.astype(BF16).T
    summed[feats:, :] = (dot_rows(hid_ref[...], tanh_grad[...]) + dot_rows(hid_q, grad_q)).astype(BF16)
    half = mine_ref.shape[0]
    core = info_ref[few + 2]

    @pl.when(core == 0)
    def _():
        mine_ref[...] = summed[:half, :]
        other_ref[...] = summed[half:, :]

    @pl.when(core != 0)
    def _():
        mine_ref[...] = summed[half:, :]
        other_ref[...] = summed[:half, :]


def backward(info, far, near, few, scale):
    items, width = far[2].shape
    units = far[3].shape[1]
    feats = far[4].shape[1]
    return pl.pallas_call(
        functools.partial(backward_kernel, few, scale),
        in_specs=[pl.BlockSpec(memory_space=pltpu.SMEM)] + [FAR] * len(far) + [NEAR] * len(near),
        out_specs=[NEAR] * 2,
        out_shape=[jax.ShapeDtypeStruct(((feats + units) // 2, width), BF16)] * 2,
        scratch_shapes=[
            *[pltpu.VMEM(a.shape, a.dtype) for a in far],
            pltpu.VMEM((items, width), F32),
            pltpu.VMEM((items, width), BF16),
            pltpu.VMEM((items, units), BF16),
            pltpu.VMEM((feats + units, width), BF16),
            pltpu.SemaphoreType.DMA((4 + items // (2 * ROWS),)),
        ],
        compiler_params=pltpu.CompilerParams(vmem_limit_bytes=VMEM),
    )(info, *pinned(*far), *near)


def assemble_kernel(core_ref, mine_ref, other_ref, in_hbm, out_hbm, sems):
    half = mine_ref.shape[0]
    rest = in_hbm.shape[0] - half

    def place(first, second):
        copies = Copies(sems)
        made = [
            copies.start(first, in_hbm.at[pl.ds(0, half), :]),
            copies.start(second.at[pl.ds(0, rest), :], in_hbm.at[pl.ds(half, rest), :]),
            copies.start(second.at[pl.ds(rest, half - rest), :], out_hbm),
        ]
        for copy in made:
            copy.wait()

    @pl.when(core_ref[0] == 0)
    def _():
        place(mine_ref, other_ref)

    @pl.when(core_ref[0] != 0)
    def _():
        place(other_ref, mine_ref)


def assemble(mine, other, feats):
    half, width = mine.shape
    return pl.pallas_call(
        assemble_kernel,
        in_specs=[pl.BlockSpec(memory_space=pltpu.SMEM)] + [NEAR] * 2,
        out_specs=[FAR] * 2,
        out_shape=[
            jax.ShapeDtypeStruct((feats, width), BF16),
            jax.ShapeDtypeStruct((2 * half - feats, width), BF16),
        ],
        scratch_shapes=[pltpu.SemaphoreType.DMA((3,))],
        compiler_params=pltpu.CompilerParams(vmem_limit_bytes=VMEM),
    )(lax.axis_index("c").reshape(1), mine, other)


def request_codes(rows, query_count, item_count, capacity, order, dp_count):
    pairs = rows.shape[0]
    owners = rows // item_count
    code = rows - owners * item_count
    owner_hot = order(owners)[:, None] == jnp.arange(dp_count, dtype=jnp.int32)[None, :]
    earlier = jnp.arange(pairs)[:, None] >= jnp.arange(pairs)[None, :]
    running = dot(earlier.astype(BF16), owner_hot.astype(BF16))
    slot = jnp.sum(jnp.where(owner_hot, running, 0.0), 1).astype(jnp.int32) - 1
    who = jnp.arange(pairs, dtype=jnp.int32) // (pairs // query_count) + 1
    lane = jnp.arange(128, dtype=jnp.int32)[None, :]
    value = jnp.zeros((pairs, 128), jnp.int32)
    for at, part in enumerate((code // 32, code % 32, who)):
        value = jnp.where(slot[:, None] + at * capacity == lane, part[:, None], value)
    return dot_rows(owner_hot.astype(BF16), value.astype(BF16)).astype(BF16)


def local(query_feats, item_feats, w_in, w_out, negatives, positives, owner_map):
    dp_count = lax.axis_size(DP)
    own_index = lax.axis_index(DP)
    z_count = lax.axis_size("z")
    x_count = lax.axis_size("x")
    yc_count = dp_count // z_count
    few = query_feats.shape[0]
    item_count = item_feats.shape[0]
    width = w_out.shape[1]
    negative_count = negatives.shape[1]
    scale = 4.0 / math.sqrt(width)
    capacity = 4 * few * negative_count // dp_count
    queries = few * dp_count

    blocks, hidden, hidden_q = forward(query_feats, item_feats, w_in, w_out)
    arrived = exchange(blocks, "x")

    named = jnp.concatenate([negatives.reshape(-1), positives])
    rows = jnp.take(owner_map, named, axis=0)
    pos_local = jnp.clip(rows[few * negative_count :] - own_index * item_count, 0, item_count - 1)
    places = [lax.axis_index(YCZ), lax.axis_index("x"), lax.axis_index("c")]
    info = jnp.concatenate([pos_local, jnp.stack(places)])
    codes = request_codes(
        rows[: few * negative_count],
        few,
        item_count,
        capacity,
        lambda o: (o % yc_count) * z_count + o // yc_count,
        dp_count,
    )
    codes = jnp.pad(codes[:, None, :], ((0, 0), (0, 1), (0, 0)))

    own = total(arrived[:, :ROWS]).astype(BF16)
    own_q = jnp.tanh(total(arrived[:, ROWS:]))
    sent_q = jnp.broadcast_to(own_q[:few].astype(BF16).reshape(1, 2, -1), (dp_count, 2, few // 2 * width))
    message = exchange(jnp.concatenate([sent_q, codes], 2), YCZ)
    message = message.reshape(2 * dp_count, -1)
    layers = [own]
    for far in range(1, x_count):
        layers.append(lax.ppermute(own, "x", [(i, (i + far) % x_count) for i in range(x_count)]))

    all_q, digits = counts(info, message, few, capacity, item_count, width)
    weight, layer_out, all_q, pay = score(info, layers, all_q, digits, few, scale, yc_count)
    first = total(exchange(pay, ("y", "c")))
    mine = queries // yc_count
    d_rows = queries // width
    d_part = first[mine : mine + d_rows] + first[mine + d_rows : mine + 2 * d_rows]
    high = d_part.astype(BF16)
    tail = jnp.concatenate([high, (d_part - high.astype(F32)).astype(BF16)], 0)
    sums = exchange(
        jnp.concatenate(
            [
                first[:mine].astype(BF16).reshape(few, z_count, width).transpose(1, 0, 2),
                jnp.broadcast_to(tail[None], (z_count, 2 * d_rows, width)),
            ],
            1,
        ),
        "z",
    )
    feats_q = jnp.pad(query_feats, ((0, 16 - few), (0, 0)))
    near = (sums, w_out, own_q, hidden_q, feats_q)
    mine, other = backward(info, (all_q, weight, layer_out, hidden, item_feats), near, few, scale)
    y_count = lax.axis_size("y")
    swap = [(0, 1), (1, 0)]
    grads = (mine.astype(F32) + lax.ppermute(other, "c", swap).astype(F32)).astype(BF16)
    grads = total(exchange(grads.reshape(y_count, -1, width), "y"))
    grads = total(spread(grads.astype(BF16), "z")).astype(BF16)
    grads = spread(grads, "y").reshape(-1, width)
    return tuple(assemble(grads, lax.ppermute(grads, "c", swap), w_in.shape[0]))


def solution(mesh):
    grid = Mesh(mesh.devices.reshape(8, 8, 2, 4), ("z", "y", "c", "x"))
    return jax.shard_map(
        local,
        mesh=grid,
        in_specs=(
            P(DP, None),
            P(DP, None),
            P(None, "x"),
            P("x", None),
            P(DP, None),
            P(DP),
            P(),
        ),
        out_specs=(P(None, "x"), P("x", None)),
        check_vma=False,
    )
```

```python
import functools
import math

import jax
import jax.numpy as jnp
from jax import lax
from jax.experimental import pallas as pl
from jax.experimental.pallas import tpu as pltpu
from jax.sharding import Mesh, PartitionSpec as P

F32 = jnp.float32
BF16 = jnp.bfloat16
DP = ("z", "y", "c")
YCZ = ("y", "c", "z")
ROWS = 256
VMEM = 20 * 1024 * 1024


def exchange(blocks, axes):
    return lax.all_to_all(blocks, axes, split_axis=0, concat_axis=0, tiled=True)


def spread(block, axes):
    count = lax.axis_size(axes)
    return exchange(jnp.broadcast_to(block[None], (count,) + block.shape), axes)


def total(blocks):
    return jnp.sum(blocks.astype(F32), 0)


def dot(a, b):
    return jnp.dot(a, b, preferred_element_type=F32)


def dot_rows(a, b):
    return lax.dot_general(a, b, (((0,), (0,)), ((), ())), preferred_element_type=F32)


def dot_lanes(a, b):
    return lax.dot_general(a, b, (((1,), (1,)), ((), ())), preferred_element_type=F32)


def blocks_of(items):
    return [pl.ds(i * ROWS, ROWS) for i in range(items // ROWS)]


class Copies:
    def __init__(self, sems):
        self.sems = sems
        self.used = 0

    def start(self, source, target):
        copy = pltpu.make_async_copy(source, target, self.sems.at[self.used])
        copy.start()
        self.used += 1
        return copy


def forward_kernel(
    q_hbm, x_hbm, w_in_hbm, w_out_hbm, part_hbm, hid_hbm, hid_q_hbm,
    q_buf, x_buf, w_in_buf, w_out_buf, part_buf, hid_buf, sems,
):
    few, feats = q_buf.shape
    steps = part_buf.shape[0]
    lead = x_buf.shape[0] - steps * ROWS
    copies = Copies(sems)
    load_in = copies.start(w_in_hbm, w_in_buf)
    load_q = copies.start(q_hbm, q_buf)
    load_x = []
    for i in range(steps):
        source = x_hbm.at[pl.ds(i * ROWS, ROWS), :]
        load_x.append(copies.start(source, x_buf.at[pl.ds(lead + i * ROWS, ROWS), :]))
    load_out = copies.start(w_out_hbm, w_out_buf)
    load_q.wait()
    padded = jnp.concatenate([q_buf[...].astype(F32), jnp.zeros((lead - few, feats), F32)], 0)
    x_buf[:lead, :] = padded.astype(BF16)
    stores = []
    load_in.wait()
    pair = 2
    for i in range(0, steps, pair):
        for load in load_x[i : i + pair]:
            load.wait()
        first = 0 if i == 0 else lead + i * ROWS
        skip = lead if i == 0 else 0
        span = pl.ds(first, skip + pair * ROWS)
        hid = jnp.maximum(dot(x_buf[span, :], w_in_buf[...]), 0.0).astype(BF16)
        hid_buf[span, :] = hid
        if i == 0:
            load_out.wait()
            stores.append(copies.start(hid_buf.at[pl.ds(0, lead), :], hid_q_hbm))
        out = dot(hid, w_out_buf[...])
        if i == 0:
            for j in range(steps):
                part_buf[j, ROWS:, :] = out[:8]
        for j in range(pair):
            part_buf[i + j, :ROWS, :] = out[skip + j * ROWS : skip + (j + 1) * ROWS]
            stores.append(copies.start(part_buf.at[i + j], part_hbm.at[i + j]))
        rows = pl.ds(lead + i * ROWS, pair * ROWS)
        stores.append(copies.start(hid_buf.at[rows, :], hid_hbm.at[pl.ds(i * ROWS, pair * ROWS), :]))
    for store in stores:
        store.wait()


FAR = pl.BlockSpec(memory_space=pltpu.HBM)
NEAR = pl.BlockSpec(memory_space=pltpu.VMEM)


def pinned(*arrays):
    return [pltpu.with_memory_space_constraint(a, pltpu.HBM) for a in arrays]


def forward(query_feats, item_feats, w_in, w_out):
    few = query_feats.shape[0]
    items, feats = item_feats.shape
    units = w_in.shape[1]
    width = w_out.shape[1]
    steps = items // ROWS
    return pl.pallas_call(
        forward_kernel,
        in_specs=[FAR] * 4,
        out_specs=[FAR] * 3,
        out_shape=[
            pltpu.HBM((steps, ROWS + 8, width), F32),
            pltpu.HBM((items, units), BF16),
            pltpu.HBM((16, units), BF16),
        ],
        scratch_shapes=[
            pltpu.VMEM((few, feats), BF16),
            pltpu.VMEM((16 + items, feats), BF16),
            pltpu.VMEM((feats, units), BF16),
            pltpu.VMEM((units, width), BF16),
            pltpu.VMEM((steps, ROWS + 8, width), F32),
            pltpu.VMEM((16 + items, units), BF16),
            pltpu.SemaphoreType.DMA((4 + 3 * steps,)),
        ],
        compiler_params=pltpu.CompilerParams(vmem_limit_bytes=VMEM),
    )(*pinned(query_feats, item_feats, w_in, w_out))


def row_ids(block, shape):
    return (lax.broadcasted_iota(jnp.int32, shape, 0) + block * shape[0]).astype(F32)


def weighed(scale, few, layer, all_q, digits):
    emb = jnp.tanh(layer.astype(F32)).astype(BF16)
    times = [((digits >> (5 * i)) & 31).astype(F32) for i in range(few)]
    weight = jnp.concatenate(times, 1) * jnp.exp(scale * dot_lanes(emb, all_q))
    return emb, weight


def share_of(info_ref, few, far):
    return pl.ds(pl.multiple_of(lax.bitwise_xor(info_ref[few + 1], far) * ROWS, ROWS), ROWS)


def counts_kernel(
    few, slots, scale, info_ref, msg_ref, own_ref, all_q_ref, digit_ref, weight_ref, d_ref, code, digit
):
    lines = msg_ref.shape[0]
    width = all_q_ref.shape[1]
    group = lines * 2 // few
    line = lax.broadcasted_iota(jnp.int32, (lines, lines), 0)
    column = lax.broadcasted_iota(jnp.int32, (lines, lines), 1)
    order = jnp.where(column == (line % group) * 2 + line // group, 1.0, 0.0).astype(BF16)
    turned = dot(order, msg_ref[...])
    parts = []
    for i in range(few):
        first = (i % 2) * width
        parts.append(turned[(i // 2) * group : (i // 2 + 1) * group, first : first + width])
    all_q_ref[...] = jnp.concatenate(parts, 0).astype(BF16)
    asked = turned[:group, 2 * width :].T
    who = asked[2 * slots : 3 * slots]
    code[:slots, :] = jnp.where(who > 0.0, asked[:slots] * 32.0 + asked[slots : 2 * slots], -1.0)
    power = jnp.zeros_like(who)
    for i in range(few):
        power = jnp.where(who == i + 1.0, 32.0**i, power)
    digit[:slots, :] = power
    lane = lax.broadcasted_iota(jnp.int32, (1, group), 1)
    for i in range(few):
        code[slots + i : slots + i + 1, :] = jnp.where(lane == info_ref[few], info_ref[i], -1).astype(F32)
        digit[slots + i : slots + i + 1, :] = jnp.full((1, group), 32.0**i, F32)
    for block, chunk in enumerate(blocks_of(digit_ref.shape[0])):
        ids = row_ids(block, (ROWS, group))
        digits = jnp.zeros((ROWS, group), F32)
        for s in range(slots + few):
            digits = digits + jnp.where(code[s : s + 1, :] == ids, digit[s : s + 1, :], 0.0)
        digit_ref[chunk, :] = digits.astype(jnp.int32)
    own_digits = digit_ref[share_of(info_ref, few, 0), :]
    weight = weighed(scale, few, own_ref[...], all_q_ref[...], own_digits)[1]
    weight_ref[...] = weight.astype(BF16)
    d_ref[...] = jnp.sum(weight, 0, keepdims=True)


def counts(info, message, own, few, slots, scale, items):
    width = own.shape[1]
    lines = message.shape[0]
    group = 2 * lines // few
    return pl.pallas_call(
        functools.partial(counts_kernel, few, slots, scale),
        in_specs=[pl.BlockSpec(memory_space=pltpu.SMEM), NEAR, NEAR],
        out_specs=[NEAR] * 4,
        out_shape=[
            jax.ShapeDtypeStruct((2 * lines, width), BF16),
            jax.ShapeDtypeStruct((items, group), jnp.int32),
            jax.ShapeDtypeStruct((own.shape[0], 2 * lines), BF16),
            jax.ShapeDtypeStruct((1, 2 * lines), F32),
        ],
        scratch_shapes=[pltpu.VMEM((slots + 8, group), F32)] * 2,
        compiler_params=pltpu.CompilerParams(vmem_limit_bytes=VMEM),
        cost_estimate=pl.CostEstimate(flops=3 * 2**30, bytes_accessed=2**20, transcendentals=0),
    )(info, message, own)


def score_kernel(
    few, scale, info_ref, own_ref, by2_ref, by1_ref, by3_ref, all_q_ref, digit_ref, own_weight_ref, own_d_ref,
    weight_hbm, layer_hbm, all_q_hbm, pay_ref, weight_ref, layer_ref, total_u, emb, sems,
):
    copies = Copies(sems)
    queries, width = all_q_ref.shape
    group = queries // few
    near = (own_ref, by1_ref, by2_ref, by3_ref)
    for far, ref in enumerate(near):
        layer_ref[share_of(info_ref, few, far), :] = ref[...]
    stores = [copies.start(layer_ref, layer_hbm), copies.start(all_q_ref, all_q_hbm)]
    all_q = all_q_ref[...]

    total_d = own_d_ref[...]
    for far, ref in enumerate(near):
        chunk = share_of(info_ref, few, far)
        if far == 0:
            emb[chunk, :] = jnp.tanh(ref[...].astype(F32)).astype(BF16)
            weight_ref[chunk, :] = own_weight_ref[...]
        else:
            e16, weight = weighed(scale, few, ref[...], all_q, digit_ref[chunk, :])
            emb[chunk, :] = e16
            weight_ref[chunk, :] = weight.astype(BF16)
            total_d = total_d + jnp.sum(weight, 0, keepdims=True)
        stores.append(copies.start(weight_ref.at[chunk, :], weight_hbm.at[chunk, :]))

    total_u[...] = dot_rows(weight_ref[...], emb[...])
    d = jnp.concatenate([total_d[:, i * width : (i + 1) * width] for i in range(queries // width)], 0)
    high = d.astype(BF16).astype(F32)
    tail = jnp.concatenate([high, d - high, jnp.zeros((8 - 2 * d.shape[0], width), F32)], 0)
    for y in range(pay_ref.shape[0]):
        mine = [total_u[i * group + y * 8 : i * group + y * 8 + 8, :] for i in range(few)]
        pay_ref[y] = jnp.concatenate([*mine, tail], 0).astype(BF16)
    for store in stores:
        store.wait()


def score(info, layers, counted, few, scale, peers):
    share, width = layers[0].shape
    items = share * len(layers)
    queries = counted[0].shape[0]
    pay = (peers, queries // peers + 8, width)
    return pl.pallas_call(
        functools.partial(score_kernel, few, scale),
        in_specs=[pl.BlockSpec(memory_space=pltpu.SMEM)] + [NEAR] * (len(layers) + len(counted)),
        out_specs=[FAR] * 3 + [NEAR],
        out_shape=[
            pltpu.HBM((items, queries), BF16),
            pltpu.HBM((items, width), BF16),
            pltpu.HBM((queries, width), BF16),
            jax.ShapeDtypeStruct(pay, BF16),
        ],
        scratch_shapes=[
            pltpu.VMEM((items, queries), BF16),
            pltpu.VMEM((items, width), BF16),
            pltpu.VMEM((queries, width), F32),
            pltpu.VMEM((items, width), BF16),
            pltpu.SemaphoreType.DMA((3 + items // ROWS,)),
        ],
        compiler_params=pltpu.CompilerParams(vmem_limit_bytes=VMEM),
    )(info, *layers, *counted)


def backward_kernel(
    few, scale, info_ref, all_q_hbm, weight_hbm, layer_hbm, hid_hbm, x_hbm, sums_ref, w_out_ref,
    emb_q_ref, hid_q_ref, q_ref, mine_ref, other_ref,
    all_q_ref, weight_ref, layer_ref, hid_ref, x_ref, item_grad, tanh_grad, pre_grad, summed, sems,
):
    items, width = layer_ref.shape
    feats = x_ref.shape[1]
    halves = [pl.ds(i * 2 * ROWS, 2 * ROWS) for i in range(items // (2 * ROWS))]
    copies = Copies(sems)
    load_q = copies.start(all_q_hbm, all_q_ref)
    load_weight = [copies.start(weight_hbm.at[half, :], weight_ref.at[half, :]) for half in halves]
    load_layer = copies.start(layer_hbm, layer_ref)
    load_hid = copies.start(hid_hbm, hid_ref)
    load_x = copies.start(x_hbm, x_ref)

    queries = all_q_ref.shape[0]
    group = queries // few
    sums = jnp.sum(sums_ref[...].astype(F32), 0)
    d = sums[few : few + 2] + sums[few + 2 : few + 4]
    d = jnp.concatenate([d[0:1], d[1:2]], 1)
    factor = jnp.broadcast_to(scale / d, (8, queries)).T[:, :1]
    line = lax.broadcasted_iota(jnp.int32, (8, queries), 0)
    own_lane = lax.broadcasted_iota(jnp.int32, (8, queries), 1)
    own_d = jnp.sum(jnp.where(own_lane == line * group + info_ref[few], d, 0.0), 1, keepdims=True)
    emb_q = emb_q_ref[...]
    own_q = emb_q.astype(BF16).astype(F32)
    load_q.wait()
    scaled = (all_q_ref[...].astype(F32) * factor).astype(BF16)
    for half, load in zip(halves, load_weight):
        load.wait()
        item_grad[half, :] = dot(weight_ref[half, :], scaled)
    load_layer.wait()
    named = []
    for i in range(few):
        place = info_ref[i]
        item_grad[pl.ds(place, 1), :] = item_grad[pl.ds(place, 1), :] - scale * own_q[i : i + 1]
        base = (place // 16) * 16
        near = layer_ref[pl.ds(pl.multiple_of(base, 16), 16), :].astype(F32)
        at = lax.broadcasted_iota(jnp.int32, near.shape, 0) == place - base
        named.append(jnp.sum(jnp.where(at, near, 0.0), 0, keepdims=True))
    named.append(jnp.zeros((8 - few, width), F32))
    pos_emb = jnp.tanh(jnp.concatenate(named, 0)).astype(BF16).astype(F32)

    load_hid.wait()
    for chunk in halves:
        e = jnp.tanh(layer_ref[chunk, :].astype(F32))
        grad = (item_grad[chunk, :] * (1.0 - e * e)).astype(BF16)
        tanh_grad[chunk, :] = grad
        hid_grad = dot_lanes(grad, w_out_ref[...])
        pre_grad[chunk, :] = jnp.where(hid_ref[chunk, :] > 0, hid_grad, 0.0).astype(BF16)

    live = lax.broadcasted_iota(jnp.int32, (8, width), 0) < few
    grad = scale * (sums / own_d - pos_emb) * (1.0 - emb_q * emb_q)
    grad = jnp.where(live, grad, 0.0)
    grad_q = jnp.concatenate([grad, jnp.zeros_like(grad)], 0).astype(BF16)
    hid_q = hid_q_ref[...]
    pre_grad_q = jnp.where(hid_q > 0, dot_lanes(grad_q, w_out_ref[...]), 0.0).astype(BF16)
    load_x.wait()
    in_total = dot_rows(pre_grad[...], x_ref[...]) + dot_rows(pre_grad_q, q_ref[...])
    summed[:feats, :] = in_total.astype(BF16).T
    summed[feats:, :] = (dot_rows(hid_ref[...], tanh_grad[...]) + dot_rows(hid_q, grad_q)).astype(BF16)
    half = mine_ref.shape[0]
    core = info_ref[few + 2]

    @pl.when(core == 0)
    def _():
        mine_ref[...] = summed[:half, :]
        other_ref[...] = summed[half:, :]

    @pl.when(core != 0)
    def _():
        mine_ref[...] = summed[half:, :]
        other_ref[...] = summed[:half, :]


def backward(info, far, near, few, scale):
    items, width = far[2].shape
    units = far[3].shape[1]
    feats = far[4].shape[1]
    return pl.pallas_call(
        functools.partial(backward_kernel, few, scale),
        in_specs=[pl.BlockSpec(memory_space=pltpu.SMEM)] + [FAR] * len(far) + [NEAR] * len(near),
        out_specs=[NEAR] * 2,
        out_shape=[jax.ShapeDtypeStruct(((feats + units) // 2, width), BF16)] * 2,
        scratch_shapes=[
            *[pltpu.VMEM(a.shape, a.dtype) for a in far],
            pltpu.VMEM((items, width), F32),
            pltpu.VMEM((items, width), BF16),
            pltpu.VMEM((items, units), BF16),
            pltpu.VMEM((feats + units, width), BF16),
            pltpu.SemaphoreType.DMA((4 + items // (2 * ROWS),)),
        ],
        compiler_params=pltpu.CompilerParams(vmem_limit_bytes=VMEM),
    )(info, *pinned(*far), *near)


def assemble_kernel(core_ref, mine_ref, other_ref, in_hbm, out_hbm, sems):
    half = mine_ref.shape[0]
    rest = in_hbm.shape[0] - half

    def place(first, second):
        copies = Copies(sems)
        made = [
            copies.start(first, in_hbm.at[pl.ds(0, half), :]),
            copies.start(second.at[pl.ds(0, rest), :], in_hbm.at[pl.ds(half, rest), :]),
            copies.start(second.at[pl.ds(rest, half - rest), :], out_hbm),
        ]
        for copy in made:
            copy.wait()

    @pl.when(core_ref[0] == 0)
    def _():
        place(mine_ref, other_ref)

    @pl.when(core_ref[0] != 0)
    def _():
        place(other_ref, mine_ref)


def assemble(mine, other, feats):
    half, width = mine.shape
    return pl.pallas_call(
        assemble_kernel,
        in_specs=[pl.BlockSpec(memory_space=pltpu.SMEM)] + [NEAR] * 2,
        out_specs=[FAR] * 2,
        out_shape=[
            jax.ShapeDtypeStruct((feats, width), BF16),
            jax.ShapeDtypeStruct((2 * half - feats, width), BF16),
        ],
        scratch_shapes=[pltpu.SemaphoreType.DMA((3,))],
        compiler_params=pltpu.CompilerParams(vmem_limit_bytes=VMEM),
    )(lax.axis_index("c").reshape(1), mine, other)


def request_codes(rows, query_count, item_count, capacity, order, dp_count):
    pairs = rows.shape[0]
    owners = rows // item_count
    code = rows - owners * item_count
    owner_hot = order(owners)[:, None] == jnp.arange(dp_count, dtype=jnp.int32)[None, :]
    earlier = jnp.arange(pairs)[:, None] >= jnp.arange(pairs)[None, :]
    running = dot(earlier.astype(BF16), owner_hot.astype(BF16))
    slot = jnp.sum(jnp.where(owner_hot, running, 0.0), 1).astype(jnp.int32) - 1
    who = jnp.arange(pairs, dtype=jnp.int32) // (pairs // query_count) + 1
    lane = jnp.arange(128, dtype=jnp.int32)[None, :]
    value = jnp.zeros((pairs, 128), jnp.int32)
    for at, part in enumerate((code // 32, code % 32, who)):
        value = jnp.where(slot[:, None] + at * capacity == lane, part[:, None], value)
    return dot_rows(owner_hot.astype(BF16), value.astype(BF16)).astype(BF16)


def local(query_feats, item_feats, w_in, w_out, negatives, positives, owner_map):
    dp_count = lax.axis_size(DP)
    own_index = lax.axis_index(DP)
    z_count = lax.axis_size("z")
    x_count = lax.axis_size("x")
    yc_count = dp_count // z_count
    few = query_feats.shape[0]
    item_count = item_feats.shape[0]
    width = w_out.shape[1]
    negative_count = negatives.shape[1]
    scale = 4.0 / math.sqrt(width)
    capacity = 4 * few * negative_count // dp_count
    queries = few * dp_count

    blocks, hidden, hidden_q = forward(query_feats, item_feats, w_in, w_out)
    arrived = exchange(blocks, "x")

    named = jnp.concatenate([negatives.reshape(-1), positives])
    rows = jnp.take(owner_map, named, axis=0)
    pos_local = jnp.clip(rows[few * negative_count :] - own_index * item_count, 0, item_count - 1)
    places = [lax.axis_index(YCZ), lax.axis_index("x"), lax.axis_index("c")]
    info = jnp.concatenate([pos_local, jnp.stack(places)])
    codes = request_codes(
        rows[: few * negative_count],
        few,
        item_count,
        capacity,
        lambda o: (o % yc_count) * z_count + o // yc_count,
        dp_count,
    )
    codes = jnp.pad(codes[:, None, :], ((0, 0), (0, 1), (0, 0)))

    own = total(arrived[:, :ROWS]).astype(BF16)
    own_q = jnp.tanh(total(arrived[:, ROWS:]))
    sent_q = jnp.broadcast_to(own_q[:few].astype(BF16).reshape(1, 2, -1), (dp_count, 2, few // 2 * width))
    message = exchange(jnp.concatenate([sent_q, codes], 2), YCZ)
    message = message.reshape(2 * dp_count, -1)
    layers = [own]
    for far in (2, 1, 3):
        layers.append(lax.ppermute(own, "x", [(i, i ^ far) for i in range(x_count)]))

    counted = counts(info, message, own, few, capacity, scale, item_count)
    weight, layer_out, all_q, pay = score(info, layers, counted, few, scale, yc_count)
    first = total(exchange(pay, ("y", "c")))
    mine = queries // yc_count
    d_rows = queries // width
    d_part = first[mine : mine + d_rows] + first[mine + d_rows : mine + 2 * d_rows]
    high = d_part.astype(BF16)
    tail = jnp.concatenate([high, (d_part - high.astype(F32)).astype(BF16)], 0)
    sums = exchange(
        jnp.concatenate(
            [
                first[:mine].astype(BF16).reshape(few, z_count, width).transpose(1, 0, 2),
                jnp.broadcast_to(tail[None], (z_count, 2 * d_rows, width)),
            ],
            1,
        ),
        "z",
    )
    feats_q = jnp.pad(query_feats, ((0, 16 - few), (0, 0)))
    near = (sums, w_out, own_q, hidden_q, feats_q)
    mine, other = backward(info, (all_q, weight, layer_out, hidden, item_feats), near, few, scale)
    y_count = lax.axis_size("y")
    swap = [(0, 1), (1, 0)]
    grads = (mine.astype(F32) + lax.ppermute(other, "c", swap).astype(F32)).astype(BF16)
    grads = total(exchange(grads.reshape(y_count, -1, width), "y"))
    grads = total(spread(grads.astype(BF16), "z")).astype(BF16)
    grads = spread(grads, "y").reshape(-1, width)
    return tuple(assemble(grads, lax.ppermute(grads, "c", swap), w_in.shape[0]))


def solution(mesh):
    grid = Mesh(mesh.devices.reshape(8, 8, 2, 4), ("z", "y", "c", "x"))
    return jax.shard_map(
        local,
        mesh=grid,
        in_specs=(
            P(DP, None),
            P(DP, None),
            P(None, "x"),
            P("x", None),
            P(DP, None),
            P(DP),
            P(),
        ),
        out_specs=(P(None, "x"), P("x", None)),
        check_vma=False,
    )
```

```python
import functools
import math

import jax
import jax.numpy as jnp
from jax import lax
from jax.experimental import pallas as pl
from jax.experimental.pallas import tpu as pltpu
from jax.sharding import Mesh, PartitionSpec as P

F32 = jnp.float32
BF16 = jnp.bfloat16
DP = ("z", "y", "c")
YCZ = ("y", "c", "z")
ROWS = 256
VMEM = 20 * 1024 * 1024


def exchange(blocks, axes):
    return lax.all_to_all(blocks, axes, split_axis=0, concat_axis=0, tiled=True)


def spread(block, axes):
    count = lax.axis_size(axes)
    return exchange(jnp.broadcast_to(block[None], (count,) + block.shape), axes)


def total(blocks):
    return jnp.sum(blocks.astype(F32), 0)


def dot(a, b):
    return jnp.dot(a, b, preferred_element_type=F32)


def dot_rows(a, b):
    return lax.dot_general(a, b, (((0,), (0,)), ((), ())), preferred_element_type=F32)


def dot_lanes(a, b):
    return lax.dot_general(a, b, (((1,), (1,)), ((), ())), preferred_element_type=F32)


def blocks_of(items):
    return [pl.ds(i * ROWS, ROWS) for i in range(items // ROWS)]


class Copies:
    def __init__(self, sems):
        self.sems = sems
        self.used = 0

    def start(self, source, target):
        copy = pltpu.make_async_copy(source, target, self.sems.at[self.used])
        copy.start()
        self.used += 1
        return copy


def forward_kernel(
    q_hbm, x_hbm, w_in_hbm, w_out_hbm, part_hbm, hid_hbm, hid_q_hbm,
    q_buf, x_buf, w_in_buf, w_out_buf, part_buf, hid_buf, sems,
):
    few, feats = q_buf.shape
    steps = part_buf.shape[0]
    lead = x_buf.shape[0] - steps * ROWS
    copies = Copies(sems)
    load_in = copies.start(w_in_hbm, w_in_buf)
    load_q = copies.start(q_hbm, q_buf)
    load_x = []
    for i in range(steps):
        source = x_hbm.at[pl.ds(i * ROWS, ROWS), :]
        load_x.append(copies.start(source, x_buf.at[pl.ds(lead + i * ROWS, ROWS), :]))
    load_out = copies.start(w_out_hbm, w_out_buf)
    load_q.wait()
    padded = jnp.concatenate([q_buf[...].astype(F32), jnp.zeros((lead - few, feats), F32)], 0)
    x_buf[:lead, :] = padded.astype(BF16)
    stores = []
    load_in.wait()
    pair = 2
    for i in range(0, steps, pair):
        for load in load_x[i : i + pair]:
            load.wait()
        first = 0 if i == 0 else lead + i * ROWS
        skip = lead if i == 0 else 0
        span = pl.ds(first, skip + pair * ROWS)
        hid = jnp.maximum(dot(x_buf[span, :], w_in_buf[...]), 0.0).astype(BF16)
        hid_buf[span, :] = hid
        if i == 0:
            load_out.wait()
            stores.append(copies.start(hid_buf.at[pl.ds(0, lead), :], hid_q_hbm))
        out = dot(hid, w_out_buf[...])
        if i == 0:
            for j in range(steps):
                part_buf[j, ROWS:, :] = out[:8]
        for j in range(pair):
            part_buf[i + j, :ROWS, :] = out[skip + j * ROWS : skip + (j + 1) * ROWS]
            stores.append(copies.start(part_buf.at[i + j], part_hbm.at[i + j]))
        rows = pl.ds(lead + i * ROWS, pair * ROWS)
        stores.append(copies.start(hid_buf.at[rows, :], hid_hbm.at[pl.ds(i * ROWS, pair * ROWS), :]))
    for store in stores:
        store.wait()


FAR = pl.BlockSpec(memory_space=pltpu.HBM)
NEAR = pl.BlockSpec(memory_space=pltpu.VMEM)


def pinned(*arrays):
    return [pltpu.with_memory_space_constraint(a, pltpu.HBM) for a in arrays]


def forward(query_feats, item_feats, w_in, w_out):
    few = query_feats.shape[0]
    items, feats = item_feats.shape
    units = w_in.shape[1]
    width = w_out.shape[1]
    steps = items // ROWS
    return pl.pallas_call(
        forward_kernel,
        in_specs=[FAR] * 4,
        out_specs=[FAR] * 3,
        out_shape=[
            pltpu.HBM((steps, ROWS + 8, width), F32),
            pltpu.HBM((items, units), BF16),
            pltpu.HBM((16, units), BF16),
        ],
        scratch_shapes=[
            pltpu.VMEM((few, feats), BF16),
            pltpu.VMEM((16 + items, feats), BF16),
            pltpu.VMEM((feats, units), BF16),
            pltpu.VMEM((units, width), BF16),
            pltpu.VMEM((steps, ROWS + 8, width), F32),
            pltpu.VMEM((16 + items, units), BF16),
            pltpu.SemaphoreType.DMA((4 + 3 * steps,)),
        ],
        compiler_params=pltpu.CompilerParams(vmem_limit_bytes=VMEM),
    )(*pinned(query_feats, item_feats, w_in, w_out))


def row_ids(block, shape):
    return (lax.broadcasted_iota(jnp.int32, shape, 0) + block * shape[0]).astype(F32)


def weighed(scale, few, layer, all_q, digits):
    emb = jnp.tanh(layer.astype(F32)).astype(BF16)
    times = [((digits >> (5 * i)) & 31).astype(F32) for i in range(few)]
    weight = jnp.concatenate(times, 1) * jnp.exp(scale * dot_lanes(emb, all_q))
    return emb, weight


def share_of(info_ref, few, far):
    return pl.ds(pl.multiple_of(lax.bitwise_xor(info_ref[few + 1], far) * ROWS, ROWS), ROWS)


def counts_kernel(
    few, slots, scale, info_ref, msg_ref, own_ref, all_q_ref, digit_ref, weight_ref, d_ref, code, digit
):
    lines = msg_ref.shape[0]
    width = all_q_ref.shape[1]
    group = lines * 2 // few
    line = lax.broadcasted_iota(jnp.int32, (lines, lines), 0)
    column = lax.broadcasted_iota(jnp.int32, (lines, lines), 1)
    order = jnp.where(column == (line % group) * 2 + line // group, 1.0, 0.0).astype(BF16)
    turned = dot(order, msg_ref[...])
    parts = []
    for i in range(few):
        first = (i % 2) * width
        parts.append(turned[(i // 2) * group : (i // 2 + 1) * group, first : first + width])
    all_q_ref[...] = jnp.concatenate(parts, 0).astype(BF16)
    asked = turned[:group, 2 * width :].T
    who = asked[2 * slots : 3 * slots]
    code[:slots, :] = jnp.where(who > 0.0, asked[:slots] * 32.0 + asked[slots : 2 * slots], -1.0)
    power = jnp.zeros_like(who)
    for i in range(few):
        power = jnp.where(who == i + 1.0, 32.0**i, power)
    digit[:slots, :] = power
    lane = lax.broadcasted_iota(jnp.int32, (1, group), 1)
    for i in range(few):
        code[slots + i : slots + i + 1, :] = jnp.where(lane == info_ref[few], info_ref[i], -1).astype(F32)
        digit[slots + i : slots + i + 1, :] = jnp.full((1, group), 32.0**i, F32)
    for block, chunk in enumerate(blocks_of(digit_ref.shape[0])):
        ids = row_ids(block, (ROWS, group))
        digits = jnp.zeros((ROWS, group), F32)
        for s in range(slots + few):
            digits = digits + jnp.where(code[s : s + 1, :] == ids, digit[s : s + 1, :], 0.0)
        digit_ref[chunk, :] = digits.astype(jnp.int32)
    own_digits = digit_ref[share_of(info_ref, few, 0), :]
    weight = weighed(scale, few, own_ref[...], all_q_ref[...], own_digits)[1]
    weight_ref[...] = weight.astype(BF16)
    d_ref[...] = jnp.sum(weight, 0, keepdims=True)


def counts(info, message, own, few, slots, scale, items):
    width = own.shape[1]
    lines = message.shape[0]
    group = 2 * lines // few
    return pl.pallas_call(
        functools.partial(counts_kernel, few, slots, scale),
        in_specs=[pl.BlockSpec(memory_space=pltpu.SMEM), NEAR, NEAR],
        out_specs=[NEAR] * 4,
        out_shape=[
            jax.ShapeDtypeStruct((2 * lines, width), BF16),
            jax.ShapeDtypeStruct((items, group), jnp.int32),
            jax.ShapeDtypeStruct((own.shape[0], 2 * lines), BF16),
            jax.ShapeDtypeStruct((1, 2 * lines), F32),
        ],
        scratch_shapes=[pltpu.VMEM((slots + 8, group), F32)] * 2,
        compiler_params=pltpu.CompilerParams(vmem_limit_bytes=VMEM),
        cost_estimate=pl.CostEstimate(flops=3 * 2**30, bytes_accessed=2**20, transcendentals=0),
    )(info, message, own)


def score_kernel(
    few, scale, info_ref, own_ref, by2_ref, by1_ref, by3_ref, all_q_ref, digit_ref, own_weight_ref, own_d_ref,
    weight_hbm, layer_hbm, all_q_hbm, pay_ref, weight_ref, layer_ref, total_u, emb, sems,
):
    copies = Copies(sems)
    queries, width = all_q_ref.shape
    group = queries // few
    near = (own_ref, by1_ref, by2_ref, by3_ref)
    for far, ref in enumerate(near):
        layer_ref[share_of(info_ref, few, far), :] = ref[...]
    stores = [copies.start(layer_ref, layer_hbm), copies.start(all_q_ref, all_q_hbm)]
    all_q = all_q_ref[...]

    total_d = own_d_ref[...]
    for far, ref in enumerate(near):
        chunk = share_of(info_ref, few, far)
        if far == 0:
            emb[chunk, :] = jnp.tanh(ref[...].astype(F32)).astype(BF16)
            weight_ref[chunk, :] = own_weight_ref[...]
        else:
            e16, weight = weighed(scale, few, ref[...], all_q, digit_ref[chunk, :])
            emb[chunk, :] = e16
            weight_ref[chunk, :] = weight.astype(BF16)
            total_d = total_d + jnp.sum(weight, 0, keepdims=True)
        stores.append(copies.start(weight_ref.at[chunk, :], weight_hbm.at[chunk, :]))

    total_u[...] = dot_rows(weight_ref[...], emb[...])
    d = jnp.concatenate([total_d[:, i * width : (i + 1) * width] for i in range(queries // width)], 0)
    high = d.astype(BF16).astype(F32)
    tail = jnp.concatenate([high, d - high, jnp.zeros((8 - 2 * d.shape[0], width), F32)], 0)
    for y in range(pay_ref.shape[0]):
        mine = [total_u[i * group + y * 8 : i * group + y * 8 + 8, :] for i in range(few)]
        pay_ref[y] = jnp.concatenate([*mine, tail], 0).astype(BF16)
    for store in stores:
        store.wait()


def score(info, layers, counted, few, scale, peers):
    share, width = layers[0].shape
    items = share * len(layers)
    queries = counted[0].shape[0]
    pay = (peers, queries // peers + 8, width)
    return pl.pallas_call(
        functools.partial(score_kernel, few, scale),
        in_specs=[pl.BlockSpec(memory_space=pltpu.SMEM)] + [NEAR] * (len(layers) + len(counted)),
        out_specs=[FAR] * 3 + [NEAR],
        out_shape=[
            pltpu.HBM((items, queries), BF16),
            pltpu.HBM((items, width), BF16),
            pltpu.HBM((queries, width), BF16),
            jax.ShapeDtypeStruct(pay, BF16),
        ],
        scratch_shapes=[
            pltpu.VMEM((items, queries), BF16),
            pltpu.VMEM((items, width), BF16),
            pltpu.VMEM((queries, width), F32),
            pltpu.VMEM((items, width), BF16),
            pltpu.SemaphoreType.DMA((3 + items // ROWS,)),
        ],
        compiler_params=pltpu.CompilerParams(vmem_limit_bytes=VMEM),
    )(info, *layers, *counted)


def backward_kernel(
    few, scale, info_ref, all_q_hbm, weight_hbm, layer_hbm, hid_hbm, x_hbm, sums_ref, w_out_ref,
    emb_q_ref, hid_q_ref, q_ref, mine_ref, other_ref,
    all_q_ref, weight_ref, layer_ref, hid_ref, x_ref, item_grad, tanh_grad, pre_grad, summed, sems,
):
    items, width = layer_ref.shape
    feats = x_ref.shape[1]
    halves = [pl.ds(i * 2 * ROWS, 2 * ROWS) for i in range(items // (2 * ROWS))]
    copies = Copies(sems)
    load_q = copies.start(all_q_hbm, all_q_ref)
    load_weight = [copies.start(weight_hbm.at[half, :], weight_ref.at[half, :]) for half in halves]
    load_layer = copies.start(layer_hbm, layer_ref)
    load_hid = copies.start(hid_hbm, hid_ref)
    load_x = copies.start(x_hbm, x_ref)

    queries = all_q_ref.shape[0]
    group = queries // few
    sums = jnp.sum(sums_ref[...].astype(F32), 0)
    d = sums[few : few + 2] + sums[few + 2 : few + 4]
    d = jnp.concatenate([d[0:1], d[1:2]], 1)
    factor = jnp.broadcast_to(scale / d, (8, queries)).T[:, :1]
    line = lax.broadcasted_iota(jnp.int32, (8, queries), 0)
    own_lane = lax.broadcasted_iota(jnp.int32, (8, queries), 1)
    own_d = jnp.sum(jnp.where(own_lane == line * group + info_ref[few], d, 0.0), 1, keepdims=True)
    emb_q = emb_q_ref[...]
    own_q = emb_q.astype(BF16).astype(F32)
    load_q.wait()
    scaled = (all_q_ref[...].astype(F32) * factor).astype(BF16)
    for half, load in zip(halves, load_weight):
        load.wait()
        item_grad[half, :] = dot(weight_ref[half, :], scaled)
    load_layer.wait()
    named = []
    for i in range(few):
        place = info_ref[i]
        item_grad[pl.ds(place, 1), :] = item_grad[pl.ds(place, 1), :] - scale * own_q[i : i + 1]
        base = (place // 16) * 16
        near = layer_ref[pl.ds(pl.multiple_of(base, 16), 16), :].astype(F32)
        at = lax.broadcasted_iota(jnp.int32, near.shape, 0) == place - base
        named.append(jnp.sum(jnp.where(at, near, 0.0), 0, keepdims=True))
    named.append(jnp.zeros((8 - few, width), F32))
    pos_emb = jnp.tanh(jnp.concatenate(named, 0)).astype(BF16).astype(F32)

    load_hid.wait()
    for chunk in halves:
        e = jnp.tanh(layer_ref[chunk, :].astype(F32))
        grad = (item_grad[chunk, :] * (1.0 - e * e)).astype(BF16)
        tanh_grad[chunk, :] = grad
        hid_grad = dot_lanes(grad, w_out_ref[...])
        pre_grad[chunk, :] = jnp.where(hid_ref[chunk, :] > 0, hid_grad, 0.0).astype(BF16)

    live = lax.broadcasted_iota(jnp.int32, (8, width), 0) < few
    grad = scale * (sums / own_d - pos_emb) * (1.0 - emb_q * emb_q)
    grad = jnp.where(live, grad, 0.0)
    grad_q = jnp.concatenate([grad, jnp.zeros_like(grad)], 0).astype(BF16)
    hid_q = hid_q_ref[...]
    pre_grad_q = jnp.where(hid_q > 0, dot_lanes(grad_q, w_out_ref[...]), 0.0).astype(BF16)
    load_x.wait()
    in_total = dot_rows(pre_grad[...], x_ref[...]) + dot_rows(pre_grad_q, q_ref[...])
    summed[:feats, :] = in_total.astype(BF16).T
    summed[feats:, :] = (dot_rows(hid_ref[...], tanh_grad[...]) + dot_rows(hid_q, grad_q)).astype(BF16)
    half = mine_ref.shape[0]
    core = info_ref[few + 2]

    @pl.when(core == 0)
    def _():
        mine_ref[...] = summed[:half, :]
        other_ref[...] = summed[half:, :]

    @pl.when(core != 0)
    def _():
        mine_ref[...] = summed[half:, :]
        other_ref[...] = summed[:half, :]


def backward(info, far, near, few, scale):
    items, width = far[2].shape
    units = far[3].shape[1]
    feats = far[4].shape[1]
    return pl.pallas_call(
        functools.partial(backward_kernel, few, scale),
        in_specs=[pl.BlockSpec(memory_space=pltpu.SMEM)] + [FAR] * len(far) + [NEAR] * len(near),
        out_specs=[NEAR] * 2,
        out_shape=[jax.ShapeDtypeStruct(((feats + units) // 2, width), BF16)] * 2,
        scratch_shapes=[
            *[pltpu.VMEM(a.shape, a.dtype) for a in far],
            pltpu.VMEM((items, width), F32),
            pltpu.VMEM((items, width), BF16),
            pltpu.VMEM((items, units), BF16),
            pltpu.VMEM((feats + units, width), BF16),
            pltpu.SemaphoreType.DMA((4 + items // (2 * ROWS),)),
        ],
        compiler_params=pltpu.CompilerParams(vmem_limit_bytes=VMEM),
    )(info, *pinned(*far), *near)


def assemble_kernel(core_ref, mine_ref, other_ref, in_hbm, out_hbm, sems):
    half = mine_ref.shape[0]
    rest = in_hbm.shape[0] - half

    def place(first, second):
        copies = Copies(sems)
        made = [
            copies.start(first, in_hbm.at[pl.ds(0, half), :]),
            copies.start(second.at[pl.ds(0, rest), :], in_hbm.at[pl.ds(half, rest), :]),
            copies.start(second.at[pl.ds(rest, half - rest), :], out_hbm),
        ]
        for copy in made:
            copy.wait()

    @pl.when(core_ref[0] == 0)
    def _():
        place(mine_ref, other_ref)

    @pl.when(core_ref[0] != 0)
    def _():
        place(other_ref, mine_ref)


def assemble(mine, other, feats):
    half, width = mine.shape
    return pl.pallas_call(
        assemble_kernel,
        in_specs=[pl.BlockSpec(memory_space=pltpu.SMEM)] + [NEAR] * 2,
        out_specs=[FAR] * 2,
        out_shape=[
            jax.ShapeDtypeStruct((feats, width), BF16),
            jax.ShapeDtypeStruct((2 * half - feats, width), BF16),
        ],
        scratch_shapes=[pltpu.SemaphoreType.DMA((3,))],
        compiler_params=pltpu.CompilerParams(vmem_limit_bytes=VMEM),
    )(lax.axis_index("c").reshape(1), mine, other)


def request_codes(rows, query_count, item_count, capacity, order, dp_count):
    pairs = rows.shape[0]
    owners = rows // item_count
    code = rows - owners * item_count
    owner_hot = order(owners)[:, None] == jnp.arange(dp_count, dtype=jnp.int32)[None, :]
    earlier = jnp.arange(pairs)[:, None] >= jnp.arange(pairs)[None, :]
    running = dot(earlier.astype(BF16), owner_hot.astype(BF16))
    slot = jnp.sum(jnp.where(owner_hot, running, 0.0), 1).astype(jnp.int32) - 1
    who = jnp.arange(pairs, dtype=jnp.int32) // (pairs // query_count) + 1
    lane = jnp.arange(128, dtype=jnp.int32)[None, :]
    value = jnp.zeros((pairs, 128), jnp.int32)
    for at, part in enumerate((code // 32, code % 32, who)):
        value = jnp.where(slot[:, None] + at * capacity == lane, part[:, None], value)
    return dot_rows(owner_hot.astype(BF16), value.astype(BF16)).astype(BF16)


def local(query_feats, item_feats, w_in, w_out, negatives, positives, owner_map):
    dp_count = lax.axis_size(DP)
    own_index = lax.axis_index(DP)
    z_count = lax.axis_size("z")
    x_count = lax.axis_size("x")
    yc_count = dp_count // z_count
    few = query_feats.shape[0]
    item_count = item_feats.shape[0]
    width = w_out.shape[1]
    negative_count = negatives.shape[1]
    scale = 4.0 / math.sqrt(width)
    capacity = 4 * few * negative_count // dp_count
    queries = few * dp_count

    blocks, hidden, hidden_q = forward(query_feats, item_feats, w_in, w_out)
    arrived = exchange(blocks, "x")

    named = jnp.concatenate([negatives.reshape(-1), positives])
    rows = jnp.take(owner_map, named, axis=0)
    pos_local = jnp.clip(rows[few * negative_count :] - own_index * item_count, 0, item_count - 1)
    places = [lax.axis_index(YCZ), lax.axis_index("x"), lax.axis_index("c")]
    info = jnp.concatenate([pos_local, jnp.stack(places)])
    codes = request_codes(
        rows[: few * negative_count],
        few,
        item_count,
        capacity,
        lambda o: (o % yc_count) * z_count + o // yc_count,
        dp_count,
    )
    codes = jnp.pad(codes[:, None, :], ((0, 0), (0, 1), (few // 2 * width, 0)))
    codes = lax.optimization_barrier(codes)

    own = total(arrived[:, :ROWS]).astype(BF16)
    own_q = jnp.tanh(total(arrived[:, ROWS:]))
    sent_q = jnp.pad(own_q[:few].astype(BF16).reshape(1, 2, -1), ((0, 0), (0, 0), (0, 128)))
    message = exchange(codes + sent_q, YCZ)
    message = message.reshape(2 * dp_count, -1)
    layers = [own]
    for far in (2, 1, 3):
        layers.append(lax.ppermute(own, "x", [(i, i ^ far) for i in range(x_count)]))

    counted = counts(info, message, own, few, capacity, scale, item_count)
    weight, layer_out, all_q, pay = score(info, layers, counted, few, scale, yc_count)
    first = total(exchange(pay, ("y", "c")))
    mine = queries // yc_count
    d_rows = queries // width
    d_part = first[mine : mine + d_rows] + first[mine + d_rows : mine + 2 * d_rows]
    high = d_part.astype(BF16)
    tail = jnp.concatenate([high, (d_part - high.astype(F32)).astype(BF16)], 0)
    sums = exchange(
        jnp.concatenate(
            [
                first[:mine].astype(BF16).reshape(few, z_count, width).transpose(1, 0, 2),
                jnp.broadcast_to(tail[None], (z_count, 2 * d_rows, width)),
            ],
            1,
        ),
        "z",
    )
    feats_q = jnp.pad(query_feats, ((0, 16 - few), (0, 0)))
    near = (sums, w_out, own_q, hidden_q, feats_q)
    mine, other = backward(info, (all_q, weight, layer_out, hidden, item_feats), near, few, scale)
    y_count = lax.axis_size("y")
    swap = [(0, 1), (1, 0)]
    grads = (mine.astype(F32) + lax.ppermute(other, "c", swap).astype(F32)).astype(BF16)
    grads = total(exchange(grads.reshape(y_count, -1, width), "y"))
    grads = total(spread(grads.astype(BF16), "z")).astype(BF16)
    grads = spread(grads, "y").reshape(-1, width)
    return tuple(assemble(grads, lax.ppermute(grads, "c", swap), w_in.shape[0]))


def solution(mesh):
    grid = Mesh(mesh.devices.reshape(8, 8, 2, 4), ("z", "y", "c", "x"))
    return jax.shard_map(
        local,
        mesh=grid,
        in_specs=(
            P(DP, None),
            P(DP, None),
            P(None, "x"),
            P("x", None),
            P(DP, None),
            P(DP),
            P(),
        ),
        out_specs=(P(None, "x"), P("x", None)),
        check_vma=False,
    )
```
